32 devices in a mesh: wide: 8 (over y, x, core), narrow: 4 (over z).
Axes of the slice: x: 2, y: 2, z: 4, core: 2. Of those that a mesh axis runs over, the one named last changes fastest.
Arguments:
- tokens: bfloat16 [4, 2048, 1152], P('narrow', 'wide'), may hold values from -6 to 6
- mixer_gain: bfloat16 [1152], P(('wide', 'narrow')), may hold values from 0.099609375 to 1.8984375
- in_weight: bfloat16 [1152, 4608], P(('wide', 'narrow')), may hold values from -0.1875 to 0.1875
- conv_weight: bfloat16 [4, 2304], P(None, ('wide', 'narrow')), may hold values from -3 to 3
- conv_bias: bfloat16 [2304], P(('wide', 'narrow')), may hold values from -3 to 3
- select_weight: bfloat16 [2304, 104], P(('wide', 'narrow')), may hold values from -0.125 to 0.125
- step_weight: bfloat16 [72, 2304], P(None, ('wide', 'narrow')), may hold values from -0.75 to 0.75
- step_bias: bfloat16 [2304], P(('wide', 'narrow')), may hold values from -6 to -2
- decay_log: bfloat16 [16, 2304], P(None, ('wide', 'narrow')), may hold values from -4 to 1
- skip_weight: bfloat16 [2304], P(('wide', 'narrow')), may hold values from 0.5 to 1.5
- out_weight: bfloat16 [2304, 1152], P(('wide', 'narrow')), may hold values from -0.125 to 0.125
- expert_gain: bfloat16 [1152], P(('wide', 'narrow')), may hold values from 0.099609375 to 1.8984375
- router_weight: bfloat16 [1152, 2], P(('wide', 'narrow')), may hold values from -0.125 to 0.125
- up_weight: bfloat16 [2, 1152, 3072], P(None, ('wide', 'narrow')), may hold values from -0.1875 to 0.1875
- down_weight: bfloat16 [2, 3072, 1152], P(None, ('wide', 'narrow')), may hold values from -0.109375 to 0.109375
- routes: int32 [4, 2048], P('narrow', 'wide'), may hold values from 0 to 1
- lengths: int32 [4], P('narrow'), may hold values from 256 to 2048, as said below
- cotangent: bfloat16 [4, 2048, 1152], P('narrow', 'wide'), may hold values from -6 to 6
Outputs:
- output: bfloat16 [4, 2048, 1152], P('narrow', 'wide')
- token_grad: float32 [4, 2048, 1152], P('narrow', 'wide')
- grad_mixer_gain: float32 [1152], P(('wide', 'narrow'))
- grad_in_weight: float32 [1152, 4608], P(('wide', 'narrow'))
- grad_conv_weight: float32 [4, 2304], P(None, ('wide', 'narrow'))
- grad_conv_bias: float32 [2304], P(('wide', 'narrow'))
- grad_select_weight: float32 [2304, 104], P(('wide', 'narrow'))
- grad_step_weight: float32 [72, 2304], P(None, ('wide', 'narrow'))
- grad_step_bias: float32 [2304], P(('wide', 'narrow'))
- grad_decay_log: float32 [16, 2304], P(None, ('wide', 'narrow'))
- grad_skip_weight: float32 [2304], P(('wide', 'narrow'))
- grad_out_weight: float32 [2304, 1152], P(('wide', 'narrow'))
- grad_expert_gain: float32 [1152], P(('wide', 'narrow'))
- grad_router_weight: float32 [1152, 2], P(('wide', 'narrow'))
- grad_up_weight: float32 [2, 1152, 3072], P(None, ('wide', 'narrow'))
- grad_down_weight: float32 [2, 3072, 1152], P(None, ('wide', 'narrow'))
The draws below stay inside these ranges and needn't reach their ends.
Inputs may be any that keep to these rules, and one draw needn't show every extreme that they name: `lengths`: one sequence, chosen by the seed, counts all its 2048 tokens.
All inputs are finite; a program needn't handle non-finite values.
Results may differ from the reference program's by a relative error of at most 0.011.
Values may be sent and summed in bfloat16 or wider, within the bound.
No kernel may reach another device: no remote copies, remote signals or barrier semaphores. Data moves between devices by JAX's collectives and lax.ppermute only.
A program may use at most 384 MiB of HBM per device.

```python
import jax
import jax.numpy as jnp
from jax import lax

D = 1152
DI = 2304
NS = 16
DT_RANK = 72
CONV = 4
FF = 3072
EXPERTS = 2
SCAN_BLOCK = 64
SEQ = 2048
SEQS = 4


def draw_lengths(key, part):
    key = jax.random.fold_in(key, 11)
    pick_key, other_key = jax.random.split(key)
    chosen = jax.random.randint(pick_key, (), 0, SEQS)
    others = jax.random.randint(other_key, (SEQS,), SEQ // 8, SEQ + 1)
    return jnp.where(jnp.arange(SEQS) == chosen, SEQ, others).astype(jnp.int32)


def plant(result, stream_key, smallest, largest):
    longest = result.shape.index(max(result.shape))
    spots = []
    for shift in (0, 1):
        where = [jax.random.randint(jax.random.fold_in(stream_key, axis), (), 0, length) for axis, length in enumerate(result.shape)]
        where[longest] = (where[longest] + shift) % result.shape[longest]
        spots.append(tuple(where))
    return result.at[spots[0]].set(smallest).at[spots[1]].set(largest)


def steps_of(stream_key, extent, cuts, least, top_value):
    factor_of, own = 1.0, jax.random.fold_in(stream_key, 6)
    for dim, shards_of in cuts:
        steps = jnp.exp(jax.random.uniform(jax.random.fold_in(own, dim), (shards_of,), jnp.float32, least / len(cuts), top_value / len(cuts)))
        factor_of = factor_of * jnp.repeat(steps, extent[dim] // shards_of).reshape([-1 if axis == dim else 1 for axis in range(len(extent))])
    return factor_of


def gaussian(stream_key, shape, scale, bound, cuts=(), dtype=jnp.bfloat16):
    values = jax.random.normal(stream_key, shape, jnp.float32) * scale
    if len(cuts) > 0:
        values = steps_of(stream_key, shape, cuts, -0.22, 0.18) * values
    return jnp.clip(values, min=-bound, max=bound).astype(dtype)


def setup_inputs(seed: int = 0) -> dict:
    key_list = jax.random.split(jax.random.key(seed), 19)
    return {
        "tokens": gaussian(key_list[0], (SEQS, SEQ, D), 1.0, 6.0, ((0, 4), (1, 8))),
        "mixer_gain": jnp.clip(1.0 + 0.18 * jax.random.normal(key_list[1], (D,), jnp.float32), 0.099609375, 1.8984375).astype(jnp.bfloat16),
        "in_weight": gaussian(key_list[2], (D, 2 * DI), D ** -0.5, 0.1875, ((0, 32),)),
        "conv_weight": gaussian(key_list[3], (CONV, DI), CONV ** -0.5, 3.0, ((1, 32),)),
        "conv_bias": gaussian(key_list[4], (DI,), 0.5, 3.0, ((0, 32),)),
        "select_weight": gaussian(key_list[5], (DI, DT_RANK + 2 * NS), DI ** -0.5, 0.125, ((0, 32),)),
        "step_weight": gaussian(key_list[6], (DT_RANK, DI), DT_RANK ** -0.5, 0.75, ((1, 32),)),
        "step_bias": jnp.clip(-6.0 + 4.0 * jax.random.uniform(key_list[7], (DI,), jnp.float32) ** steps_of(key_list[7], (DI,), ((0, 32),), -0.2, 0.2), -6.0, -2.0).astype(jnp.bfloat16),
        "decay_log": jnp.clip(-4.0 + 5.0 * jax.random.uniform(key_list[8], (NS, DI), jnp.float32) ** steps_of(key_list[8], (NS, DI), ((1, 32),), -0.2, 0.2), -4.0, 1.0).astype(jnp.bfloat16),
        "skip_weight": jnp.clip(0.5 + 1.0 * jax.random.uniform(key_list[9], (DI,), jnp.float32) ** steps_of(key_list[9], (DI,), ((0, 32),), -0.2, 0.2), 0.5, 1.5).astype(jnp.bfloat16),
        "out_weight": gaussian(key_list[10], (DI, D), DI ** -0.5, 0.125, ((0, 32),)),
        "expert_gain": jnp.clip(1.0 + 0.18 * jax.random.normal(key_list[11], (D,), jnp.float32), 0.099609375, 1.8984375).astype(jnp.bfloat16),
        "router_weight": gaussian(key_list[12], (D, EXPERTS), (2 * D) ** -0.5, 0.125, ((0, 32),)),
        "up_weight": gaussian(key_list[13], (EXPERTS, D, FF), D ** -0.5, 0.1875, ((1, 32),)),
        "down_weight": gaussian(key_list[14], (EXPERTS, FF, D), FF ** -0.5, 0.109375, ((1, 32),)),
        "routes": plant(jax.random.randint(key_list[15], (SEQS, SEQ), 0, EXPERTS), jax.random.fold_in(key_list[15], 1), 0, EXPERTS - 1).astype(jnp.int32),
        "lengths": draw_lengths(jax.random.fold_in(key_list[18], 71), 0),
        "cotangent": gaussian(key_list[17], (SEQS, SEQ, D), 1.0, 6.0, ((0, 4), (1, 8))),
    }


@jax.custom_vjp
def low(v):
    return lax.optimization_barrier(v.astype(jnp.bfloat16)).astype(jnp.float32)

@jax.custom_vjp
def low_back(v):
    return v

def low_keep(v):
    return (low(v), None)

def low_pass(kept, grad):
    return (grad,)

def back_keep(v):
    return (v, None)

def back_low(kept, grad):
    return (low(grad),)
low.defvjp(low_keep, low_pass)
low_back.defvjp(back_keep, back_low)
EPSILON = 1e-05

def matmul(left, right):
    return jnp.dot(left, right, precision=lax.Precision.HIGHEST, preferred_element_type=jnp.float32)

def rms_norm(values, gain_vec):
    return values * lax.rsqrt(lax.optimization_barrier(jnp.mean(values * values, axis=-1, keepdims=True)) + EPSILON) * gain_vec

def linked(first, second):
    return (first[0] * second[0], second[0] * first[1] + second[1])

def block_scan(carry_state, pieces, a_neg):
    conv_act, step_size, in_select, out_select = pieces
    decays = jnp.exp(step_size[:, None, :] * a_neg[None, :, :])
    drives = (step_size * conv_act)[:, None, :] * in_select[:, :, None]
    factor, summed = lax.associative_scan(linked, (decays, drives), axis=0)
    states = factor * carry_state[None] + summed
    return (states[-1], lax.optimization_barrier(jnp.sum(out_select[:, :, None] * states, axis=1)))

def selective_scan(conv_act, step_size, in_select, out_select, a_neg):
    length = conv_act.shape[0]
    block_count = length // SCAN_BLOCK

    def advance(carry_state, pieces):
        return block_scan(carry_state, pieces, a_neg)

    def to_blocks(values):
        return values.reshape(block_count, SCAN_BLOCK, values.shape[1])
    start_state = jnp.zeros((NS, DI), jnp.float32)
    end_state, outputs = lax.scan(jax.checkpoint(advance), start_state, (to_blocks(conv_act), to_blocks(step_size), to_blocks(in_select), to_blocks(out_select)))
    return outputs.reshape(length, DI)

def layer(params, inputs, routes):
    mixer_gain, in_weight, conv_weight, conv_bias, select_weight, step_weight, step_bias, decay_log, skip_weight, out_weight, expert_gain, router_weight, up_weight, down_weight = params
    length = inputs.shape[0]
    normed = low(rms_norm(inputs, mixer_gain))
    projected = low_back(matmul(normed, in_weight))
    x_branch = projected[:, :DI]
    z_branch = projected[:, DI:]
    padded = jnp.concatenate([jnp.zeros((CONV - 1, DI), jnp.float32), x_branch], axis=0)
    conv_sum = conv_bias + jnp.zeros_like(x_branch)
    for offset in range(CONV):
        conv_sum = conv_sum + conv_weight[offset] * padded[offset:offset + length]
    conv_act = low(jax.nn.silu(conv_sum))
    selected = low_back(matmul(conv_act, select_weight))
    step_low = low(selected[:, :DT_RANK])
    in_select = selected[:, DT_RANK:DT_RANK + NS]
    out_select = selected[:, DT_RANK + NS:]
    step_size = jax.nn.softplus(low_back(matmul(step_low, step_weight)) + step_bias)
    a_neg = -jnp.exp(decay_log)
    scanned = selective_scan(conv_act, step_size, in_select, out_select, a_neg)
    mixer_out = scanned + skip_weight * conv_act
    gated_act = low(mixer_out * jax.nn.silu(z_branch))
    hidden_one = inputs + low_back(matmul(gated_act, out_weight))
    normed_two = low(rms_norm(hidden_one, expert_gain))
    logits = low_back(matmul(normed_two, router_weight))
    router_probs = jax.nn.softmax(logits, axis=-1)
    onehot = (routes[:, None] == jnp.arange(EXPERTS)[None, :]).astype(jnp.float32)
    gate_val = lax.optimization_barrier(jnp.sum(router_probs * onehot, axis=-1))
    expert_sum = jnp.zeros_like(inputs)
    for expert in range(EXPERTS):
        hidden = low(jax.nn.gelu(low_back(matmul(normed_two, up_weight[expert])), approximate=False))
        expert_sum = expert_sum + onehot[:, expert:expert + 1] * low_back(matmul(hidden, down_weight[expert]))
    return hidden_one + gate_val[:, None] * expert_sum

def reference(tokens, mixer_gain, in_weight, conv_weight, conv_bias, select_weight, step_weight, step_bias, decay_log, skip_weight, out_weight, expert_gain, router_weight, up_weight, down_weight, routes, lengths, cotangent):
    params = tuple((weight.astype(jnp.float32) for weight in (mixer_gain, in_weight, conv_weight, conv_bias, select_weight, step_weight, step_bias, decay_log, skip_weight, out_weight, expert_gain, router_weight, up_weight, down_weight)))
    inputs = tokens.astype(jnp.float32)

    def forward(weights, values):

        def one_sequence(pieces):
            return layer(weights, pieces[0], pieces[1])
        return lax.map(one_sequence, (values, routes))
    output, pullback = jax.vjp(forward, params, inputs)
    valid = (jnp.arange(SEQ)[None, :] < lengths[:, None]).astype(jnp.float32)
    grads, token_grad = pullback(cotangent.astype(jnp.float32) * valid[:, :, None])
    return (output.astype(jnp.bfloat16), token_grad, grads[0], grads[1], grads[2], grads[3], grads[4], grads[5], grads[6], grads[7], grads[8], grads[9], grads[10], grads[11], grads[12], grads[13])
```

```python
import math

import jax
import jax.numpy as jnp
from jax import lax
from jax.experimental import pallas as pl
from jax.experimental.pallas import tpu as pltpu
from jax.sharding import PartitionSpec as P

D = 1152
DI = 2304
NS = 16
DT_RANK = 72
CONV = 4
FF = 3072
EXPERTS = 2
EPSILON = 1e-05
TIME_BLOCK = 128
UNROLL = 64
LANES = 128
LN2 = math.log(2.0)

f32 = jnp.float32
bf16 = jnp.bfloat16


def swap(x, k):
    n = lax.axis_size("wide")
    return lax.ppermute(x, "wide", [(i, i ^ k) for i in range(n)])


def turn(x, k):
    n = lax.axis_size("narrow")
    return lax.ppermute(x, "narrow", [(i, (i + k) % n) for i in range(n)])


def place():
    w = lax.axis_index("wide")
    return w // 2, w % 2


def pick(x, i, axis=0):
    return lax.dynamic_index_in_dim(x, i, axis, False)


def gather_wide(block):
    n = lax.axis_size("wide")
    if n != 8:
        return lax.all_gather(block, "wide", axis=0, tiled=True)
    chip, core = place()
    rows, cols = block.shape
    half = rows // 2
    mate = swap(block, 1)
    a, b = swap(block, 2), swap(block, 4)
    c = jnp.concatenate([swap(a[:half], 4), swap(b[half:], 2)], axis=0)
    mine = (block, a, b, c)
    theirs = (mate, swap(a, 1), swap(b, 1), swap(c, 1))
    out = jnp.zeros((8, rows, cols), block.dtype)
    for q in range(4):
        at = (chip ^ q) * 2
        out = lax.dynamic_update_index_in_dim(out, mine[q], at + core, 0)
        out = lax.dynamic_update_index_in_dim(out, theirs[q], at + 1 - core, 0)
    return out.reshape(8 * rows, cols)


def scatter_wide(partial):
    n = lax.axis_size("wide")
    if n != 8:
        return lax.psum_scatter(partial, "wide", scatter_dimension=0, tiled=True).astype(f32)
    chip, core = place()
    rows = partial.shape[0] // 8
    half = rows // 2
    parts = partial.reshape(4, 2, rows, partial.shape[1])
    own = pick(parts, core, 1)
    other = swap(pick(parts, 1 - core, 1), 1)

    def summed(q):
        return pick(own, chip ^ q).astype(f32) + pick(other, chip ^ q).astype(f32)

    far = summed(3).astype(bf16)
    sx, sy = summed(1), summed(2)
    r0, r1 = swap(far[:half], 2), swap(far[half:], 4)
    x0, y1 = swap(sx[:half].astype(bf16), 2), swap(sy[half:].astype(bf16), 4)
    x1 = swap((sx[half:] + r1.astype(f32)).astype(bf16), 2)
    y0 = swap((sy[:half] + r0.astype(f32)).astype(bf16), 4)
    x = jnp.concatenate([x0, x1], axis=0).astype(f32)
    y = jnp.concatenate([y0, y1], axis=0).astype(f32)
    return summed(0) + x + y


def reduce_wide(partial):
    n = lax.axis_size("wide")
    if n != 8:
        return lax.psum(partial.astype(bf16), "wide")
    _, core = place()
    half = partial.shape[0] // 2
    parts = partial.astype(bf16).reshape(2, half, partial.shape[1])
    total = pick(parts, core).astype(f32) + swap(pick(parts, 1 - core), 1).astype(f32)
    low = total.astype(bf16)
    total = (
        total + swap(low, 2).astype(f32) + swap(low, 4).astype(f32) + swap(low, 6).astype(f32)
    )
    low = total.astype(bf16)
    out = jnp.zeros((2, half, partial.shape[1]), bf16)
    out = lax.dynamic_update_index_in_dim(out, low, core, 0)
    out = lax.dynamic_update_index_in_dim(out, swap(low, 1), 1 - core, 0)
    return out.reshape(partial.shape)


def gather_narrow(x):
    n, z = lax.axis_size("narrow"), lax.axis_index("narrow")
    out = lax.dynamic_update_index_in_dim(jnp.zeros((n,) + x.shape, x.dtype), x, z, 0)
    for k in range(1, n):
        out = lax.dynamic_update_index_in_dim(out, turn(x, k), (z - k) % n, 0)
    return out


def scatter_narrow(x):
    n, z = lax.axis_size("narrow"), lax.axis_index("narrow")
    total = pick(x, z).astype(f32)
    for k in range(1, n):
        total = total + turn(pick(x, (z + k) % n), k).astype(f32)
    return total


def exchange_wide(x):
    return lax.all_to_all(x, "wide", 0, 0)


def scan_forward_kernel(x_ref, dt_ref, b_ref, c_ref, a_ref, y_ref, kept_ref, end_ref, state):
    @pl.when(pl.program_id(0) == 0)
    def _():
        state[...] = jnp.zeros_like(state)

    a2 = a_ref[...]
    in_sel, out_sel = b_ref[...], c_ref[...]

    def group(g, h):
        t0 = pl.multiple_of(g * UNROLL, UNROLL)
        back = lax.rem(TIME_BLOCK - t0, TIME_BLOCK)
        b, c = pltpu.roll(in_sel, back, 1), pltpu.roll(out_sel, back, 1)
        dt = dt_ref[pl.ds(t0, UNROLL), :]
        u = dt * x_ref[pl.ds(t0, UNROLL), :].astype(f32)
        for j in range(UNROLL):
            kept_ref[t0 + j] = h
            h = jnp.exp2(dt[j : j + 1, :] * a2) * h + u[j : j + 1, :] * b[:, j : j + 1]
            y_ref[pl.ds(t0 + j, 1), :] = jnp.sum(h * c[:, j : j + 1], axis=0, keepdims=True)
        return h

    h = lax.fori_loop(0, TIME_BLOCK // UNROLL, group, state[...])
    state[...] = h
    end_ref[...] = h


def scan_forward(x, dt, in_sel, out_sel, a2):
    length, chans = x.shape
    row = pl.BlockSpec((TIME_BLOCK, chans), lambda i: (i, 0))
    sel = pl.BlockSpec((NS, TIME_BLOCK), lambda i: (0, i))
    whole = pl.BlockSpec((NS, chans), lambda i: (0, 0))
    return pl.pallas_call(
        scan_forward_kernel,
        grid=(length // TIME_BLOCK,),
        in_specs=[row, row, sel, sel, whole],
        out_specs=[row, pl.BlockSpec((TIME_BLOCK, NS, chans), lambda i: (i, 0, 0)), whole],
        out_shape=[
            jax.ShapeDtypeStruct((length, chans), f32),
            jax.ShapeDtypeStruct((length, NS, chans), f32),
            jax.ShapeDtypeStruct((NS, chans), f32),
        ],
        scratch_shapes=[pltpu.VMEM((NS, chans), f32)],
        compiler_params=pltpu.CompilerParams(vmem_limit_bytes=24 * 2**20),
        cost_estimate=pl.CostEstimate(
            flops=8 * length * NS * chans,
            bytes_accessed=4 * length * chans * (NS + 3),
            transcendentals=length * NS * chans,
        ),
    )(x, dt, in_sel, out_sel, a2)


def scan_backward_kernel(
    x_ref,
    dt_ref,
    dy_ref,
    b_ref,
    c_ref,
    a_ref,
    kept_ref,
    end_ref,
    dstep_ref,
    dconv_ref,
    db_ref,
    dc_ref,
    da_ref,
    lam_s,
    next_s,
    pb_s,
    pc_s,
):
    chans = x_ref.shape[1]
    groups = TIME_BLOCK // UNROLL

    @pl.when(pl.program_id(0) == 0)
    def _():
        lam_s[...] = jnp.zeros_like(lam_s)
        next_s[...] = end_ref[...]
        da_ref[...] = jnp.zeros_like(da_ref)

    a2 = a_ref[...]
    in_sel, out_sel = b_ref[...], c_ref[...]

    def fold(v):
        total = v[:, :LANES]
        for k in range(1, chans // LANES):
            total = total + v[:, k * LANES : (k + 1) * LANES]
        return total

    def group(i, carry):
        p, after, acc = carry
        t0 = pl.multiple_of((groups - 1 - i) * UNROLL, UNROLL)
        back = lax.rem(TIME_BLOCK - t0, TIME_BLOCK)
        b, c = pltpu.roll(in_sel, back, 1), pltpu.roll(out_sel, back, 1)
        dt = dt_ref[pl.ds(t0, UNROLL), :]
        x = x_ref[pl.ds(t0, UNROLL), :].astype(f32)
        dy = dy_ref[pl.ds(t0, UNROLL), :]
        u = dt * x
        for j in range(UNROLL - 1, -1, -1):
            before = kept_ref[t0 + j]
            dt_j, dy_j = dt[j : j + 1, :], dy[j : j + 1, :]
            lam = dy_j * c[:, j : j + 1] + p
            p = lam * jnp.exp2(dt_j * a2)
            moved = p * before
            acc = acc + dt_j * moved
            dconv_ref[pl.ds(t0 + j, 1), :] = jnp.sum(lam * b[:, j : j + 1], axis=0, keepdims=True)
            dstep_ref[pl.ds(t0 + j, 1), :] = jnp.sum(a2 * moved, axis=0, keepdims=True)
            pb_s[t0 + j] = fold(lam * u[j : j + 1, :])
            pc_s[t0 + j] = fold(after * dy_j)
            after = before
        through = dconv_ref[pl.ds(t0, UNROLL), :]
        dstep_ref[pl.ds(t0, UNROLL), :] = dstep_ref[pl.ds(t0, UNROLL), :] * LN2 + x * through
        dconv_ref[pl.ds(t0, UNROLL), :] = dt * through
        return p, after, acc

    p, after, acc = lax.fori_loop(0, groups, group, (lam_s[...], next_s[...], da_ref[...]))
    lam_s[...] = p
    next_s[...] = after
    da_ref[...] = acc
    ones = jnp.ones((LANES, LANES), bf16)
    lane = lax.broadcasted_iota(jnp.int32, (NS, TIME_BLOCK), 1)
    for part, out in ((pb_s, db_ref), (pc_s, dc_ref)):

        def reduced(g, total):
            t0 = pl.multiple_of(g * 16, 16)
            rows = part[pl.ds(t0, 16)].reshape(16 * NS, LANES).astype(bf16)
            sums = jnp.dot(rows, ones, preferred_element_type=f32).reshape(16, NS, LANES)
            for j in range(16):
                total = jnp.where(lane == t0 + j, sums[j], total)
            return total

        out[...] = lax.fori_loop(0, TIME_BLOCK // 16, reduced, jnp.zeros((NS, TIME_BLOCK), f32))


def scan_backward(x, dt, dy, in_sel, out_sel, a2, kept, end):
    length, chans = x.shape
    n = length // TIME_BLOCK
    row = pl.BlockSpec((TIME_BLOCK, chans), lambda i: (n - 1 - i, 0))
    sel = pl.BlockSpec((NS, TIME_BLOCK), lambda i: (0, n - 1 - i))
    whole = pl.BlockSpec((NS, chans), lambda i: (0, 0))
    states = pl.BlockSpec((TIME_BLOCK, NS, chans), lambda i: (n - 1 - i, 0, 0))
    return pl.pallas_call(
        scan_backward_kernel,
        grid=(n,),
        in_specs=[row, row, row, sel, sel, whole, states, whole],
        out_specs=[row, row, sel, sel, whole],
        out_shape=[jax.ShapeDtypeStruct((length, chans), f32)] * 2
        + [jax.ShapeDtypeStruct((NS, length), f32)] * 2
        + [jax.ShapeDtypeStruct((NS, chans), f32)],
        scratch_shapes=[pltpu.VMEM((NS, chans), f32)] * 2
        + [pltpu.VMEM((TIME_BLOCK, NS, LANES), f32)] * 2,
        compiler_params=pltpu.CompilerParams(vmem_limit_bytes=24 * 2**20),
        cost_estimate=pl.CostEstimate(
            flops=20 * length * NS * chans,
            bytes_accessed=4 * length * chans * (NS + 5),
            transcendentals=length * NS * chans,
        ),
    )(x, dt, dy, in_sel, out_sel, a2, kept, end)


def mm(a, b):
    return jnp.dot(a, b, preferred_element_type=f32)


def mm_t(a, b):
    return lax.dot_general(a, b, (((1,), (1,)), ((), ())), preferred_element_type=f32)


def t_mm(a, b):
    return lax.dot_general(a, b, (((0,), (0,)), ((), ())), preferred_element_type=f32)


def norm_backward(values, inverse, gain_vec, upstream):
    scaled = upstream * gain_vec
    inner_mean = jnp.mean(values * scaled, axis=-1, keepdims=True)
    return inverse * scaled - values * (inverse * inverse * inverse) * inner_mean


def pad_to(x, axis, size):
    pads = [(0, 0)] * x.ndim
    pads[axis] = (0, size - x.shape[axis])
    return jnp.pad(x, pads)


def local(
    tokens,
    mixer_gain,
    in_weight,
    conv_weight,
    conv_bias,
    select_weight,
    step_weight,
    step_bias,
    decay_log,
    skip_weight,
    out_weight,
    expert_gain,
    router_weight,
    up_weight,
    down_weight,
    routes,
    lengths,
    cotangent,
):
    wide, narrow = lax.axis_size("wide"), lax.axis_size("narrow")
    w = lax.axis_index("wide")
    rows = tokens.shape[1]
    length = rows * wide
    chans = DI // wide
    wid = -(-chans // LANES) * LANES
    ff = FF // wide
    d_rows = D // (wide * narrow)
    c_rows = DI // (wide * narrow)
    f_rows = FF // (wide * narrow)
    sel_cols = DT_RANK + 2 * NS

    tokens_own = tokens[0].astype(f32)
    tokens_all = gather_wide(tokens[0])

    in_parts = in_weight.reshape(d_rows, 2, wide, chans).transpose(1, 2, 0, 3)
    gains = jnp.stack([mixer_gain, expert_gain], axis=1)
    gains = jnp.broadcast_to(gains[None], (wide, d_rows, 2))
    x_parts = exchange_wide(jnp.concatenate([in_parts[0], gains], axis=2))
    z_parts = exchange_wide(in_parts[1])
    x_full = gather_narrow(x_parts).transpose(1, 0, 2, 3).reshape(D, chans + 2)
    z_full = gather_narrow(z_parts).transpose(1, 0, 2, 3).reshape(D, chans)
    weight_x = pad_to(x_full[:, :chans], 1, wid)
    weight_z = pad_to(z_full, 1, wid)
    gain_one = x_full[:, chans].astype(f32)
    gain_two = x_full[:, chans + 1].astype(f32)

    channel_pack = jnp.concatenate(
        [
            conv_weight.T,
            conv_bias[:, None],
            step_bias[:, None],
            skip_weight[:, None],
            decay_log.T,
            step_weight.T,
            select_weight,
        ],
        axis=1,
    )
    packed = gather_narrow(channel_pack).reshape(chans, channel_pack.shape[1])
    packed = pad_to(packed, 0, wid)
    flat = packed[:, : CONV + 3 + NS].T.astype(f32)
    taps, conv_shift, step_shift, skip = flat[:CONV], flat[CONV], flat[CONV + 1], flat[CONV + 2]
    a_neg = -jnp.exp(flat[CONV + 3 :])
    a2 = a_neg * (1.0 / LN2)
    at = CONV + 3 + NS
    weight_step = packed[:, at : at + DT_RANK]
    weight_sel = pad_to(packed[:, at + DT_RANK :], 1, LANES)
    weight_out = pad_to(gather_narrow(out_weight).reshape(chans, D), 0, wid)

    up_parts = up_weight.reshape(EXPERTS, d_rows, wide, ff).transpose(2, 1, 0, 3)
    up_parts = up_parts.reshape(wide, d_rows, EXPERTS * ff)
    router_parts = jnp.broadcast_to(router_weight[None], (wide, d_rows, EXPERTS))
    up_parts = exchange_wide(jnp.concatenate([up_parts, router_parts], axis=2))
    up_full = gather_narrow(up_parts).transpose(1, 0, 2, 3).reshape(D, EXPERTS * ff + EXPERTS)
    up_cols = -(-(EXPERTS * ff + EXPERTS) // LANES) * LANES
    up_full = pad_to(up_full, 1, up_cols)
    down_full = gather_narrow(down_weight).transpose(1, 0, 2, 3).reshape(EXPERTS * ff, D)

    cot_ext = jnp.concatenate(
        [cotangent[0], pad_to(routes[0].astype(bf16)[:, None], 1, LANES)], axis=1
    )
    cot_all = gather_wide(cot_ext)
    second = cot_all[:, D : D + 1] > 0.5
    count = lengths[0]
    valid_all = jnp.arange(length)[:, None] < count
    up_low = jnp.where(valid_all, cot_all[:, :D], jnp.zeros((), bf16))
    valid_own = (w * rows + jnp.arange(rows))[:, None] < count
    upstream = jnp.where(valid_own, cotangent[0].astype(f32), 0.0)

    values = tokens_all.astype(f32)
    inverse_all = lax.rsqrt(jnp.mean(values * values, axis=-1, keepdims=True) + EPSILON)
    normed = (values * inverse_all * gain_one).astype(bf16)
    proj_x = mm(normed, weight_x)
    padded = jnp.concatenate([jnp.zeros((CONV - 1, wid), f32), proj_x], axis=0)
    conv_sum = conv_shift + sum(taps[k] * padded[k : k + length] for k in range(CONV))
    conv_gate = jax.nn.sigmoid(conv_sum)
    conv_act = (conv_sum * conv_gate).astype(bf16)
    selected = reduce_wide(mm(conv_act, weight_sel))
    proj_z = mm(normed, weight_z)
    step_low = selected[:, :DT_RANK]
    step_lin = mm_t(step_low, weight_step) + step_shift
    step_size = jax.nn.softplus(step_lin)
    turned = selected[:, DT_RANK:sel_cols].astype(f32).T
    in_sel, out_sel = turned[:NS], turned[NS:]
    scanned, kept, end = scan_forward(conv_act, step_size, in_sel, out_sel, a2)
    conv_full = conv_act.astype(f32)
    mixer_out = scanned + skip * conv_full
    z_gate = jax.nn.sigmoid(proj_z)
    silu_z = proj_z * z_gate
    gated = (mixer_out * silu_z).astype(bf16)
    hidden_one = tokens_own + scatter_wide(mm(gated, weight_out).astype(bf16))
    inverse_two = lax.rsqrt(jnp.mean(hidden_one * hidden_one, axis=-1, keepdims=True) + EPSILON)
    normed_two = gather_wide((hidden_one * inverse_two * gain_two).astype(bf16))

    raised = mm(normed_two, up_full)
    logits = raised[:, EXPERTS * ff : EXPERTS * ff + EXPERTS]
    probs = jax.nn.softmax(logits, axis=-1)
    onehot = jnp.concatenate([~second, second], axis=1).astype(f32)
    gate = jnp.sum(probs * onehot, axis=-1, keepdims=True)
    pre = jnp.where(second, raised[:, ff : 2 * ff], raised[:, :ff])
    bell = (1.0 + lax.erf(pre * (1.0 / math.sqrt(2.0)))) * 0.5
    hidden = (pre * bell).astype(bf16)
    slope = bell + pre * jnp.exp(-0.5 * pre * pre) * (1.0 / math.sqrt(2.0 * math.pi))
    zero = jnp.zeros((), bf16)

    def split(v):
        return [jnp.where(second, zero, v), jnp.where(second, v, zero)]

    hidden_both = jnp.concatenate(split(hidden), axis=1)
    expert_part = mm(hidden_both, down_full).astype(bf16)

    lowered = mm_t(up_low, down_full)
    d_hid = jnp.where(second, lowered[:, ff:], lowered[:, :ff])
    d_gate = jnp.sum(hidden.astype(f32) * d_hid, axis=-1, keepdims=True)
    d_pre = (gate * d_hid * slope).astype(bf16)
    d_logits = (probs * d_gate * (onehot - gate)).astype(bf16)
    d_both = pad_to(jnp.concatenate(split(d_pre) + [d_logits], axis=1), 1, up_cols)
    d_normed_two = scatter_wide(mm_t(d_both, up_full).astype(bf16))
    expert_out = scatter_wide(expert_part)
    gate_own = lax.dynamic_slice_in_dim(gate, w * rows, rows, 0)
    output = (hidden_one + gate_own * expert_out).astype(bf16)
    d_hidden_one = upstream + norm_backward(hidden_one, inverse_two, gain_two, d_normed_two)
    d_mix = gather_wide(d_hidden_one.astype(bf16))

    d_expert = (gate * up_low.astype(f32)).astype(bf16)
    grad_down = t_mm(hidden_both, d_expert).astype(bf16)
    grad_down = grad_down.reshape(EXPERTS, narrow, f_rows, D).transpose(1, 0, 2, 3)
    grad_down = scatter_narrow(grad_down)
    grad_up = t_mm(normed_two, d_both)[:, : EXPERTS * ff + EXPERTS].astype(bf16)
    grad_up = grad_up.reshape(wide, narrow, d_rows, EXPERTS * ff + EXPERTS).transpose(1, 0, 2, 3)
    grad_up = exchange_wide(scatter_narrow(grad_up).astype(bf16)).astype(f32)
    grad_router = jnp.sum(grad_up[:, :, EXPERTS * ff :], axis=0)
    grad_up = grad_up[:, :, : EXPERTS * ff].reshape(wide, d_rows, EXPERTS, ff)
    grad_up = grad_up.transpose(2, 1, 0, 3).reshape(EXPERTS, d_rows, FF)
    grad_gain_two = (
        jnp.sum(up_weight.astype(f32) * grad_up, axis=(0, 2))
        + jnp.sum(router_weight.astype(f32) * grad_router, axis=1)
    ) / expert_gain.astype(f32)

    d_gated = mm_t(d_mix, weight_out)
    grad_out = t_mm(gated, d_mix).astype(bf16)[:chans].reshape(narrow, c_rows, D)
    grad_out = scatter_narrow(grad_out)
    d_mixer = d_gated * silu_z
    d_z = (d_gated * mixer_out * (z_gate * (1.0 + proj_z * (1.0 - z_gate)))).astype(bf16)
    grad_skip = jnp.sum(d_mixer * conv_full, axis=0)
    d_step, d_conv_scan, d_in, d_out, d_a = scan_backward(
        conv_act, step_size, d_mixer, in_sel, out_sel, a2, kept, end
    )
    grad_decay = d_a * a_neg
    step_grad = d_step * jax.nn.sigmoid(step_lin)
    grad_step_bias = jnp.sum(step_grad, axis=0)
    step_grad_low = step_grad.astype(bf16)
    d_sel = jnp.concatenate([mm(step_grad_low, weight_step), d_in.T, d_out.T], axis=1)
    d_sel = reduce_wide(pad_to(d_sel, 1, LANES))
    grad_step = t_mm(step_grad_low, step_low)
    grad_sel = t_mm(conv_act, d_sel)[:, :sel_cols]
    d_act = mm_t(d_sel, weight_sel) + skip * d_mixer + d_conv_scan
    d_conv = d_act * (conv_gate * (1.0 + conv_sum * (1.0 - conv_gate)))
    grad_conv_bias = jnp.sum(d_conv, axis=0)
    grad_conv = jnp.stack(
        [jnp.sum(d_conv * padded[k : k + length], axis=0) for k in range(CONV)], axis=1
    )
    d_ext = jnp.concatenate([d_conv, jnp.zeros((CONV - 1, wid), f32)], axis=0)
    d_x = sum(taps[k] * d_ext[CONV - 1 - k : CONV - 1 - k + length] for k in range(CONV))
    d_x = d_x.astype(bf16)
    d_normed = scatter_wide((mm_t(d_x, weight_x) + mm_t(d_z, weight_z)).astype(bf16))
    inverse_one = lax.rsqrt(jnp.mean(tokens_own * tokens_own, axis=-1, keepdims=True) + EPSILON)
    token_grad = d_hidden_one + norm_backward(tokens_own, inverse_one, gain_one, d_normed)

    def in_grad(d_part):
        grad = t_mm(normed, d_part)[:, :chans].astype(bf16)
        grad = grad.reshape(wide, narrow, d_rows, chans).transpose(1, 0, 2, 3)
        grad = exchange_wide(scatter_narrow(grad).astype(bf16))
        return grad.astype(f32).transpose(1, 0, 2).reshape(d_rows, DI)

    grad_in = jnp.concatenate([in_grad(d_x), in_grad(d_z)], axis=1)
    grad_gain_one = jnp.sum(in_weight.astype(f32) * grad_in, axis=1) / mixer_gain.astype(f32)

    channel_grads = jnp.concatenate(
        [
            grad_conv,
            grad_conv_bias[:, None],
            grad_step_bias[:, None],
            grad_skip[:, None],
            grad_decay.T,
            grad_step,
            grad_sel,
        ],
        axis=1,
    ).astype(bf16)
    channel_grads = channel_grads[:chans].reshape(narrow, c_rows, channel_grads.shape[1])
    channel_grads = scatter_narrow(channel_grads)
    flat_grads = channel_grads[:, :at].T
    return (
        output[None],
        token_grad[None],
        grad_gain_one,
        grad_in,
        flat_grads[:CONV],
        flat_grads[CONV],
        channel_grads[:, at + DT_RANK :],
        channel_grads[:, at : at + DT_RANK].T,
        flat_grads[CONV + 1],
        flat_grads[CONV + 3 :],
        flat_grads[CONV + 2],
        grad_out,
        grad_gain_two,
        grad_router,
        grad_up,
        grad_down,
    )


def solution(mesh):
    both = ("wide", "narrow")
    return jax.shard_map(
        local,
        mesh=mesh,
        in_specs=(
            P("narrow", "wide", None),
            P(both),
            P(both, None),
            P(None, both),
            P(both),
            P(both, None),
            P(None, both),
            P(both),
            P(None, both),
            P(both),
            P(both, None),
            P(both),
            P(both, None),
            P(None, both, None),
            P(None, both, None),
            P("narrow", "wide"),
            P("narrow"),
            P("narrow", "wide", None),
        ),
        out_specs=(
            P("narrow", "wide", None),
            P("narrow", "wide", None),
            P(both),
            P(both, None),
            P(None, both),
            P(both),
            P(both, None),
            P(None, both),
            P(both),
            P(None, both),
            P(both),
            P(both, None),
            P(both),
            P(both, None),
            P(None, both, None),
            P(None, both, None),
        ),
        check_vma=False,
    )
```

```python
import math

import jax
import jax.numpy as jnp
from jax import lax
from jax.experimental import pallas as pl
from jax.experimental.pallas import tpu as pltpu
from jax.sharding import PartitionSpec as P

D = 1152
DI = 2304
NS = 16
DT_RANK = 72
CONV = 4
FF = 3072
EXPERTS = 2
EPSILON = 1e-05
TIME_BLOCK = 128
VMEM = 40 * 2**20
LANES = 128
LN2 = math.log(2.0)

f32 = jnp.float32
bf16 = jnp.bfloat16


def relative():
    return lax.axis_size("wide") == 8


def swap(x, k):
    n = lax.axis_size("wide")
    return lax.ppermute(x, "wide", [(i, i ^ k) for i in range(n)])


def turn(x, k):
    n = lax.axis_size("narrow")
    return lax.ppermute(x, "narrow", [(i, (i + k) % n) for i in range(n)])


def pick(x, i, axis=0):
    return lax.dynamic_index_in_dim(x, i, axis, False)


def gather_wide(block, meanwhile=None):
    if not relative():
        made = meanwhile(block) if meanwhile else ()
        return lax.all_gather(block, "wide", axis=0, tiled=True), made
    half = block.shape[0] // 2
    mate = swap(block, 1)
    a, b = swap(block, 2), swap(block, 4)
    made = ()
    if meanwhile:
        made = meanwhile(block)
        a, b, made = lax.optimization_barrier((a, b, made))
    c0, c1 = swap(a[:half], 4), swap(b[half:], 2)
    out = jnp.concatenate(
        [block, mate, a, swap(a, 1), b, swap(b, 1), c0, c1, swap(c0, 1), swap(c1, 1)], axis=0
    )
    return out, made


def scatter_wide(partial):
    if not relative():
        return lax.psum_scatter(partial, "wide", scatter_dimension=0, tiled=True).astype(f32)
    rows = partial.shape[0] // 8
    half = rows // 2
    parts = partial.reshape(8, rows, partial.shape[1])

    def summed(q):
        return parts[2 * q].astype(f32) + swap(parts[2 * q + 1], 1).astype(f32)

    far = summed(3).astype(bf16)
    r0, r1 = swap(far[:half], 2), swap(far[half:], 4)
    sx, sy = summed(1), summed(2)
    x0, y1 = swap(sx[:half].astype(bf16), 2), swap(sy[half:].astype(bf16), 4)
    x1 = swap((sx[half:] + r1.astype(f32)).astype(bf16), 2)
    y0 = swap((sy[:half] + r0.astype(f32)).astype(bf16), 4)
    x = jnp.concatenate([x0, x1], axis=0).astype(f32)
    y = jnp.concatenate([y0, y1], axis=0).astype(f32)
    return summed(0) + x + y


def reduce_wide(partial, meanwhile):
    if not relative():
        return lax.psum(partial, "wide"), meanwhile(partial)
    core = lax.axis_index("wide") % 2
    half = partial.shape[0] // 2
    parts = partial.reshape(2, half, partial.shape[1])
    total = pick(parts, core).astype(f32) + swap(pick(parts, 1 - core), 1).astype(f32)
    low = total.astype(bf16)
    got = [swap(low, 2), swap(low, 4), swap(low, 6)]
    got, made = lax.optimization_barrier((got, meanwhile(low)))
    total = total + sum(p.astype(f32) for p in got)
    low = total.astype(bf16)
    mate = swap(low, 1)
    first = core == 0
    out = jnp.concatenate([jnp.where(first, low, mate), jnp.where(first, mate, low)], axis=0)
    return out, made


def after(x, *others):
    return lax.optimization_barrier((x,) + others)[0]


def turns(x):
    return [x] + [turn(x, k) for k in range(1, lax.axis_size("narrow"))]


def pad_to(x, axis, size):
    pads = [(0, 0)] * x.ndim
    pads[axis] = (0, size - x.shape[axis])
    return jnp.pad(x, pads)


def gather_channels(x, splits, total):
    n, z = lax.axis_size("narrow"), lax.axis_index("narrow")
    rows, cols = x.shape
    pieces = [x] + [turn(x, k) for k in range(1, n)]
    order = jnp.stack([(z - k) % n * rows for k in range(n)]).astype(jnp.int32)

    def kernel(order_ref, *refs):
        value = jnp.zeros((total, cols), f32)
        r = lax.broadcasted_iota(jnp.int32, (total, rows), 0)
        j = lax.broadcasted_iota(jnp.int32, (total, rows), 1)
        for k in range(n):
            spots = jnp.where(r == j + order_ref[k], 1.0, 0.0).astype(bf16)
            value = value + jnp.dot(spots, refs[k][...], preferred_element_type=f32)
        value = value.astype(bf16)
        at = 0
        for out in refs[n:]:
            out[...] = value[:, at : at + out.shape[1]]
            at += out.shape[1]

    vmem = pl.BlockSpec(memory_space=pltpu.VMEM)
    return pl.pallas_call(
        kernel,
        in_specs=[pl.BlockSpec(memory_space=pltpu.SMEM)] + [vmem] * n,
        out_specs=[vmem] * len(splits),
        out_shape=[jax.ShapeDtypeStruct((total, c), bf16) for c in splits],
        compiler_params=pltpu.CompilerParams(vmem_limit_bytes=VMEM),
    )(order, *pieces)


def turned(pieces):
    return [pieces[0]] + [turn(pieces[k], k) for k in range(1, len(pieces))]


def split_narrow(x, axis):
    n, z = lax.axis_size("narrow"), lax.axis_index("narrow")
    return [pick(x, (z + k) % n, axis) for k in range(n)]


def exchange(x):
    return lax.all_to_all(x, ("wide", "narrow"), 0, 0)


def gather_rows(parts):
    wide, rows, cols = parts.shape
    narrow = lax.axis_size("narrow")
    parts = jnp.broadcast_to(parts[:, None], (wide, narrow, rows, cols))
    got = exchange(parts.reshape(wide * narrow, rows, cols))
    return got.reshape(wide * narrow * rows, cols)


def scatter_rows(grad, rows):
    wide, narrow = lax.axis_size("wide"), lax.axis_size("narrow")
    got = exchange(grad.reshape(wide * narrow, rows, grad.shape[1]))
    return got.reshape(wide, narrow, rows, grad.shape[1])


def summed_rows(got):
    return sum(got[:, k].astype(f32) for k in range(got.shape[1]))


def mm(a, b):
    return jnp.dot(a, b, preferred_element_type=f32)


def mm_t(a, b):
    return lax.dot_general(a, b, (((1,), (1,)), ((), ())), preferred_element_type=f32)


def t_mm(a, b):
    return lax.dot_general(a, b, (((0,), (0,)), ((), ())), preferred_element_type=f32)


def sigmoid(v):
    return 1.0 / (1.0 + jnp.exp(-v))


def softplus(v):
    return jnp.maximum(v, 0.0) + jnp.log1p(jnp.exp(-jnp.abs(v)))


def call(kernel, grid, flip, ins, outs, scratch, flops, exps=0):
    def spec(block, where):
        if where is None:
            zeros = (0,) * len(block)
            return pl.BlockSpec(block, lambda i, s: zeros)
        return pl.BlockSpec(block, lambda i, s: (where(i, s[0]),) + (0,) * (len(block) - 1))

    size = sum(a.size * a.dtype.itemsize for a, _, _ in ins)
    size += sum(math.prod(o[0]) * jnp.dtype(o[1]).itemsize for o in outs)
    return pl.pallas_call(
        kernel,
        grid_spec=pltpu.PrefetchScalarGridSpec(
            num_scalar_prefetch=1,
            grid=(grid,),
            in_specs=[spec(b, f) for _, b, f in ins],
            out_specs=[spec(b, f) for _, _, b, f in outs],
            scratch_shapes=scratch,
        ),
        out_shape=[jax.ShapeDtypeStruct(o[0], o[1]) for o in outs],
        compiler_params=pltpu.CompilerParams(vmem_limit_bytes=VMEM),
        cost_estimate=pl.CostEstimate(flops=flops, bytes_accessed=size, transcendentals=exps),
    )(flip, *[a for a, _, _ in ins])


def front(flip, tokens, gain, weight_x, taps, shift, weight_sel):
    length, wid = tokens.shape[0], weight_x.shape[1]
    blocks = lax.axis_size("wide")
    rows = length // blocks

    def kernel(s_ref, tok, gain_r, wx, taps_r, shift_r, wsel, normed, proj, conv, act, part, pad):
        @pl.when(pl.program_id(0) == 0)
        def _():
            pad[:8, :] = jnp.zeros((8, wid), f32)

        values = tok[...].astype(f32)
        inverse = lax.rsqrt(jnp.mean(values * values, axis=-1, keepdims=True) + EPSILON)
        low = (values * inverse * gain_r[...]).astype(bf16)
        normed[...] = low
        x = mm(low, wx[...])
        proj[...] = x
        pad[8:, :] = x
        total = shift_r[...] + taps_r[CONV - 1 : CONV, :] * x
        for k in range(CONV - 1):
            start = 8 - (CONV - 1) + k
            total = total + taps_r[k : k + 1, :] * pad[start : start + rows, :]
        pad[:8, :] = x[rows - 8 :, :]
        conv[...] = total
        low = (total * sigmoid(total)).astype(bf16)
        act[...] = low
        part[...] = mm(low, wsel[...]).astype(bf16)

    here = lambda i, s: i
    rel = lambda i, s: i ^ s
    return call(
        kernel,
        blocks,
        flip,
        [
            (tokens, (rows, D), rel),
            (gain, (1, D), None),
            (weight_x, (D, wid), None),
            (taps, (CONV, wid), None),
            (shift, (1, wid), None),
            (weight_sel, (wid, LANES), None),
        ],
        [
            ((length, D), bf16, (rows, D), rel),
            ((length, wid), f32, (rows, wid), here),
            ((length, wid), f32, (rows, wid), here),
            ((length, wid), bf16, (rows, wid), here),
            ((length, LANES), bf16, (rows, LANES), here),
        ],
        [pltpu.VMEM((rows + 8, wid), f32)],
        2 * length * wid * (D + LANES),
    )


FLAT = CONV + 4 + NS
def row_sums(terms, masks):
    high, mid, low = masks
    c = [
        jnp.where(high, terms[i + 4], terms[i])
        + pltpu.roll(jnp.where(high, terms[i], terms[i + 4]), 4, 0)
        for i in range(4)
    ]
    c = [
        jnp.where(mid, c[i + 2] + pltpu.roll(c[i + 2], 2, 0), c[i] + pltpu.roll(c[i], 6, 0))
        for i in range(2)
    ]
    return jnp.where(low, c[1] + pltpu.roll(c[1], 1, 0), c[0] + pltpu.roll(c[0], 7, 0))


def row_masks(wid):
    row = lax.broadcasted_iota(jnp.int32, (8, wid), 0)
    return row >= 4, (row & 2) > 0, (row & 1) > 0


IN_AT = DT_RANK
OUT_AT = DT_RANK + NS


def middle(flip, sel, act, proj_z, weight_step, shift, skip, a2, weight_out):
    length, wid = act.shape
    blocks = length // TIME_BLOCK
    per = blocks // lax.axis_size("wide")

    def kernel(
        s_ref, sel_r, act_r, z_r, wstep, shift_r, skip_r, a_r, wout, lin_o, kept, end, mixed, gated_o, part, state, dt_s, u_s, y_s
    ):
        @pl.when(pl.program_id(0) == 0)
        def _():
            state[...] = jnp.zeros_like(state)

        low = sel_r[...]
        lin = mm_t(low, wstep[...]) + shift_r[...]
        lin_o[...] = lin
        dt_s[...] = softplus(lin)
        u_s[...] = dt_s[...] * act_r[...].astype(f32)
        turned = low.astype(f32).T
        in_sel, out_sel = turned[IN_AT : IN_AT + NS, :], turned[OUT_AT : OUT_AT + NS, :]
        a2 = a_r[...]

        masks = row_masks(wid)
        h = state[...]
        terms = [None] * 8
        for t in range(TIME_BLOCK):
            kept[t] = h
            h = jnp.exp2(dt_s[t : t + 1, :] * a2) * h + u_s[t : t + 1, :] * in_sel[:, t : t + 1]
            y = h * out_sel[:, t : t + 1]
            terms[t % 8] = y[:8] + y[8:]
            if t % 8 == 7:
                y_s[t - 7 : t + 1, :] = row_sums(terms, masks)
        state[...] = h
        end[...] = h
        out = y_s[...] + skip_r[...] * act_r[...].astype(f32)
        mixed[...] = out
        z = z_r[...]
        gated = (out * z * sigmoid(z)).astype(bf16)
        gated_o[...] = gated
        part[...] = mm(gated, wout[...]).astype(bf16)

    here = lambda i, s: i
    rel = lambda i, s: ((i // per) ^ s) * per + i % per
    row = (TIME_BLOCK, wid)
    return call(
        kernel,
        blocks,
        flip,
        [
            (sel, (TIME_BLOCK, LANES), here),
            (act, row, here),
            (proj_z, row, rel),
            (weight_step, (wid, LANES), None),
            (shift, (1, wid), None),
            (skip, (1, wid), None),
            (a2, (NS, wid), None),
            (weight_out, (wid, D), None),
        ],
        [
            ((length, wid), f32, row, here),
            ((length, NS, wid), f32, (TIME_BLOCK, NS, wid), here),
            ((NS, wid), f32, (NS, wid), None),
            ((length, wid), f32, row, here),
            ((length, wid), bf16, row, rel),
            ((length, D), bf16, (TIME_BLOCK, D), rel),
        ],
        [pltpu.VMEM((NS, wid), f32)] + [pltpu.VMEM(row, f32)] * 3,
        length * wid * (8 * NS + 2 * D + 2 * LANES),
        length * NS * wid,
    )


def experts(span, normed, cot, up, down, ff):
    length = normed.shape[0]
    blocks = lax.axis_size("wide")
    rows = length // blocks
    cols = up.shape[1]

    def kernel(s_ref, n_r, cot_r, up_r, down_r, out_part, back_part, hid_o, both_o, dex_o):
        i = pl.program_id(0)
        position = (i ^ s_ref[0]) * rows + lax.broadcasted_iota(jnp.int32, (rows, 1), 0)
        cot_b = cot_r[...]
        second = cot_b[:, D : D + 1] > 0.5
        upstream = jnp.where(position < s_ref[1], cot_b[:, :D], jnp.zeros((), bf16))
        raised = mm(n_r[...], up_r[...])
        first_l, second_l = raised[:, EXPERTS * ff : EXPERTS * ff + 1], raised[:, EXPERTS * ff + 1 : EXPERTS * ff + 2]
        lead = jnp.where(second, second_l - first_l, first_l - second_l)
        gate = sigmoid(lead)
        other = sigmoid(-lead)
        pre = jnp.where(second, raised[:, ff : 2 * ff], raised[:, :ff])
        bell = (1.0 + lax.erf(pre * (1.0 / math.sqrt(2.0)))) * 0.5
        hidden = pre * bell
        slope = bell + pre * jnp.exp(-0.5 * pre * pre) * (1.0 / math.sqrt(2.0 * math.pi))
        hidden = hidden.astype(bf16)
        hid_f = hidden.astype(f32)
        both = jnp.concatenate(
            [jnp.where(second, 0.0, hid_f), jnp.where(second, hid_f, 0.0)], axis=1
        ).astype(bf16)
        hid_o[...] = both
        out_part[...] = (gate * mm(both, down_r[...])).astype(bf16)
        dex_o[...] = (gate * upstream.astype(f32)).astype(bf16)
        lowered = mm_t(upstream, down_r[...])
        d_hid = jnp.where(second, lowered[:, ff:], lowered[:, :ff])
        d_gate = jnp.sum(hid_f * d_hid, axis=-1, keepdims=True)
        d_pre = gate * d_hid * slope
        d_lead = gate * other * d_gate
        lane = lax.broadcasted_iota(jnp.int32, (rows, cols - EXPERTS * ff), 1)
        d_second = jnp.where(second, d_lead, -d_lead)
        d_logits = jnp.where(lane == 1, d_second, jnp.where(lane == 0, -d_second, 0.0))
        d_both = jnp.concatenate(
            [jnp.where(second, 0.0, d_pre), jnp.where(second, d_pre, 0.0), d_logits], axis=1
        ).astype(bf16)
        both_o[...] = d_both
        back_part[...] = mm_t(d_both, up_r[...]).astype(bf16)

    here = lambda i, s: i
    return call(
        kernel,
        blocks,
        span,
        [
            (normed, (rows, D), here),
            (cot, (rows, D + LANES), lambda i, s: i ^ s),
            (up, up.shape, None),
            (down, down.shape, None),
        ],
        [
            ((length, D), bf16, (rows, D), lambda i, s: i ^ s),
            ((length, D), bf16, (rows, D), here),
            ((length, EXPERTS * ff), bf16, (rows, EXPERTS * ff), here),
            ((length, cols), bf16, (rows, cols), here),
            ((length, D), bf16, (rows, D), here),
        ],
        [],
        4 * length * D * (cols + EXPERTS * ff),
        3 * length * ff,
    )


def back(flip, d_mix, weight_out, sel, act, proj_z, lin, mixed, kept, end, weight_step, skip, a2):
    length, wid = act.shape
    blocks = length // TIME_BLOCK
    per = blocks // lax.axis_size("wide")

    def kernel(
        s_ref, mix_r, wout, sel_r, act_r, z_r, lin_r, mixed_r, kept_r, end_r, wstep, skip_r, a_r,
        dz_o, part, dact_o, gstep_o, da_o, dskip_o, dbias_o,
        lam_s, next_s, pb_s, pc_s, dt_s, u_s, dy_s, s1_s, s2_s, turned_s,
    ):
        @pl.when(pl.program_id(0) == 0)
        def _():
            lam_s[...] = jnp.zeros_like(lam_s)
            next_s[...] = end_r[...]
            da_o[...] = jnp.zeros_like(da_o)
            for ref in (gstep_o, dskip_o, dbias_o):
                ref[...] = jnp.zeros_like(ref)
            turned_s[...] = jnp.zeros_like(turned_s)

        d_gated = mm_t(mix_r[...], wout[...])
        z = z_r[...]
        s = sigmoid(z)
        dz_o[...] = (d_gated * mixed_r[...] * (s * (1.0 + z * (1.0 - s)))).astype(bf16)
        dy_s[...] = d_gated * (z * s)
        x_all = act_r[...].astype(f32)
        dskip_o[...] += jnp.sum(dy_s[...] * x_all, axis=0, keepdims=True)
        dt_s[...] = softplus(lin_r[...])
        u_s[...] = dt_s[...] * x_all
        low = sel_r[...]
        turned = low.astype(f32).T
        in_sel, out_sel = turned[IN_AT : IN_AT + NS, :], turned[OUT_AT : OUT_AT + NS, :]
        a2 = a_r[...]

        def fold(v):
            total = v[:, :LANES]
            for k in range(1, wid // LANES):
                total = total + v[:, k * LANES : (k + 1) * LANES]
            return total

        masks = row_masks(wid)
        p, after, acc = lam_s[...], next_s[...], da_o[...]
        first, second = [None] * 8, [None] * 8
        for t in range(TIME_BLOCK - 1, -1, -1):
            before = kept_r[t]
            dt_t, dy_t = dt_s[t : t + 1, :], dy_s[t : t + 1, :]
            lam = dy_t * out_sel[:, t : t + 1] + p
            p = lam * jnp.exp2(dt_t * a2)
            moved = p * before
            acc = acc + dt_t * moved
            term = lam * in_sel[:, t : t + 1]
            first[t % 8] = term[:8] + term[8:]
            term = a2 * moved
            second[t % 8] = term[:8] + term[8:]
            if t % 8 == 0:
                s1_s[t : t + 8, :] = row_sums(first, masks)
                s2_s[t : t + 8, :] = row_sums(second, masks)
            pb_s[t] = fold(lam * u_s[t : t + 1, :])
            pc_s[t] = fold(after * dy_t)
            after = before
        lam_s[...] = p
        next_s[...] = after
        da_o[...] = acc
        ones = jnp.ones((LANES, LANES), bf16)
        lane = lax.broadcasted_iota(jnp.int32, (NS, TIME_BLOCK), 1)
        for source, at in ((pb_s, IN_AT), (pc_s, OUT_AT)):
            sums = mm(source[...].reshape(TIME_BLOCK * NS, LANES).astype(bf16), ones)
            sums = sums.reshape(TIME_BLOCK, NS, LANES)
            parts = [jnp.zeros((NS, TIME_BLOCK), f32)] * 4
            for t in range(TIME_BLOCK):
                parts[t % 4] = jnp.where(lane == t, sums[t], parts[t % 4])
            turned_s[at : at + NS, :] = (parts[0] + parts[1]) + (parts[2] + parts[3])
        through = s1_s[...]
        d_step = s2_s[...] * LN2 + x_all * through
        dact_o[...] = dt_s[...] * through + skip_r[...] * dy_s[...]
        grad = d_step * sigmoid(lin_r[...])
        dbias_o[...] += jnp.sum(grad, axis=0, keepdims=True)
        grad = grad.astype(bf16)
        gstep_o[...] += t_mm(grad, low)
        part[...] = (mm(grad, wstep[...]) + turned_s[...].T).astype(bf16)

    here = lambda i, s: blocks - 1 - i
    rel = lambda i, s: (((blocks - 1 - i) // per) ^ s) * per + (blocks - 1 - i) % per
    row = (TIME_BLOCK, wid)
    one = ((1, wid), f32, (1, wid), None)
    return call(
        kernel,
        blocks,
        flip,
        [
            (d_mix, (TIME_BLOCK, D), rel),
            (weight_out, (wid, D), None),
            (sel, (TIME_BLOCK, LANES), here),
            (act, row, here),
            (proj_z, row, rel),
            (lin, row, here),
            (mixed, row, here),
            (kept, (TIME_BLOCK, NS, wid), here),
            (end, (NS, wid), None),
            (weight_step, (wid, LANES), None),
            (skip, (1, wid), None),
            (a2, (NS, wid), None),
        ],
        [
            ((length, wid), bf16, row, rel),
            ((length, LANES), bf16, (TIME_BLOCK, LANES), here),
            ((length, wid), f32, row, here),
            ((wid, LANES), f32, (wid, LANES), None),
            ((NS, wid), f32, (NS, wid), None),
            one,
            one,
        ],
        [pltpu.VMEM((NS, wid), f32)] * 2
        + [pltpu.VMEM((TIME_BLOCK, NS, LANES), f32)] * 2
        + [pltpu.VMEM(row, f32)] * 5
        + [pltpu.VMEM((LANES, TIME_BLOCK), f32)],
        length * wid * (20 * NS + 2 * D + 2 * LANES),
        length * NS * wid,
    )


def tail(
    flip, d_sel, d_act, conv, proj, d_z, normed, act, weight_x, weight_z, weight_sel, taps,
    grad_step, grad_flat, chans,
):
    length, wid = act.shape
    blocks = lax.axis_size("wide")
    rows = length // blocks

    def kernel(
        s_ref, sel_r, dact_r, conv_r, proj_r, dz_r, n_r, act_r, wx, wz, wsel, taps_r, gstep_r, flat_r,
        part, *refs,
    ):
        gx_o, pack_o, ext, gx, gsel, flat = refs

        @pl.when(pl.program_id(0) == 0)
        def _():
            ext[rows:, :] = jnp.zeros((8, wid), f32)
            gx[...] = jnp.zeros_like(gx)
            gsel[...] = jnp.zeros_like(gsel)
            flat[...] = flat_r[...]

        low = sel_r[...]
        c = conv_r[...]
        q = sigmoid(c)
        d_conv = (mm_t(low, wsel[...]) + dact_r[...]) * (q * (1.0 + c * (1.0 - q)))
        ext[:rows, :] = d_conv
        flat[CONV : CONV + 1, :] += jnp.sum(d_conv, axis=0, keepdims=True)
        x = proj_r[...]
        d_x = jnp.zeros((rows, wid), f32)
        for k in range(CONV):
            moved = ext[CONV - 1 - k : CONV - 1 - k + rows, :]
            d_x = d_x + taps_r[k : k + 1, :] * moved
            flat[k : k + 1, :] += jnp.sum(moved * x, axis=0, keepdims=True)
        ext[rows:, :] = d_conv[:8, :]
        d_x = d_x.astype(bf16)
        part[...] = (mm_t(d_x, wx[...]) + mm_t(dz_r[...], wz[...])).astype(bf16)
        gx[...] += t_mm(n_r[...], d_x)
        gsel[...] += t_mm(act_r[...], low)

        @pl.when(pl.program_id(0) == blocks - 1)
        def _():
            gx_o[...] = gx[:, :chans].astype(bf16)
            tall = jnp.concatenate(
                [jnp.zeros((DT_RANK, wid), f32), flat[...], jnp.zeros((LANES - DT_RANK - FLAT, wid), f32)], axis=0
            )
            lane = lax.broadcasted_iota(jnp.int32, (wid, LANES), 1)
            left = jnp.where(lane < DT_RANK, gstep_r[...], tall.T)
            pack = jnp.concatenate([left, gsel[...]], axis=1).astype(bf16)
            pack_o[...] = pack[:chans]

    here = lambda i, s: blocks - 1 - i
    rel = lambda i, s: (blocks - 1 - i) ^ s
    row = (rows, wid)
    pack = (chans, 2 * LANES)
    return call(
        kernel,
        blocks,
        flip,
        [
            (d_sel, (rows, LANES), here),
            (d_act, row, here),
            (conv, row, here),
            (proj, row, here),
            (d_z, row, rel),
            (normed, (rows, D), rel),
            (act, row, here),
            (weight_x, (D, wid), None),
            (weight_z, (D, wid), None),
            (weight_sel, (wid, LANES), None),
            (taps, (CONV, wid), None),
            (grad_step, (wid, LANES), None),
            (grad_flat, (FLAT, wid), None),
        ],
        [((length, D), bf16, (rows, D), rel), ((D, chans), bf16, (D, chans), None), (pack, bf16, pack, None)],
        [
            pltpu.VMEM((rows + 8, wid), f32),
            pltpu.VMEM((D, wid), f32),
            pltpu.VMEM((wid, LANES), f32),
            pltpu.VMEM((FLAT, wid), f32),
        ],
        2 * length * wid * (3 * D + 2 * LANES),
    )


def row_grad(flip, a, b, cols):
    length, total = a.shape
    n = b.shape[1]
    blocks = lax.axis_size("wide")
    rows = length // blocks

    def kernel(s_ref, a_r, b_r, out, acc):
        @pl.when(pl.program_id(0) == 0)
        def _():
            acc[...] = jnp.zeros_like(acc)

        acc[...] += t_mm(a_r[...], b_r[...])

        @pl.when(pl.program_id(0) == blocks - 1)
        def _():
            out[...] = acc[:, :cols].astype(bf16)

    here = lambda i, s: i
    return call(
        kernel,
        blocks,
        flip,
        [(a, (rows, total), here), (b, (rows, n), here)],
        [((total, cols), bf16, (total, cols), None)],
        [pltpu.VMEM((total, n), f32)],
        2 * length * total * n,
    )[0]


def norm_backward(values, inverse, gain_vec, upstream):
    scaled = upstream * gain_vec
    inner_mean = jnp.mean(values * scaled, axis=-1, keepdims=True)
    return inverse * scaled - values * (inverse * inverse * inverse) * inner_mean


def local(
    tokens,
    mixer_gain,
    in_weight,
    conv_weight,
    conv_bias,
    select_weight,
    step_weight,
    step_bias,
    decay_log,
    skip_weight,
    out_weight,
    expert_gain,
    router_weight,
    up_weight,
    down_weight,
    routes,
    lengths,
    cotangent,
):
    wide, narrow = lax.axis_size("wide"), lax.axis_size("narrow")
    w = lax.axis_index("wide")
    rows = tokens.shape[1]
    chans = DI // wide
    wid = -(-chans // LANES) * LANES
    ff = FF // wide
    d_rows = D // (wide * narrow)
    c_rows = DI // (wide * narrow)
    f_rows = FF // (wide * narrow)
    both = EXPERTS * ff
    flip = w if relative() else 0 * w
    span = jnp.stack([flip, lengths[0]]).astype(jnp.int32)

    tokens_own = tokens[0].astype(f32)
    tokens_all, _ = gather_wide(tokens[0])

    in_parts = in_weight.reshape(d_rows, 2, wide, chans).transpose(1, 2, 0, 3)
    gains = jnp.stack([mixer_gain, expert_gain], axis=1)
    gains = jnp.broadcast_to(gains[None], (wide, d_rows, 2))
    x_full = gather_rows(jnp.concatenate([in_parts[0], gains], axis=2))
    weight_x = pad_to(x_full[:, :chans], 1, wid)
    gains = x_full[:, chans:].T.astype(f32)
    gain_one, gain_two = gains[:1], gains[1:]
    weight_z = pad_to(gather_rows(after(in_parts[1], x_full)), 1, wid)
    zero_col = jnp.zeros((c_rows, 1), bf16)
    channel_pack = jnp.concatenate(
        [
            conv_weight.T,
            conv_bias[:, None],
            step_bias[:, None],
            skip_weight[:, None],
            zero_col,
            decay_log.T,
            step_weight.T,
            select_weight,
        ],
        axis=1,
    )
    pack_cols = channel_pack.shape[1]
    wide_cols = -(-pack_cols // LANES) * LANES
    channel_pack = jnp.concatenate([out_weight, pad_to(channel_pack, 1, wide_cols)], axis=1)
    weight_out, packed = gather_channels(channel_pack, (D, wide_cols), wid)
    flat = packed[:, :FLAT].T.astype(f32)
    taps = flat[:CONV]
    conv_shift, step_shift, skip = (flat[CONV + k : CONV + k + 1] for k in range(3))
    a_neg = -jnp.exp(flat[CONV + 4 :])
    a2 = a_neg * (1.0 / LN2)
    weight_step = pad_to(packed[:, FLAT : FLAT + DT_RANK], 1, LANES)
    weight_sel = pad_to(packed[:, FLAT + DT_RANK : pack_cols], 1, LANES)

    normed, proj_x, conv_sum, conv_act, sel_part = front(
        flip[None], tokens_all, gain_one, weight_x, taps, conv_shift, weight_sel
    )
    sel_part, weight_z = lax.optimization_barrier((sel_part, weight_z))
    selected, proj_z = reduce_wide(sel_part, lambda low: mm(after(normed, low), weight_z))

    up_cols = -(-(both + EXPERTS) // LANES) * LANES
    up_parts = up_weight.reshape(EXPERTS, d_rows, wide, ff).transpose(2, 1, 0, 3)
    up_parts = up_parts.reshape(wide, d_rows, both)
    router_parts = jnp.broadcast_to(router_weight[None], (wide, d_rows, EXPERTS))
    up_parts = jnp.concatenate([up_parts, router_parts], axis=2)
    up_full = gather_rows(after(up_parts, selected))
    down_full = lax.all_gather(after(down_weight, selected), "narrow")
    down_full = down_full.transpose(1, 0, 2, 3).reshape(both, D)
    route_cols = jnp.broadcast_to(routes[0].astype(bf16)[:, None], (rows, LANES))
    cot_ext = jnp.concatenate([cotangent[0], route_cols], axis=1)
    cot_all = lax.all_gather(after(cot_ext, selected), "wide", axis=0, tiled=True)
    valid_own = (w * rows + jnp.arange(rows))[:, None] < lengths[0]
    upstream = jnp.where(valid_own, cotangent[0].astype(f32), 0.0)

    step_lin, kept, end, mixed, gated, mix_part = middle(
        flip[None], selected, conv_act, proj_z, weight_step, step_shift, skip, a2, weight_out
    )
    up_full = pad_to(up_full, 1, up_cols)
    hidden_one = tokens_own + scatter_wide(mix_part)
    inverse_two = lax.rsqrt(jnp.mean(hidden_one * hidden_one, axis=-1, keepdims=True) + EPSILON)
    normed_two, _ = gather_wide((hidden_one * inverse_two * gain_two).astype(bf16))
    out_part, back_part, hidden_both, d_both, d_expert = experts(
        span, normed_two, cot_all, up_full, down_full, ff
    )

    d_normed_two = scatter_wide(back_part)
    grad_down = t_mm(hidden_both, d_expert).astype(bf16)
    grad_down = split_narrow(grad_down.reshape(EXPERTS, narrow, f_rows, D), 1)
    d_normed_two = after(d_normed_two, grad_down)
    d_hidden_one = upstream + norm_backward(hidden_one, inverse_two, gain_two, d_normed_two)
    d_low = d_hidden_one.astype(bf16)
    d_mix, grad_up = gather_wide(
        d_low,
        lambda low: row_grad(flip[None], normed_two, after(d_both, low), both + EXPERTS),
    )
    grad_up = scatter_rows(after(grad_up, d_mix), d_rows)
    grad_down = turned([after(p, d_mix) for p in grad_down])
    expert_sum = lax.psum_scatter(after(out_part, d_mix), "wide", scatter_dimension=0, tiled=True)

    d_z, d_sel_part, d_act, grad_step, d_a, grad_skip, grad_step_bias = back(
        flip[None], d_mix, weight_out, selected, conv_act, proj_z, step_lin, mixed, kept, end,
        weight_step, skip, a2,
    )
    d_sel_part, grad_up, grad_down = lax.optimization_barrier((d_sel_part, grad_up, grad_down))

    def meanwhile(low):
        grad_out = t_mm(after(gated, low), d_mix).astype(bf16)[:chans].reshape(narrow, c_rows, D)
        return split_narrow(grad_out, 0), row_grad(flip[None], after(normed, low), d_z, chans)

    d_sel, (grad_out, grad_z) = reduce_wide(d_sel_part, meanwhile)
    grad_out = turned([after(p, d_sel) for p in grad_out])
    grad_flat = jnp.concatenate(
        [jnp.zeros((CONV + 1, wid), f32), grad_step_bias, grad_skip, jnp.zeros((1, wid), f32), d_a * a_neg],
        axis=0,
    )
    in_part, grad_x, grad_pack = tail(
        flip[None], d_sel, d_act, conv_sum, proj_x, d_z, normed, conv_act, weight_x, weight_z,
        weight_sel, taps, grad_step, grad_flat, chans,
    )
    grad_in = scatter_rows(jnp.concatenate([grad_x, grad_z], axis=1), d_rows)
    in_part, grad_out = lax.optimization_barrier((in_part, grad_out))
    channel_grads = turned(split_narrow(grad_pack.reshape(narrow, c_rows, 2 * LANES), 0))
    d_normed = scatter_wide(in_part)
    d_normed, grad_in, channel_grads, grad_out = lax.optimization_barrier(
        (d_normed, grad_in, channel_grads, grad_out)
    )
    channel_grads = sum(p.astype(f32) for p in channel_grads)
    grad_out = sum(p.astype(f32) for p in grad_out)
    inverse_one = lax.rsqrt(jnp.mean(tokens_own * tokens_own, axis=-1, keepdims=True) + EPSILON)
    token_grad = d_hidden_one + norm_backward(tokens_own, inverse_one, gain_one, d_normed)
    output = (hidden_one + after(expert_sum, in_part).astype(f32)).astype(bf16)

    grad_up, grad_down, _ = lax.optimization_barrier((grad_up, grad_down, in_part))
    grad_up = summed_rows(grad_up)
    grad_down = sum(p.astype(f32) for p in grad_down)
    grad_router = jnp.sum(grad_up[:, :, both:], axis=0)
    grad_up = grad_up[:, :, :both].reshape(wide, d_rows, EXPERTS, ff)
    grad_up = grad_up.transpose(2, 1, 0, 3).reshape(EXPERTS, d_rows, FF)
    grad_gain_two = (
        jnp.sum(up_weight.astype(f32) * grad_up, axis=(0, 2))
        + jnp.sum(router_weight.astype(f32) * grad_router, axis=1)
    ) / expert_gain.astype(f32)

    grad_in = summed_rows(grad_in).reshape(wide, d_rows, 2, chans)
    grad_in = grad_in.transpose(1, 2, 0, 3).reshape(d_rows, 2 * DI)
    grad_gain_one = jnp.sum(in_weight.astype(f32) * grad_in, axis=1) / mixer_gain.astype(f32)
    flat_grads = channel_grads[:, DT_RANK : DT_RANK + FLAT].T
    return (
        output[None],
        token_grad[None],
        grad_gain_one,
        grad_in,
        flat_grads[:CONV],
        flat_grads[CONV],
        channel_grads[:, LANES : LANES + DT_RANK + 2 * NS],
        channel_grads[:, :DT_RANK].T,
        flat_grads[CONV + 1],
        flat_grads[CONV + 4 :],
        flat_grads[CONV + 2],
        grad_out,
        grad_gain_two,
        grad_router,
        grad_up,
        grad_down,
    )


def solution(mesh):
    both = ("wide", "narrow")
    return jax.shard_map(
        local,
        mesh=mesh,
        in_specs=(
            P("narrow", "wide", None),
            P(both),
            P(both, None),
            P(None, both),
            P(both),
            P(both, None),
            P(None, both),
            P(both),
            P(None, both),
            P(both),
            P(both, None),
            P(both),
            P(both, None),
            P(None, both, None),
            P(None, both, None),
            P("narrow", "wide"),
            P("narrow"),
            P("narrow", "wide", None),
        ),
        out_specs=(
            P("narrow", "wide", None),
            P("narrow", "wide", None),
            P(both),
            P(both, None),
            P(None, both),
            P(both),
            P(both, None),
            P(None, both),
            P(both),
            P(None, both),
            P(both),
            P(both, None),
            P(both),
            P(both, None),
            P(None, both, None),
            P(None, both, None),
        ),
        check_vma=False,
    )
```

```python
import math

import jax
import jax.numpy as jnp
from jax import lax
from jax.experimental import pallas as pl
from jax.experimental.pallas import tpu as pltpu
from jax.sharding import PartitionSpec as P

D = 1152
DI = 2304
NS = 16
DT_RANK = 72
CONV = 4
FF = 3072
EXPERTS = 2
EPSILON = 1e-05
TIME_BLOCK = 128
VMEM = 60 * 2**20
LANES = 128
LN2 = math.log(2.0)

f32 = jnp.float32
bf16 = jnp.bfloat16


def relative():
    return lax.axis_size("wide") == 8


def swap(x, k):
    n = lax.axis_size("wide")
    return lax.ppermute(x, "wide", [(i, i ^ k) for i in range(n)])


def turn(x, k):
    n = lax.axis_size("narrow")
    return lax.ppermute(x, "narrow", [(i, (i + k) % n) for i in range(n)])


def pick(x, i, axis=0):
    return lax.dynamic_index_in_dim(x, i, axis, False)


def blocks_of(x):
    return [[b] for b in jnp.split(x, lax.axis_size("wide"), axis=0)]


def gather_wide(block, meanwhile=None):
    if not relative():
        made = meanwhile(block) if meanwhile else ()
        return blocks_of(lax.all_gather(block, "wide", axis=0, tiled=True)), made
    half = block.shape[0] // 2
    mate = swap(block, 1)
    a, b = swap(block, 2), swap(block, 4)
    made = ()
    if meanwhile:
        made = meanwhile(block)
        a, b, made = lax.optimization_barrier((a, b, made))
    c0, c1 = swap(a[:half], 4), swap(b[half:], 2)
    out = [[block], [mate], [a], [swap(a, 1)], [b], [swap(b, 1)], [c0, c1], [swap(c0, 1), swap(c1, 1)]]
    return out, made


def scatter_wide(parts, beside=(), early=()):
    if not relative():
        whole = jnp.concatenate(parts, axis=0)
        total = lax.psum_scatter(whole, "wide", scatter_dimension=0, tiled=True).astype(f32)
        return total, beside(total) if callable(beside) else beside, early
    half = parts[0].shape[0] // 2

    def summed(q):
        return parts[2 * q].astype(f32) + swap(parts[2 * q + 1], 1).astype(f32)

    far = summed(3).astype(bf16)
    r0, r1 = swap(far[:half], 2), swap(far[half:], 4)
    r0, r1, early = lax.optimization_barrier((r0, r1, early))
    sx, sy = summed(1), summed(2)
    x0, y1 = swap(sx[:half].astype(bf16), 2), swap(sy[half:].astype(bf16), 4)
    x1 = swap((sx[half:] + r1.astype(f32)).astype(bf16), 2)
    y0 = swap((sy[:half] + r0.astype(f32)).astype(bf16), 4)
    x1, y0, beside = lax.optimization_barrier((x1, y0, beside(r0) if callable(beside) else beside))
    x = jnp.concatenate([x0, x1], axis=0).astype(f32)
    y = jnp.concatenate([y0, y1], axis=0).astype(f32)
    return summed(0) + x + y, beside, early


def reduce_wide(partial, meanwhile):
    if not relative():
        return lax.psum(partial, "wide"), meanwhile(partial)
    core = lax.axis_index("wide") % 2
    half = partial.shape[0] // 2
    parts = partial.reshape(2, half, partial.shape[1])
    total = pick(parts, core).astype(f32) + swap(pick(parts, 1 - core), 1).astype(f32)
    low = total.astype(bf16)
    got = [swap(low, 2), swap(low, 4), swap(low, 6)]
    got, made = lax.optimization_barrier((got, meanwhile(low)))
    total = total + sum(p.astype(f32) for p in got)
    low = total.astype(bf16)
    mate = swap(low, 1)
    first = core == 0
    out = jnp.concatenate([jnp.where(first, low, mate), jnp.where(first, mate, low)], axis=0)
    return out, made


def after(x, *others):
    return lax.optimization_barrier((x,) + others)[0]


def turns(x):
    return [x] + [turn(x, k) for k in range(1, lax.axis_size("narrow"))]


def pad_to(x, axis, size):
    pads = [(0, 0)] * x.ndim
    pads[axis] = (0, size - x.shape[axis])
    return jnp.pad(x, pads)


def ordered_rows(pieces, group, cols):
    n, z = lax.axis_size("narrow"), lax.axis_index("narrow")
    rows, width = pieces[0].shape
    order = jnp.stack([(z - k) % n * group for k in range(n)]).astype(jnp.int32)

    def kernel(order_ref, *refs):
        out = refs[n]
        r = lax.broadcasted_iota(jnp.int32, (n * rows, rows), 0)
        j = lax.broadcasted_iota(jnp.int32, (n * rows, rows), 1)
        spot = j
        for i in range(1, rows // group):
            spot = spot + jnp.where(j >= i * group, (n - 1) * group, 0)
        value = jnp.zeros((n * rows, width), f32)
        for k in range(n):
            spots = jnp.where(r == spot + order_ref[k], 1.0, 0.0).astype(bf16)
            value = value + jnp.dot(spots, refs[k][...], preferred_element_type=f32)
        out[...] = jnp.zeros(out.shape, bf16)
        out[:, :width] = value.astype(bf16)

    vmem = pl.BlockSpec(memory_space=pltpu.VMEM)
    return pl.pallas_call(
        kernel,
        in_specs=[pl.BlockSpec(memory_space=pltpu.SMEM)] + [vmem] * n,
        out_specs=vmem,
        out_shape=jax.ShapeDtypeStruct((n * rows, cols), bf16),
        compiler_params=pltpu.CompilerParams(vmem_limit_bytes=VMEM),
    )(order, *pieces)


def gather_channels(pieces, splits, total):
    n, z = lax.axis_size("narrow"), lax.axis_index("narrow")
    rows, cols = pieces[0].shape
    order = jnp.stack([(z - k) % n * rows for k in range(n)]).astype(jnp.int32)

    def kernel(order_ref, *refs):
        value = jnp.zeros((total, cols), f32)
        r = lax.broadcasted_iota(jnp.int32, (total, rows), 0)
        j = lax.broadcasted_iota(jnp.int32, (total, rows), 1)
        for k in range(n):
            spots = jnp.where(r == j + order_ref[k], 1.0, 0.0).astype(bf16)
            value = value + jnp.dot(spots, refs[k][...], preferred_element_type=f32)
        value = value.astype(bf16)
        at = 0
        for out in refs[n:]:
            out[...] = value[:, at : at + out.shape[1]]
            at += out.shape[1]

    vmem = pl.BlockSpec(memory_space=pltpu.VMEM)
    return pl.pallas_call(
        kernel,
        in_specs=[pl.BlockSpec(memory_space=pltpu.SMEM)] + [vmem] * n,
        out_specs=[vmem] * len(splits),
        out_shape=[jax.ShapeDtypeStruct((total, c), bf16) for c in splits],
        compiler_params=pltpu.CompilerParams(vmem_limit_bytes=VMEM),
    )(order, *pieces)


def turns(x):
    return [x] + [turn(x, k) for k in range(1, lax.axis_size("narrow"))]


def turned(pieces):
    return [pieces[0]] + [turn(pieces[k], k) for k in range(1, len(pieces))]


def split_narrow(x, axis):
    n, z = lax.axis_size("narrow"), lax.axis_index("narrow")
    return [pick(x, (z + k) % n, axis) for k in range(n)]


def exchange(x):
    return lax.all_to_all(x, ("wide", "narrow"), 0, 0)


def gather_rows(parts):
    wide, rows, cols = parts.shape
    narrow = lax.axis_size("narrow")
    parts = jnp.broadcast_to(parts[:, None], (wide, narrow, rows, cols))
    got = exchange(parts.reshape(wide * narrow, rows, cols))
    return got.reshape(wide * narrow * rows, cols)


def scatter_rows(grad):
    got = exchange(grad)
    return got.reshape(lax.axis_size("wide"), lax.axis_size("narrow"), *grad.shape[1:])


def summed_rows(got):
    return sum(got[:, k].astype(f32) for k in range(got.shape[1]))


def mm(a, b):
    return jnp.dot(a, b, preferred_element_type=f32)


def mm_t(a, b):
    return lax.dot_general(a, b, (((1,), (1,)), ((), ())), preferred_element_type=f32)


def t_mm(a, b):
    return lax.dot_general(a, b, (((0,), (0,)), ((), ())), preferred_element_type=f32)


def sigmoid(v):
    return 1.0 / (1.0 + jnp.exp(-v))


def softplus(v):
    return jnp.maximum(v, 0.0) + jnp.log1p(jnp.exp(-jnp.abs(v)))


def call(kernel, grid, flip, ins, outs, scratch, flops, exps=0, aliases={}):
    def spec(block, where):
        if block is None:
            return pl.BlockSpec(memory_space=pltpu.HBM)
        if where is None:
            zeros = (0,) * len(block)
            return pl.BlockSpec(block, lambda i, s: zeros)
        return pl.BlockSpec(block, lambda i, s: (where(i, s[0]),) + (0,) * (len(block) - 1))

    size = sum(a.size * a.dtype.itemsize for a, _, _ in ins)
    size += sum(math.prod(o[0]) * jnp.dtype(o[1]).itemsize for o in outs)
    return pl.pallas_call(
        kernel,
        grid_spec=pltpu.PrefetchScalarGridSpec(
            num_scalar_prefetch=1,
            grid=(grid,),
            in_specs=[spec(b, f) for _, b, f in ins],
            out_specs=[spec(b, f) for _, _, b, f in outs],
            scratch_shapes=scratch,
        ),
        out_shape=[jax.ShapeDtypeStruct(o[0], o[1]) for o in outs],
        input_output_aliases=aliases,
        compiler_params=pltpu.CompilerParams(vmem_limit_bytes=VMEM),
        cost_estimate=pl.CostEstimate(flops=flops // 64, bytes_accessed=size // 64, transcendentals=0),
    )(flip, *[a for a, _, _ in ins])


def fetch_blocks(groups, held, sems, shift):
    for k, group in enumerate(groups):
        at = 0
        for ref in group:
            n = ref.shape[0]
            pltpu.make_async_copy(ref, held.at[k ^ shift, pl.ds(at, n)], sems.at[k ^ shift]).start()
            at += n


def wait_block(held, sems, i):
    pltpu.make_async_copy(held.at[i], held.at[i], sems.at[i]).wait()


def send_rows(value, stage, sems, outs, step, steps, block, at):
    slot = step % 2
    n = value.shape[0]

    def sent(k):
        return pltpu.make_async_copy(stage.at[k], stage.at[k], sems.at[k])

    @pl.when(step >= 2)
    def _():
        sent(slot).wait()

    stage[slot] = value
    for k, out in enumerate(outs):

        @pl.when(block == k)
        def _(out=out):
            pltpu.make_async_copy(stage.at[slot], out.at[pl.ds(at, n)], sems.at[slot]).start()

    @pl.when(step == steps - 1)
    def _():
        sent(0).wait()
        sent(1).wait()


def taken(refs, lengths):
    out, at = [], 0
    for n in lengths:
        out.append(refs[at : at + n])
        at += n
    return out, refs[at:]


def front(flip, tokens, gain, weight_x, taps, shift, weight_sel):
    wid = weight_x.shape[1]
    blocks = lax.axis_size("wide")
    rows = tokens[0][0].shape[0]
    length = rows * blocks
    counts = [len(g) for g in tokens]

    def kernel(s_ref, *refs):
        groups, refs = taken(refs, counts)
        gain_r, wx, taps_r, shift_r, wsel, normed, proj, conv, act, part, pad, held, sems = refs
        i = pl.program_id(0)

        @pl.when(i == 0)
        def _():
            fetch_blocks(groups, held, sems, s_ref[0])
            pad[:8, :] = jnp.zeros((8, wid), f32)

        wait_block(held, sems, i)
        values = held[i].astype(f32)
        inverse = lax.rsqrt(jnp.mean(values * values, axis=-1, keepdims=True) + EPSILON)
        low = (values * inverse * gain_r[...]).astype(bf16)
        normed[...] = low
        x = mm(low, wx[...])
        proj[...] = x
        pad[8:, :] = x
        total = shift_r[...] + taps_r[CONV - 1 : CONV, :] * x
        for k in range(CONV - 1):
            start = 8 - (CONV - 1) + k
            total = total + taps_r[k : k + 1, :] * pad[start : start + rows, :]
        pad[:8, :] = x[rows - 8 :, :]
        conv[...] = total
        low = (total * sigmoid(total)).astype(bf16)
        act[...] = low
        part[...] = mm(low, wsel[...]).astype(bf16)

    here = lambda i, s: i
    rel = lambda i, s: i ^ s
    return call(
        kernel,
        blocks,
        flip,
        [
            *[(part, None, None) for group in tokens for part in group],
            (gain, (1, D), None),
            (weight_x, (D, wid), None),
            (taps, (CONV, wid), None),
            (shift, (1, wid), None),
            (weight_sel, (wid, LANES), None),
        ],
        [
            ((length, D), bf16, (rows, D), rel),
            ((length, wid), f32, (rows, wid), here),
            ((length, wid), f32, (rows, wid), here),
            ((length, wid), bf16, (rows, wid), here),
            ((length, LANES), bf16, (rows, LANES), here),
        ],
        [
            pltpu.VMEM((rows + 8, wid), f32),
            pltpu.VMEM((blocks, rows, D), bf16),
            pltpu.SemaphoreType.DMA((blocks,)),
        ],
        2 * length * wid * (D + LANES),
    )


FLAT = CONV + 4 + NS
def row_sums(terms, masks):
    high, mid, low = masks
    c = [
        jnp.where(high, terms[i + 4], terms[i])
        + pltpu.roll(jnp.where(high, terms[i], terms[i + 4]), 4, 0)
        for i in range(4)
    ]
    c = [
        jnp.where(mid, c[i + 2] + pltpu.roll(c[i + 2], 2, 0), c[i] + pltpu.roll(c[i], 6, 0))
        for i in range(2)
    ]
    return jnp.where(low, c[1] + pltpu.roll(c[1], 1, 0), c[0] + pltpu.roll(c[0], 7, 0))


def row_masks(wid):
    row = lax.broadcasted_iota(jnp.int32, (8, wid), 0)
    return row >= 4, (row & 2) > 0, (row & 1) > 0


IN_AT = DT_RANK
OUT_AT = DT_RANK + NS


def middle(flip, sel, act, normed, weight_z, weight_step, shift, skip, a2, weight_out):
    length, wid = act.shape
    blocks = length // TIME_BLOCK
    per = blocks // lax.axis_size("wide")

    wide = lax.axis_size("wide")

    def kernel(
        s_ref, sel_r, act_r, n_r, wz, wstep, shift_r, skip_r, a_r, wout, z_o, lin_o, kept, end, mixed, gated_o, *refs
    ):
        (parts,), refs = taken(refs, [wide])
        state, dt_s, u_s, y_s, stage, sems = refs
        i = pl.program_id(0)

        @pl.when(pl.program_id(0) == 0)
        def _():
            state[...] = jnp.zeros_like(state)

        low = sel_r[...]
        lin = mm_t(low, wstep[...]) + shift_r[...]
        lin_o[...] = lin
        dt_s[...] = softplus(lin)
        u_s[...] = dt_s[...] * act_r[...].astype(f32)
        turned = low.astype(f32).T
        in_sel, out_sel = turned[IN_AT : IN_AT + NS, :], turned[OUT_AT : OUT_AT + NS, :]
        a2 = a_r[...]

        masks = row_masks(wid)
        h = state[...]
        terms = [None] * 8
        for t in range(TIME_BLOCK):
            kept[t] = h
            h = jnp.exp2(dt_s[t : t + 1, :] * a2) * h + u_s[t : t + 1, :] * in_sel[:, t : t + 1]
            y = h * out_sel[:, t : t + 1]
            terms[t % 8] = y[:8] + y[8:]
            if t % 8 == 7:
                y_s[t - 7 : t + 1, :] = row_sums(terms, masks)
        state[...] = h
        end[...] = h
        out = y_s[...] + skip_r[...] * act_r[...].astype(f32)
        mixed[...] = out
        z = mm(n_r[...], wz[...])
        z_o[...] = z
        gated = (out * z * sigmoid(z)).astype(bf16)
        gated_o[...] = gated
        value = mm(gated, wout[...]).astype(bf16)
        send_rows(value, stage, sems, parts, i, blocks, (i // per) ^ s_ref[0], i % per * TIME_BLOCK)

    here = lambda i, s: i
    rel = lambda i, s: ((i // per) ^ s) * per + i % per
    row = (TIME_BLOCK, wid)
    return call(
        kernel,
        blocks,
        flip,
        [
            (sel, (TIME_BLOCK, LANES), here),
            (act, row, here),
            (normed, (TIME_BLOCK, D), rel),
            (weight_z, (D, wid), None),
            (weight_step, (wid, LANES), None),
            (shift, (1, wid), None),
            (skip, (1, wid), None),
            (a2, (NS, wid), None),
            (weight_out, (wid, D), None),
        ],
        [
            ((length, wid), f32, row, here),
            ((length, wid), f32, row, here),
            ((length, NS, wid), f32, (TIME_BLOCK, NS, wid), here),
            ((NS, wid), f32, (NS, wid), None),
            ((length, wid), f32, row, here),
            ((length, wid), bf16, row, here),
            *[((length // wide, D), bf16, None, None)] * wide,
        ],
        [pltpu.VMEM((NS, wid), f32)]
        + [pltpu.VMEM(row, f32)] * 3
        + [pltpu.VMEM((2, TIME_BLOCK, D), bf16), pltpu.SemaphoreType.DMA((2,))],
        length * wid * (8 * NS + 4 * D + 2 * LANES),
        length * NS * wid,
    )


def experts(span, base, normed, cot, up, down, ff, whole):
    rows = normed[0].shape[0]
    length = rows * lax.axis_size("wide")
    blocks = len(normed)
    cols = up.shape[1]

    def kernel(s_ref, *refs):
        (n_refs, (cot_r, up_r, down_r), _, backs, outs), refs = taken(
            refs, [blocks, 3, len(whole), blocks, blocks]
        )
        n_o, hid_o, both_o, dex_o = refs
        i = pl.program_id(0)
        for k, ref in enumerate(n_refs):

            @pl.when(i == k)
            def _(ref=ref):
                n_o[...] = ref[...]

        position = ((i + base) ^ s_ref[0]) * rows + lax.broadcasted_iota(jnp.int32, (rows, 1), 0)
        cot_b = cot_r[...]
        second = cot_b[:, D : D + 1] > 0.5
        upstream = jnp.where(position < s_ref[1], cot_b[:, :D], jnp.zeros((), bf16))
        raised = mm(n_o[...], up_r[...])
        first_l, second_l = raised[:, EXPERTS * ff : EXPERTS * ff + 1], raised[:, EXPERTS * ff + 1 : EXPERTS * ff + 2]
        lead = jnp.where(second, second_l - first_l, first_l - second_l)
        gate = sigmoid(lead)
        other = sigmoid(-lead)
        pre = jnp.where(second, raised[:, ff : 2 * ff], raised[:, :ff])
        bell = (1.0 + lax.erf(pre * (1.0 / math.sqrt(2.0)))) * 0.5
        hidden = pre * bell
        slope = bell + pre * jnp.exp(-0.5 * pre * pre) * (1.0 / math.sqrt(2.0 * math.pi))
        hidden = hidden.astype(bf16)
        hid_f = hidden.astype(f32)
        both = jnp.concatenate(
            [jnp.where(second, 0.0, hid_f), jnp.where(second, hid_f, 0.0)], axis=1
        ).astype(bf16)
        hid_o[...] = both
        value = (gate * mm(both, down_r[...])).astype(bf16)
        for k, ref in enumerate(outs):

            @pl.when(i == k)
            def _(ref=ref, value=value):
                ref[...] = value

        dex_o[...] = (gate * upstream.astype(f32)).astype(bf16)
        lowered = mm_t(upstream, down_r[...])
        d_hid = jnp.where(second, lowered[:, ff:], lowered[:, :ff])
        d_gate = jnp.sum(hid_f * d_hid, axis=-1, keepdims=True)
        d_pre = gate * d_hid * slope
        d_lead = gate * other * d_gate
        lane = lax.broadcasted_iota(jnp.int32, (rows, cols - EXPERTS * ff), 1)
        d_second = jnp.where(second, d_lead, -d_lead)
        d_logits = jnp.where(lane == 1, d_second, jnp.where(lane == 0, -d_second, 0.0))
        d_both = jnp.concatenate(
            [jnp.where(second, 0.0, d_pre), jnp.where(second, d_pre, 0.0), d_logits], axis=1
        ).astype(bf16)
        both_o[...] = d_both
        value = mm_t(d_both, up_r[...]).astype(bf16)
        for k, ref in enumerate(backs):

            @pl.when(i == k)
            def _(ref=ref):
                ref[...] = value

    here = lambda i, s: i + base
    place = lambda i, s: (i + base) ^ s
    first = 1 + blocks + 3
    made = call(
        kernel,
        blocks,
        span,
        [
            *[(n, (rows, D), None) for n in normed],
            (cot, (rows, D + LANES), place),
            (up, up.shape, None),
            (down, down.shape, None),
            *[(x, None, None) for x in whole],
        ],
        [
            *[((rows, D), bf16, (rows, D), None)] * (2 * blocks),
            ((length, D), bf16, (rows, D), here),
            ((length, EXPERTS * ff), bf16, (rows, EXPERTS * ff), here),
            ((length, cols), bf16, (rows, cols), here),
            ((length, D), bf16, (rows, D), here),
        ],
        [],
        4 * blocks * rows * D * (cols + EXPERTS * ff),
        3 * blocks * rows * ff,
        {first + k: 2 * blocks + k for k in range(len(whole))},
    )
    return made[:blocks], made[blocks : 2 * blocks], made[2 * blocks :]


def back(flip, d_mix, weight_out, sel, act, proj_z, lin, mixed, kept, end, weight_step, skip, a2):
    length, wid = act.shape
    blocks = length // TIME_BLOCK
    per = blocks // lax.axis_size("wide")

    counts = [len(g) for g in d_mix]

    def kernel(s_ref, *refs):
        mix_groups, refs = taken(refs, counts)
        (
            wout, sel_r, act_r, z_r, lin_r, mixed_r, kept_r, end_r, wstep, skip_r, a_r,
            mix_o, dz_o, part, dact_o, gstep_o, da_o, dskip_o, dbias_o,
            lam_s, next_s, pb_s, pc_s, dt_s, u_s, dy_s, s1_s, s2_s, turned_s, held, sems,
        ) = refs
        place = blocks - 1 - pl.program_id(0)

        @pl.when(pl.program_id(0) == 0)
        def _():
            fetch_blocks(mix_groups, held, sems, s_ref[0])
            lam_s[...] = jnp.zeros_like(lam_s)
            next_s[...] = end_r[...]
            da_o[...] = jnp.zeros_like(da_o)
            for ref in (gstep_o, dskip_o, dbias_o):
                ref[...] = jnp.zeros_like(ref)
            turned_s[...] = jnp.zeros_like(turned_s)

        @pl.when(pl.program_id(0) % per == 0)
        def _():
            wait_block(held, sems, place // per)

        mix = held[place // per, pl.ds(pl.multiple_of(place % per * TIME_BLOCK, TIME_BLOCK), TIME_BLOCK)]
        mix_o[...] = mix
        d_gated = mm_t(mix, wout[...])
        z = z_r[...]
        s = sigmoid(z)
        dz_o[...] = (d_gated * mixed_r[...] * (s * (1.0 + z * (1.0 - s)))).astype(bf16)
        dy_s[...] = d_gated * (z * s)
        x_all = act_r[...].astype(f32)
        dskip_o[...] += jnp.sum(dy_s[...] * x_all, axis=0, keepdims=True)
        dt_s[...] = softplus(lin_r[...])
        u_s[...] = dt_s[...] * x_all
        low = sel_r[...]
        turned = low.astype(f32).T
        in_sel, out_sel = turned[IN_AT : IN_AT + NS, :], turned[OUT_AT : OUT_AT + NS, :]
        a2 = a_r[...]

        def fold(v):
            total = v[:, :LANES]
            for k in range(1, wid // LANES):
                total = total + v[:, k * LANES : (k + 1) * LANES]
            return total

        masks = row_masks(wid)
        p, after, acc = lam_s[...], next_s[...], da_o[...]
        first, second = [None] * 8, [None] * 8
        for t in range(TIME_BLOCK - 1, -1, -1):
            before = kept_r[t]
            dt_t, dy_t = dt_s[t : t + 1, :], dy_s[t : t + 1, :]
            lam = dy_t * out_sel[:, t : t + 1] + p
            p = lam * jnp.exp2(dt_t * a2)
            moved = p * before
            acc = acc + dt_t * moved
            term = lam * in_sel[:, t : t + 1]
            first[t % 8] = term[:8] + term[8:]
            term = a2 * moved
            second[t % 8] = term[:8] + term[8:]
            if t % 8 == 0:
                s1_s[t : t + 8, :] = row_sums(first, masks)
                s2_s[t : t + 8, :] = row_sums(second, masks)
            pb_s[t] = fold(lam * u_s[t : t + 1, :])
            pc_s[t] = fold(after * dy_t)
            after = before
        lam_s[...] = p
        next_s[...] = after
        da_o[...] = acc
        ones = jnp.ones((LANES, LANES), bf16)
        lane = lax.broadcasted_iota(jnp.int32, (NS, TIME_BLOCK), 1)
        for source, at in ((pb_s, IN_AT), (pc_s, OUT_AT)):
            sums = mm(source[...].reshape(TIME_BLOCK * NS, LANES).astype(bf16), ones)
            sums = sums.reshape(TIME_BLOCK, NS, LANES)
            parts = [jnp.zeros((NS, TIME_BLOCK), f32)] * 4
            for t in range(TIME_BLOCK):
                parts[t % 4] = jnp.where(lane == t, sums[t], parts[t % 4])
            turned_s[at : at + NS, :] = (parts[0] + parts[1]) + (parts[2] + parts[3])
        through = s1_s[...]
        d_step = s2_s[...] * LN2 + x_all * through
        dact_o[...] = dt_s[...] * through + skip_r[...] * dy_s[...]
        grad = d_step * sigmoid(lin_r[...])
        dbias_o[...] += jnp.sum(grad, axis=0, keepdims=True)
        grad = grad.astype(bf16)
        gstep_o[...] += t_mm(grad, low)
        part[...] = (mm(grad, wstep[...]) + turned_s[...].T).astype(bf16)

    here = lambda i, s: blocks - 1 - i
    rel = lambda i, s: (((blocks - 1 - i) // per) ^ s) * per + (blocks - 1 - i) % per
    row = (TIME_BLOCK, wid)
    one = ((1, wid), f32, (1, wid), None)
    return call(
        kernel,
        blocks,
        flip,
        [
            *[(part, None, None) for group in d_mix for part in group],
            (weight_out, (wid, D), None),
            (sel, (TIME_BLOCK, LANES), here),
            (act, row, here),
            (proj_z, row, here),
            (lin, row, here),
            (mixed, row, here),
            (kept, (TIME_BLOCK, NS, wid), here),
            (end, (NS, wid), None),
            (weight_step, (wid, LANES), None),
            (skip, (1, wid), None),
            (a2, (NS, wid), None),
        ],
        [
            ((length, D), bf16, (TIME_BLOCK, D), here),
            ((length, wid), bf16, row, rel),
            ((length, LANES), bf16, (TIME_BLOCK, LANES), here),
            ((length, wid), f32, row, here),
            ((wid, LANES), f32, (wid, LANES), None),
            ((NS, wid), f32, (NS, wid), None),
            one,
            one,
        ],
        [pltpu.VMEM((NS, wid), f32)] * 2
        + [pltpu.VMEM((TIME_BLOCK, NS, LANES), f32)] * 2
        + [pltpu.VMEM(row, f32)] * 5
        + [pltpu.VMEM((LANES, TIME_BLOCK), f32)]
        + [
            pltpu.VMEM((lax.axis_size("wide"), length // lax.axis_size("wide"), D), bf16),
            pltpu.SemaphoreType.DMA((lax.axis_size("wide"),)),
        ],
        length * wid * (20 * NS + 2 * D + 2 * LANES),
        length * NS * wid,
    )


def tail(
    flip, d_sel, d_act, conv, proj, d_z, normed, act, weight_x, weight_z, weight_sel, taps,
    grad_step, grad_flat, grad_z, grad_out, beyond, chans,
):
    length, wid = act.shape
    blocks, count = lax.axis_size("wide"), lax.axis_size("narrow")
    rows = length // blocks
    group, c_rows = D // (blocks * count), chans // count

    def kernel(
        s_ref, sel_r, dact_r, conv_r, proj_r, dz_r, n_r, act_r, wx, wz, wsel, taps_r, gstep_r, flat_r,
        gz_r, gout_r, *refs,
    ):
        (parts, packs), refs = taken(refs, [blocks, count])
        gx_o, ext, gx, gsel, flat, held, stage, sems = refs
        i = pl.program_id(0)

        @pl.when(pl.program_id(0) == 0)
        def _():
            ext[rows:, :] = jnp.zeros((8, wid), f32)
            gx[...] = jnp.zeros_like(gx)
            gsel[...] = jnp.zeros_like(gsel)
            flat[...] = flat_r[...]

        low = sel_r[...]
        c = conv_r[...]
        q = sigmoid(c)
        d_conv = (mm_t(low, wsel[...]) + dact_r[...]) * (q * (1.0 + c * (1.0 - q)))
        ext[:rows, :] = d_conv
        flat[CONV : CONV + 1, :] += jnp.sum(d_conv, axis=0, keepdims=True)
        x = proj_r[...]
        d_x = jnp.zeros((rows, wid), f32)
        for k in range(CONV):
            moved = ext[CONV - 1 - k : CONV - 1 - k + rows, :]
            d_x = d_x + taps_r[k : k + 1, :] * moved
            flat[k : k + 1, :] += jnp.sum(moved * x, axis=0, keepdims=True)
        ext[rows:, :] = d_conv[:8, :]
        d_x = d_x.astype(bf16)
        value = (mm_t(d_x, wx[...]) + mm_t(dz_r[...], wz[...])).astype(bf16)
        send_rows(value, stage, sems, parts, i, blocks, (blocks - 1 - i) ^ s_ref[0], 0)
        gx[...] += t_mm(n_r[...], d_x)
        gsel[...] += t_mm(act_r[...], low)

        @pl.when(pl.program_id(0) == blocks - 1)
        def _():
            for k in range(blocks * count):
                x = gx[k * group : (k + 1) * group, :chans]
                gx_o[k] = jnp.concatenate([x, gz_r[k].astype(f32)], axis=1).astype(bf16)
            tall = jnp.concatenate(
                [jnp.zeros((DT_RANK, wid), f32), flat[...], jnp.zeros((LANES - DT_RANK - FLAT, wid), f32)], axis=0
            )
            lane = lax.broadcasted_iota(jnp.int32, (wid, LANES), 1)
            left = jnp.where(lane < DT_RANK, gstep_r[...], tall.T)
            held[:, :LANES] = left
            held[:, LANES:] = gsel[...]
            for k, out in enumerate(packs):
                if c_rows % 8 == 0:
                    at = pl.multiple_of(s_ref[1 + k] * c_rows, 8)
                    out[:, :D] = gout_r[pl.ds(at, c_rows), :].astype(bf16)
                    out[:, D:] = held[pl.ds(at, c_rows), :].astype(bf16)
                    continue
                for p in range(count):

                    @pl.when(s_ref[1 + k] == p)
                    def _(out=out, at=p * c_rows):
                        out[:, :D] = gout_r[at : at + c_rows, :].astype(bf16)
                        out[:, D:] = held[at : at + c_rows, :].astype(bf16)

    here = lambda i, s: blocks - 1 - i
    rel = lambda i, s: (blocks - 1 - i) ^ s
    row = (rows, wid)
    pack = (c_rows, D + 2 * LANES)
    sent = (blocks * count, group, 2 * chans)
    return call(
        kernel,
        blocks,
        jnp.concatenate([flip, beyond]),
        [
            (d_sel, (rows, LANES), here),
            (d_act, row, here),
            (conv, row, here),
            (proj, row, here),
            (d_z, row, rel),
            (normed, (rows, D), rel),
            (act, row, here),
            (weight_x, (D, wid), None),
            (weight_z, (D, wid), None),
            (weight_sel, (wid, LANES), None),
            (taps, (CONV, wid), None),
            (grad_step, (wid, LANES), None),
            (grad_flat, (FLAT, wid), None),
            (grad_z, grad_z.shape, None),
            (grad_out, (wid, D), None),
        ],
        [*[((rows, D), bf16, None, None)] * blocks, *[(pack, bf16, pack, None)] * count, (sent, bf16, sent, None)],
        [
            pltpu.VMEM((rows + 8, wid), f32),
            pltpu.VMEM((D, wid), f32),
            pltpu.VMEM((wid, LANES), f32),
            pltpu.VMEM((FLAT, wid), f32),
            pltpu.VMEM((wid, 2 * LANES), f32),
            pltpu.VMEM((2, rows, D), bf16),
            pltpu.SemaphoreType.DMA((2,)),
        ],
        2 * length * wid * (3 * D + 2 * LANES),
    )


def row_grad(flip, a, b, cols, group, along):
    narrow = lax.axis_size("narrow")
    length, total = a.shape
    n = b.shape[1]
    blocks = lax.axis_size("wide")
    rows = length // blocks

    def kernel(s_ref, a_r, b_r, out, acc):
        @pl.when(pl.program_id(0) == 0)
        def _():
            acc[...] = jnp.zeros_like(acc)

        acc[...] += t_mm(a_r[...], b_r[...])

        @pl.when(pl.program_id(0) == blocks - 1)
        def _():
            for k in range(total // group):
                at = k % narrow * blocks + k // narrow if along else k
                out[at] = acc[k * group : (k + 1) * group, :cols].astype(bf16)

    here = lambda i, s: i
    return call(
        kernel,
        blocks,
        flip,
        [(a, (rows, total), here), (b, (rows, n), here)],
        [((total // group, group, cols), bf16, (total // group, group, cols), None)],
        [pltpu.VMEM((total, n), f32)],
        2 * length * total * n,
    )[0]


def joined(got):
    wide, narrow, rows, cols = got.shape
    half = cols // 2

    def kernel(got_r, out):
        parts = [sum(got_r[w, k].astype(f32) for k in range(narrow)) for w in range(wide)]
        out[:, : wide * half] = jnp.concatenate([p[:, :half] for p in parts], axis=1)
        out[:, wide * half :] = jnp.concatenate([p[:, half:] for p in parts], axis=1)

    vmem = pl.BlockSpec(memory_space=pltpu.VMEM)
    return pl.pallas_call(
        kernel,
        in_specs=[vmem],
        out_specs=vmem,
        out_shape=jax.ShapeDtypeStruct((rows, wide * cols), f32),
        compiler_params=pltpu.CompilerParams(vmem_limit_bytes=VMEM),
    )(got)


def norm_backward(values, inverse, gain_vec, upstream):
    scaled = upstream * gain_vec
    inner_mean = jnp.mean(values * scaled, axis=-1, keepdims=True)
    return inverse * scaled - values * (inverse * inverse * inverse) * inner_mean


def local(
    tokens,
    mixer_gain,
    in_weight,
    conv_weight,
    conv_bias,
    select_weight,
    step_weight,
    step_bias,
    decay_log,
    skip_weight,
    out_weight,
    expert_gain,
    router_weight,
    up_weight,
    down_weight,
    routes,
    lengths,
    cotangent,
):
    wide, narrow = lax.axis_size("wide"), lax.axis_size("narrow")
    w = lax.axis_index("wide")
    rows = tokens.shape[1]
    chans = DI // wide
    wid = -(-chans // LANES) * LANES
    ff = FF // wide
    d_rows = D // (wide * narrow)
    c_rows = DI // (wide * narrow)
    f_rows = FF // (wide * narrow)
    both = EXPERTS * ff
    flip = w if relative() else 0 * w
    span = jnp.stack([flip, lengths[0]]).astype(jnp.int32)

    tokens_own = tokens[0].astype(f32)

    in_parts = in_weight.reshape(d_rows, 2, wide, chans).transpose(1, 2, 0, 3)
    gains = jnp.stack([mixer_gain, expert_gain], axis=1)
    gains = jnp.broadcast_to(gains[None], (wide, d_rows, 2))
    zero_col = jnp.zeros((c_rows, 1), bf16)
    channel_pack = jnp.concatenate(
        [
            conv_weight.T,
            conv_bias[:, None],
            step_bias[:, None],
            skip_weight[:, None],
            zero_col,
            decay_log.T,
            step_weight.T,
            select_weight,
        ],
        axis=1,
    )
    pack_cols = channel_pack.shape[1]
    wide_cols = -(-pack_cols // LANES) * LANES
    channel_pack = pad_to(channel_pack, 1, wide_cols)
    x_parts = jnp.concatenate([in_parts[0], gains], axis=2)
    tokens_all, channel_pack = gather_wide(tokens[0], lambda block: turns(channel_pack))
    x_full = gather_rows(after(x_parts, channel_pack))
    x_full, tokens_all = lax.optimization_barrier((x_full, tokens_all))
    weight_x = pad_to(x_full[:, :chans], 1, wid)
    gains = x_full[:, chans:].T.astype(f32)
    gain_one, gain_two = gains[:1], gains[1:]
    up_parts = up_weight.reshape(EXPERTS, d_rows, wide, ff).transpose(2, 1, 0, 3)
    up_parts = up_parts.reshape(wide, d_rows, both)
    router_parts = jnp.broadcast_to(router_weight[None], (wide, d_rows, EXPERTS))
    up_parts = jnp.concatenate([up_parts, router_parts, in_parts[1]], axis=2)
    up_parts = lax.all_to_all(after(up_parts, x_full), "wide", 0, 0)
    up_parts = up_parts.reshape(wide * d_rows, both + EXPERTS + chans)
    route_cols = jnp.broadcast_to(routes[0].astype(bf16)[:, None], (rows, LANES))
    cot_ext = jnp.concatenate([cotangent[0], route_cols], axis=1)
    cot_all = lax.all_gather(after(cot_ext, tokens_all), "wide", axis=0, tiled=True)
    (packed,) = gather_channels(channel_pack, (wide_cols,), wid)
    flat = packed[:, :FLAT].T.astype(f32)
    taps = flat[:CONV]
    conv_shift, step_shift, skip = (flat[CONV + k : CONV + k + 1] for k in range(3))
    a_neg = -jnp.exp(flat[CONV + 4 :])
    a2 = a_neg * (1.0 / LN2)
    weight_step = pad_to(packed[:, FLAT : FLAT + DT_RANK], 1, LANES)
    weight_sel = pad_to(packed[:, FLAT + DT_RANK : pack_cols], 1, LANES)

    normed, proj_x, conv_sum, conv_act, sel_part = front(
        flip[None], tokens_all, gain_one, weight_x, taps, conv_shift, weight_sel
    )
    out_pieces = turns(after(out_weight, x_full))
    sel_part, up_parts, out_pieces = lax.optimization_barrier((sel_part, up_parts, out_pieces))
    z_pieces = turns(up_parts[:, both + EXPERTS :])
    up_parts = up_parts[:, : both + EXPERTS]
    selected, z_pieces = reduce_wide(sel_part, lambda low: z_pieces)
    weight_z = ordered_rows(z_pieces, d_rows, wid)

    up_cols = -(-(both + EXPERTS) // LANES) * LANES
    up_pieces = turns(after(up_parts, selected, out_pieces))
    valid_own = (w * rows + jnp.arange(rows))[:, None] < lengths[0]
    upstream = jnp.where(valid_own, cotangent[0].astype(f32), 0.0)

    (weight_out,) = gather_channels(out_pieces, (D,), wid)
    proj_z, step_lin, kept, end, mixed, gated, *mix_part = middle(
        flip[None], selected, conv_act, normed, weight_z, weight_step, step_shift, skip, a2, weight_out
    )
    mix_part, up_pieces = lax.optimization_barrier((mix_part, up_pieces))
    down_full = lax.all_gather(after(down_weight, cot_all, *up_pieces), "narrow")
    up_full = ordered_rows(up_pieces, d_rows, up_cols)
    down_full = down_full.transpose(1, 0, 2, 3).reshape(both, D)
    mixer_sum, up_full, _ = scatter_wide(mix_part, up_full)
    hidden_one = tokens_own + mixer_sum
    inverse_two = lax.rsqrt(jnp.mean(hidden_one * hidden_one, axis=-1, keepdims=True) + EPSILON)
    own = (hidden_one * inverse_two * gain_two).astype(bf16)

    def run(base, blocks, whole):
        return experts(span, base, blocks, cot_all, up_full, down_full, ff, whole)

    if relative():
        mate, a, b = swap(own, 1), swap(own, 2), swap(own, 4)
        back_own, out_own, whole = run(0, [own, mate], [])
        a, b, whole = lax.optimization_barrier((a, b, whole))
        far = swap(after(own, a, b), 6)
        back_near, out_near, whole = run(2, [a, swap(a, 1), b, swap(b, 1)], whole)
        far, back_near = lax.optimization_barrier((far, back_near))
        pair = lambda parts: parts[0].astype(f32) + swap(parts[1], 1).astype(f32)
        from_x = swap(pair(back_near[:2]).astype(bf16), 2)
        from_y = swap(pair(back_near[2:]).astype(bf16), 4)
        d_normed_two = pair(back_own)
        back_far, out_far, whole = run(6, [far, swap(far, 1)], whole)
        far_low = pair(back_far).astype(bf16)
        from_far = swap(far_low, 6)
        d_normed_two = d_normed_two + from_x.astype(f32) + from_y.astype(f32) + from_far.astype(f32)
        out_parts, whole = lax.optimization_barrier(([*out_own, *out_near, *out_far], whole, far_low))[:2]
        out_sums = [pair(out_parts[2 * q : 2 * q + 2]).astype(bf16) for q in range(4)]
    else:
        whole, parts, out_sums = [], [], []
        blocks = [group[0] for group in gather_wide(own)[0]]
        for k in range(0, wide, 2):
            made, out, whole = run(k, blocks[k : k + 2], whole)
            parts += made
            out_sums += out
        d_normed_two, _, _ = scatter_wide(parts)
    normed_two, hidden_both, d_both, d_expert = whole

    grad_down = t_mm(hidden_both, d_expert).astype(bf16)
    grad_down = grad_down.reshape(EXPERTS, narrow, f_rows, D).transpose(1, 0, 2, 3)
    d_normed_two, grad_down, out_sums = lax.optimization_barrier((d_normed_two, grad_down, out_sums))
    grad_down = lax.psum_scatter(grad_down, "narrow", scatter_dimension=0)
    d_hidden_one = upstream + norm_backward(hidden_one, inverse_two, gain_two, d_normed_two)
    d_low = d_hidden_one.astype(bf16)
    d_mix, grad_up = gather_wide(
        d_low,
        lambda low: row_grad(flip[None], normed_two, after(d_both, low), both + EXPERTS, d_rows, True),
    )
    d_mix, grad_down = lax.optimization_barrier((d_mix, grad_down))
    grad_up = lax.psum_scatter(
        after(grad_up, d_mix).reshape(narrow, wide, d_rows, both + EXPERTS), "narrow", scatter_dimension=0
    )
    if relative():
        sent = after(out_sums, d_mix)
        out_got = [swap(sent[q], 2 * q) for q in (1, 2, 3)]
    else:
        out_got = []

    d_mix_all, d_z, d_sel_part, d_act, grad_step, d_a, grad_skip, grad_step_bias = back(
        flip[None], d_mix, weight_out, selected, conv_act, proj_z, step_lin, mixed, kept, end,
        weight_step, skip, a2,
    )

    d_sel_part, out_got = lax.optimization_barrier((d_sel_part, out_got))

    def meanwhile(low):
        grad_out = t_mm(after(gated, low), d_mix_all)
        return grad_out, row_grad(flip[None], after(normed, low), d_z, chans, d_rows, False)

    d_sel, (grad_out, grad_z) = reduce_wide(d_sel_part, meanwhile)
    z = lax.axis_index("narrow")
    beyond = jnp.stack([(z + k) % narrow for k in range(narrow)]).astype(jnp.int32)
    grad_flat = jnp.concatenate(
        [jnp.zeros((CONV + 1, wid), f32), grad_step_bias, grad_skip, jnp.zeros((1, wid), f32), d_a * a_neg],
        axis=0,
    )
    grad_up = lax.all_to_all(after(grad_up, d_sel), "wide", 0, 0)
    made = tail(
        flip[None], d_sel, d_act, conv_sum, proj_x, d_z, normed, conv_act, weight_x, weight_z,
        weight_sel, taps, grad_step, grad_flat, grad_z, grad_out, beyond, chans,
    )
    in_part, channel_grads, grad_in = made[:wide], made[wide:-1], made[-1]
    in_part, grad_up = lax.optimization_barrier((in_part, grad_up))
    grad_in = scatter_rows(grad_in)

    def beside(hop):
        up, down = lax.optimization_barrier((grad_up, grad_down, hop))[:2]
        up = up.astype(f32)
        router = jnp.sum(up[:, :, both:], axis=0)
        up = up[:, :, :both].reshape(wide, d_rows, EXPERTS, ff)
        up = up.transpose(2, 1, 0, 3).reshape(EXPERTS, d_rows, FF)
        gain = (
            jnp.sum(up_weight.astype(f32) * up, axis=(0, 2))
            + jnp.sum(router_weight.astype(f32) * router, axis=1)
        ) / expert_gain.astype(f32)
        if relative():
            out = sum(p.astype(f32) for p in lax.optimization_barrier(([out_sums[0], *out_got], hop))[0])
        else:
            out, _, _ = scatter_wide(out_sums)
        return up, router, gain, down.astype(f32), out, turned(channel_grads)

    d_normed, made, _ = scatter_wide(in_part, beside)
    channel_grads = made[-1]
    made = made[:-1]
    grad_up, grad_router, grad_gain_two, grad_down, expert_sum = made
    d_normed, grad_in = lax.optimization_barrier((d_normed, grad_in))
    channel_grads = sum(p.astype(f32) for p in channel_grads)
    grad_out, channel_grads = channel_grads[:, :D], channel_grads[:, D:]
    inverse_one = lax.rsqrt(jnp.mean(tokens_own * tokens_own, axis=-1, keepdims=True) + EPSILON)
    token_grad = d_hidden_one + norm_backward(tokens_own, inverse_one, gain_one, d_normed)
    output = (hidden_one + expert_sum).astype(bf16)

    grad_in = joined(grad_in)
    grad_gain_one = jnp.sum(in_weight.astype(f32) * grad_in, axis=1) / mixer_gain.astype(f32)
    flat_grads = channel_grads[:, DT_RANK : DT_RANK + FLAT].T
    return (
        output[None],
        token_grad[None],
        grad_gain_one,
        grad_in,
        flat_grads[:CONV],
        flat_grads[CONV],
        channel_grads[:, LANES : LANES + DT_RANK + 2 * NS],
        channel_grads[:, :DT_RANK].T,
        flat_grads[CONV + 1],
        flat_grads[CONV + 4 :],
        flat_grads[CONV + 2],
        grad_out,
        grad_gain_two,
        grad_router,
        grad_up,
        grad_down,
    )


def solution(mesh):
    both = ("wide", "narrow")
    return jax.shard_map(
        local,
        mesh=mesh,
        in_specs=(
            P("narrow", "wide", None),
            P(both),
            P(both, None),
            P(None, both),
            P(both),
            P(both, None),
            P(None, both),
            P(both),
            P(None, both),
            P(both),
            P(both, None),
            P(both),
            P(both, None),
            P(None, both, None),
            P(None, both, None),
            P("narrow", "wide"),
            P("narrow"),
            P("narrow", "wide", None),
        ),
        out_specs=(
            P("narrow", "wide", None),
            P("narrow", "wide", None),
            P(both),
            P(both, None),
            P(None, both),
            P(both),
            P(both, None),
            P(None, both),
            P(both),
            P(None, both),
            P(both),
            P(both, None),
            P(both),
            P(both, None),
            P(None, both, None),
            P(None, both, None),
        ),
        check_vma=False,
    )
```

```python
import math

import jax
import jax.numpy as jnp
from jax import lax
from jax.experimental import pallas as pl
from jax.experimental.pallas import tpu as pltpu
from jax.sharding import PartitionSpec as P

D = 1152
DI = 2304
NS = 16
DT_RANK = 72
CONV = 4
FF = 3072
EXPERTS = 2
EPSILON = 1e-05
TIME_BLOCK = 128
VMEM = 60 * 2**20
LANES = 128
LN2 = math.log(2.0)

f32 = jnp.float32
bf16 = jnp.bfloat16


def relative():
    return lax.axis_size("wide") == 8


def swap(x, k):
    n = lax.axis_size("wide")
    return lax.ppermute(x, "wide", [(i, i ^ k) for i in range(n)])


def turn(x, k):
    n = lax.axis_size("narrow")
    return lax.ppermute(x, "narrow", [(i, (i + k) % n) for i in range(n)])


def pick(x, i, axis=0):
    return lax.dynamic_index_in_dim(x, i, axis, False)


def blocks_of(x):
    return [[b] for b in jnp.split(x, lax.axis_size("wide"), axis=0)]


def gather_wide(block, meanwhile=None):
    if not relative():
        made = meanwhile(block) if meanwhile else ()
        return blocks_of(lax.all_gather(block, "wide", axis=0, tiled=True)), made
    half = block.shape[0] // 2
    mate = swap(block, 1)
    a, b = swap(block, 2), swap(block, 4)
    made = ()
    if meanwhile:
        made = meanwhile(block)
        a, b, made = lax.optimization_barrier((a, b, made))
    c0, c1 = swap(a[:half], 4), swap(b[half:], 2)
    out = [[block], [mate], [a], [swap(a, 1)], [b], [swap(b, 1)], [c0, c1], [swap(c0, 1), swap(c1, 1)]]
    return out, made


def scatter_wide(parts, beside=(), eager=False):
    if not relative():
        whole = jnp.concatenate(parts, axis=0)
        total = lax.psum_scatter(whole, "wide", scatter_dimension=0, tiled=True).astype(f32)
        return total, beside(total) if callable(beside) else beside
    half = parts[0].shape[0] // 2

    def summed(q):
        return parts[2 * q].astype(f32) + swap(parts[2 * q + 1], 1).astype(f32)

    far = summed(3).astype(bf16)
    r0, r1 = swap(far[:half], 2), swap(far[half:], 4)
    sx, sy = summed(1), summed(2)
    x0, y1 = swap(sx[:half].astype(bf16), 2), swap(sy[half:].astype(bf16), 4)
    if eager:
        r0, r1, x0, y1 = lax.optimization_barrier((r0, r1, x0, y1))
    x1 = swap((sx[half:] + r1.astype(f32)).astype(bf16), 2)
    y0 = swap((sy[:half] + r0.astype(f32)).astype(bf16), 4)
    x1, y0, beside = lax.optimization_barrier((x1, y0, beside(r0) if callable(beside) else beside))
    x = jnp.concatenate([x0, x1], axis=0).astype(f32)
    y = jnp.concatenate([y0, y1], axis=0).astype(f32)
    return summed(0) + x + y, beside


def reduce_wide(partial, meanwhile):
    if not relative():
        return lax.psum(partial, "wide"), meanwhile(partial)
    core = lax.axis_index("wide") % 2
    half = partial.shape[0] // 2
    parts = partial.reshape(2, half, partial.shape[1])
    total = pick(parts, core).astype(f32) + swap(pick(parts, 1 - core), 1).astype(f32)
    low = total.astype(bf16)
    got = [swap(low, 2), swap(low, 4), swap(low, 6)]
    got, made = lax.optimization_barrier((got, meanwhile(low)))
    total = total + sum(p.astype(f32) for p in got)
    low = total.astype(bf16)
    mate = swap(low, 1)
    first = core == 0
    out = jnp.concatenate([jnp.where(first, low, mate), jnp.where(first, mate, low)], axis=0)
    return out, made


def after(x, *others):
    return lax.optimization_barrier((x,) + others)[0]


def turns(x):
    return [x] + [turn(x, k) for k in range(1, lax.axis_size("narrow"))]


def pad_to(x, axis, size):
    pads = [(0, 0)] * x.ndim
    pads[axis] = (0, size - x.shape[axis])
    return jnp.pad(x, pads)


def ordered_rows(pieces, group, cols):
    n, z = lax.axis_size("narrow"), lax.axis_index("narrow")
    rows, width = pieces[0].shape
    order = jnp.stack([(z - k) % n * group for k in range(n)]).astype(jnp.int32)

    def kernel(order_ref, *refs):
        out = refs[n]
        r = lax.broadcasted_iota(jnp.int32, (n * rows, rows), 0)
        j = lax.broadcasted_iota(jnp.int32, (n * rows, rows), 1)
        spot = j
        for i in range(1, rows // group):
            spot = spot + jnp.where(j >= i * group, (n - 1) * group, 0)
        value = jnp.zeros((n * rows, width), f32)
        for k in range(n):
            spots = jnp.where(r == spot + order_ref[k], 1.0, 0.0).astype(bf16)
            value = value + jnp.dot(spots, refs[k][...], preferred_element_type=f32)
        out[...] = jnp.zeros(out.shape, bf16)
        out[:, :width] = value.astype(bf16)

    vmem = pl.BlockSpec(memory_space=pltpu.VMEM)
    return pl.pallas_call(
        kernel,
        in_specs=[pl.BlockSpec(memory_space=pltpu.SMEM)] + [vmem] * n,
        out_specs=vmem,
        out_shape=jax.ShapeDtypeStruct((n * rows, cols), bf16),
        compiler_params=pltpu.CompilerParams(vmem_limit_bytes=VMEM),
    )(order, *pieces)


def gather_channels(pieces, splits, total):
    n, z = lax.axis_size("narrow"), lax.axis_index("narrow")
    rows, cols = pieces[0].shape
    order = jnp.stack([(z - k) % n * rows for k in range(n)]).astype(jnp.int32)

    def kernel(order_ref, *refs):
        value = jnp.zeros((total, cols), f32)
        r = lax.broadcasted_iota(jnp.int32, (total, rows), 0)
        j = lax.broadcasted_iota(jnp.int32, (total, rows), 1)
        for k in range(n):
            spots = jnp.where(r == j + order_ref[k], 1.0, 0.0).astype(bf16)
            value = value + jnp.dot(spots, refs[k][...], preferred_element_type=f32)
        value = value.astype(bf16)
        at = 0
        for out in refs[n:]:
            out[...] = value[:, at : at + out.shape[1]]
            at += out.shape[1]

    vmem = pl.BlockSpec(memory_space=pltpu.VMEM)
    return pl.pallas_call(
        kernel,
        in_specs=[pl.BlockSpec(memory_space=pltpu.SMEM)] + [vmem] * n,
        out_specs=[vmem] * len(splits),
        out_shape=[jax.ShapeDtypeStruct((total, c), bf16) for c in splits],
        compiler_params=pltpu.CompilerParams(vmem_limit_bytes=VMEM),
    )(order, *pieces)


def turns(x):
    return [x] + [turn(x, k) for k in range(1, lax.axis_size("narrow"))]


def turned(pieces):
    return [pieces[0]] + [turn(pieces[k], k) for k in range(1, len(pieces))]


def split_narrow(x, axis):
    n, z = lax.axis_size("narrow"), lax.axis_index("narrow")
    return [pick(x, (z + k) % n, axis) for k in range(n)]


def exchange(x):
    return lax.all_to_all(x, ("wide", "narrow"), 0, 0)


def gather_rows(parts):
    wide, rows, cols = parts.shape
    narrow = lax.axis_size("narrow")
    parts = jnp.broadcast_to(parts[:, None], (wide, narrow, rows, cols))
    got = exchange(parts.reshape(wide * narrow, rows, cols))
    return got.reshape(wide * narrow * rows, cols)


def scatter_rows(grad):
    got = exchange(grad)
    return got.reshape(lax.axis_size("wide"), lax.axis_size("narrow"), *grad.shape[1:])


def summed_rows(got):
    return sum(got[:, k].astype(f32) for k in range(got.shape[1]))


def mm(a, b):
    return jnp.dot(a, b, preferred_element_type=f32)


def mm_t(a, b):
    return lax.dot_general(a, b, (((1,), (1,)), ((), ())), preferred_element_type=f32)


def t_mm(a, b):
    return lax.dot_general(a, b, (((0,), (0,)), ((), ())), preferred_element_type=f32)


def sigmoid(v):
    return 1.0 / (1.0 + jnp.exp(-v))


def softplus(v):
    return jnp.maximum(v, 0.0) + jnp.log1p(jnp.exp(-jnp.abs(v)))


def call(kernel, grid, flip, ins, outs, scratch, flops, exps=0, aliases={}):
    def spec(block, where):
        if block is None:
            return pl.BlockSpec(memory_space=pltpu.HBM)
        if where is None:
            zeros = (0,) * len(block)
            return pl.BlockSpec(block, lambda i, s: zeros)
        return pl.BlockSpec(block, lambda i, s: (where(i, s[0]),) + (0,) * (len(block) - 1))

    size = sum(a.size * a.dtype.itemsize for a, _, _ in ins)
    size += sum(math.prod(o[0]) * jnp.dtype(o[1]).itemsize for o in outs)
    return pl.pallas_call(
        kernel,
        grid_spec=pltpu.PrefetchScalarGridSpec(
            num_scalar_prefetch=1,
            grid=(grid,),
            in_specs=[spec(b, f) for _, b, f in ins],
            out_specs=[spec(b, f) for _, _, b, f in outs],
            scratch_shapes=scratch,
        ),
        out_shape=[jax.ShapeDtypeStruct(o[0], o[1]) for o in outs],
        input_output_aliases=aliases,
        compiler_params=pltpu.CompilerParams(vmem_limit_bytes=VMEM),
        cost_estimate=pl.CostEstimate(flops=flops // 64, bytes_accessed=size // 64, transcendentals=0),
    )(flip, *[a for a, _, _ in ins])


def fetch_blocks(groups, held, sems, shift):
    for k, group in enumerate(groups):
        at = 0
        for ref in group:
            n = ref.shape[0]
            pltpu.make_async_copy(ref, held.at[k ^ shift, pl.ds(at, n)], sems.at[k ^ shift]).start()
            at += n


def wait_block(held, sems, i):
    pltpu.make_async_copy(held.at[i], held.at[i], sems.at[i]).wait()


def send_rows(value, stage, sems, outs, step, steps, block, at):
    slot = step % 2
    n = value.shape[0]

    def sent(k):
        return pltpu.make_async_copy(stage.at[k], stage.at[k], sems.at[k])

    @pl.when(step >= 2)
    def _():
        sent(slot).wait()

    stage[slot] = value
    for k, out in enumerate(outs):

        @pl.when(block == k)
        def _(out=out):
            pltpu.make_async_copy(stage.at[slot], out.at[pl.ds(at, n)], sems.at[slot]).start()

    @pl.when(step == steps - 1)
    def _():
        sent(0).wait()
        sent(1).wait()


def taken(refs, lengths):
    out, at = [], 0
    for n in lengths:
        out.append(refs[at : at + n])
        at += n
    return out, refs[at:]


def front(flip, tokens, gain, weight_x, taps, shift, weight_sel):
    wid = weight_x.shape[1]
    blocks = lax.axis_size("wide")
    rows = tokens[0][0].shape[0]
    length = rows * blocks
    counts = [len(g) for g in tokens]

    def kernel(s_ref, *refs):
        groups, refs = taken(refs, counts)
        gain_r, wx, taps_r, shift_r, wsel, normed, proj, conv, act, part, pad, held, sems = refs
        i = pl.program_id(0)

        @pl.when(i == 0)
        def _():
            fetch_blocks(groups, held, sems, s_ref[0])
            pad[:8, :] = jnp.zeros((8, wid), f32)

        wait_block(held, sems, i)
        values = held[i].astype(f32)
        inverse = lax.rsqrt(jnp.mean(values * values, axis=-1, keepdims=True) + EPSILON)
        low = (values * inverse * gain_r[...]).astype(bf16)
        normed[...] = low
        x = mm(low, wx[...])
        proj[...] = x
        pad[8:, :] = x
        total = shift_r[...] + taps_r[CONV - 1 : CONV, :] * x
        for k in range(CONV - 1):
            start = 8 - (CONV - 1) + k
            total = total + taps_r[k : k + 1, :] * pad[start : start + rows, :]
        pad[:8, :] = x[rows - 8 :, :]
        conv[...] = total
        low = (total * sigmoid(total)).astype(bf16)
        act[...] = low
        part[...] = mm(low, wsel[...]).astype(bf16)

    here = lambda i, s: i
    rel = lambda i, s: i ^ s
    return call(
        kernel,
        blocks,
        flip,
        [
            *[(part, None, None) for group in tokens for part in group],
            (gain, (1, D), None),
            (weight_x, (D, wid), None),
            (taps, (CONV, wid), None),
            (shift, (1, wid), None),
            (weight_sel, (wid, LANES), None),
        ],
        [
            ((length, D), bf16, (rows, D), rel),
            ((length, wid), f32, (rows, wid), here),
            ((length, wid), f32, (rows, wid), here),
            ((length, wid), bf16, (rows, wid), here),
            ((length, LANES), bf16, (rows, LANES), here),
        ],
        [
            pltpu.VMEM((rows + 8, wid), f32),
            pltpu.VMEM((blocks, rows, D), bf16),
            pltpu.SemaphoreType.DMA((blocks,)),
        ],
        2 * length * wid * (D + LANES),
    )


FLAT = CONV + 4 + NS
def row_sums(terms, masks):
    high, mid, low = masks
    c = [
        jnp.where(high, terms[i + 4], terms[i])
        + pltpu.roll(jnp.where(high, terms[i], terms[i + 4]), 4, 0)
        for i in range(4)
    ]
    c = [
        jnp.where(mid, c[i + 2] + pltpu.roll(c[i + 2], 2, 0), c[i] + pltpu.roll(c[i], 6, 0))
        for i in range(2)
    ]
    return jnp.where(low, c[1] + pltpu.roll(c[1], 1, 0), c[0] + pltpu.roll(c[0], 7, 0))


def row_masks(wid):
    row = lax.broadcasted_iota(jnp.int32, (8, wid), 0)
    return row >= 4, (row & 2) > 0, (row & 1) > 0


IN_AT = DT_RANK
OUT_AT = DT_RANK + NS


def middle(flip, sel, act, normed, weight_z, weight_step, shift, skip, a2, weight_out):
    length, wid = act.shape
    blocks = length // TIME_BLOCK
    per = blocks // lax.axis_size("wide")

    wide = lax.axis_size("wide")

    def kernel(
        s_ref, sel_r, act_r, n_r, wz, wstep, shift_r, skip_r, a_r, wout, z_o, lin_o, kept, end, mixed, gated_o, *refs
    ):
        (parts,), refs = taken(refs, [wide])
        state, dt_s, u_s, y_s, stage, sems = refs
        i = pl.program_id(0)

        @pl.when(pl.program_id(0) == 0)
        def _():
            state[...] = jnp.zeros_like(state)

        low = sel_r[...]
        lin = mm_t(low, wstep[...]) + shift_r[...]
        lin_o[...] = lin
        dt_s[...] = softplus(lin)
        u_s[...] = dt_s[...] * act_r[...].astype(f32)
        turned = low.astype(f32).T
        in_sel, out_sel = turned[IN_AT : IN_AT + NS, :], turned[OUT_AT : OUT_AT + NS, :]
        a2 = a_r[...]

        masks = row_masks(wid)
        h = state[...]
        terms = [None] * 8
        for t in range(TIME_BLOCK):
            kept[t] = h
            h = jnp.exp2(dt_s[t : t + 1, :] * a2) * h + u_s[t : t + 1, :] * in_sel[:, t : t + 1]
            y = h * out_sel[:, t : t + 1]
            terms[t % 8] = y[:8] + y[8:]
            if t % 8 == 7:
                y_s[t - 7 : t + 1, :] = row_sums(terms, masks)
        state[...] = h
        end[...] = h
        out = y_s[...] + skip_r[...] * act_r[...].astype(f32)
        mixed[...] = out
        z = mm(n_r[...], wz[...])
        z_o[...] = z
        gated = (out * z * sigmoid(z)).astype(bf16)
        gated_o[...] = gated
        value = mm(gated, wout[...]).astype(bf16)
        send_rows(value, stage, sems, parts, i, blocks, (i // per) ^ s_ref[0], i % per * TIME_BLOCK)

    here = lambda i, s: i
    rel = lambda i, s: ((i // per) ^ s) * per + i % per
    row = (TIME_BLOCK, wid)
    return call(
        kernel,
        blocks,
        flip,
        [
            (sel, (TIME_BLOCK, LANES), here),
            (act, row, here),
            (normed, (TIME_BLOCK, D), rel),
            (weight_z, (D, wid), None),
            (weight_step, (wid, LANES), None),
            (shift, (1, wid), None),
            (skip, (1, wid), None),
            (a2, (NS, wid), None),
            (weight_out, (wid, D), None),
        ],
        [
            ((length, wid), f32, row, here),
            ((length, wid), f32, row, here),
            ((length, NS, wid), f32, (TIME_BLOCK, NS, wid), here),
            ((NS, wid), f32, (NS, wid), None),
            ((length, wid), f32, row, here),
            ((length, wid), bf16, row, here),
            *[((length // wide, D), bf16, None, None)] * wide,
        ],
        [pltpu.VMEM((NS, wid), f32)]
        + [pltpu.VMEM(row, f32)] * 3
        + [pltpu.VMEM((2, TIME_BLOCK, D), bf16), pltpu.SemaphoreType.DMA((2,))],
        length * wid * (8 * NS + 4 * D + 2 * LANES),
        length * NS * wid,
    )


def experts(span, normed, cot, up, down, ff):
    rows = sum(p.shape[0] for p in normed[0])
    blocks = lax.axis_size("wide")
    length = rows * blocks
    cols = up.shape[1]
    share = down.shape[2]
    counts = [len(g) for g in normed]

    def kernel(s_ref, *refs):
        groups, refs = taken(refs, counts)
        ((cot_r, up_r, down_r), backs, outs), refs = taken(refs, [3, blocks, blocks])
        n_o, hid_o, both_o, dex_o, down_s, held, sems, stage, stage_sems, stage_2, stage_2_sems = refs
        i = pl.program_id(0)

        @pl.when(i == 0)
        def _():
            fetch_blocks(groups, held, sems, 0)
            for k in range(down.shape[0]):
                for e in range(EXPERTS):
                    down_s[e * ff + k * share : e * ff + (k + 1) * share, :] = down_r[k, e]

        wait_block(held, sems, i)
        n_o[...] = held[i]
        position = (i ^ s_ref[0]) * rows + lax.broadcasted_iota(jnp.int32, (rows, 1), 0)
        cot_b = cot_r[...]
        second = cot_b[:, D : D + 1] > 0.5
        upstream = jnp.where(position < s_ref[1], cot_b[:, :D], jnp.zeros((), bf16))
        raised = mm(n_o[...], up_r[...])
        first_l, second_l = raised[:, EXPERTS * ff : EXPERTS * ff + 1], raised[:, EXPERTS * ff + 1 : EXPERTS * ff + 2]
        lead = jnp.where(second, second_l - first_l, first_l - second_l)
        gate = sigmoid(lead)
        other = sigmoid(-lead)
        pre = jnp.where(second, raised[:, ff : 2 * ff], raised[:, :ff])
        bell = (1.0 + lax.erf(pre * (1.0 / math.sqrt(2.0)))) * 0.5
        hidden = pre * bell
        slope = bell + pre * jnp.exp(-0.5 * pre * pre) * (1.0 / math.sqrt(2.0 * math.pi))
        hidden = hidden.astype(bf16)
        hid_f = hidden.astype(f32)
        both = jnp.concatenate(
            [jnp.where(second, 0.0, hid_f), jnp.where(second, hid_f, 0.0)], axis=1
        ).astype(bf16)
        hid_o[...] = both
        value = (gate * mm(both, down_s[...])).astype(bf16)
        send_rows(value, stage_2, stage_2_sems, outs, i, blocks, i, 0)
        dex_o[...] = (gate * upstream.astype(f32)).astype(bf16)
        lowered = mm_t(upstream, down_s[...])
        d_hid = jnp.where(second, lowered[:, ff:], lowered[:, :ff])
        d_gate = jnp.sum(hid_f * d_hid, axis=-1, keepdims=True)
        d_pre = gate * d_hid * slope
        d_lead = gate * other * d_gate
        lane = lax.broadcasted_iota(jnp.int32, (rows, cols - EXPERTS * ff), 1)
        d_second = jnp.where(second, d_lead, -d_lead)
        d_logits = jnp.where(lane == 1, d_second, jnp.where(lane == 0, -d_second, 0.0))
        d_both = jnp.concatenate(
            [jnp.where(second, 0.0, d_pre), jnp.where(second, d_pre, 0.0), d_logits], axis=1
        ).astype(bf16)
        both_o[...] = d_both
        value = mm_t(d_both, up_r[...]).astype(bf16)
        send_rows(value, stage, stage_sems, backs, i, blocks, i, 0)

    here = lambda i, s: i
    made = call(
        kernel,
        blocks,
        span,
        [
            *[(part, None, None) for group in normed for part in group],
            (cot, (rows, D + LANES), lambda i, s: i ^ s),
            (up, up.shape, None),
            (down, down.shape, None),
        ],
        [
            *[((rows, D), bf16, None, None)] * (2 * blocks),
            ((length, D), bf16, (rows, D), here),
            ((length, EXPERTS * ff), bf16, (rows, EXPERTS * ff), here),
            ((length, cols), bf16, (rows, cols), here),
            ((length, D), bf16, (rows, D), here),
        ],
        [
            pltpu.VMEM((EXPERTS * ff, D), bf16),
            pltpu.VMEM((blocks, rows, D), bf16),
            pltpu.SemaphoreType.DMA((blocks,)),
            pltpu.VMEM((2, rows, D), bf16),
            pltpu.SemaphoreType.DMA((2,)),
            pltpu.VMEM((2, rows, D), bf16),
            pltpu.SemaphoreType.DMA((2,)),
        ],
        4 * length * D * (cols + EXPERTS * ff),
        3 * length * ff,
    )
    return made[:blocks], made[blocks : 2 * blocks], made[2 * blocks :]


def back(flip, d_mix, weight_out, sel, act, proj_z, lin, mixed, kept, end, weight_step, skip, a2):
    length, wid = act.shape
    blocks = length // TIME_BLOCK
    per = blocks // lax.axis_size("wide")

    counts = [len(g) for g in d_mix]

    def kernel(s_ref, *refs):
        mix_groups, refs = taken(refs, counts)
        (
            wout, sel_r, act_r, z_r, lin_r, mixed_r, kept_r, end_r, wstep, skip_r, a_r,
            mix_o, dz_o, part, dact_o, gstep_o, da_o, dskip_o, dbias_o,
            lam_s, next_s, pb_s, pc_s, dt_s, u_s, dy_s, s1_s, s2_s, turned_s, held, sems,
        ) = refs
        place = blocks - 1 - pl.program_id(0)

        @pl.when(pl.program_id(0) == 0)
        def _():
            fetch_blocks(mix_groups, held, sems, s_ref[0])
            lam_s[...] = jnp.zeros_like(lam_s)
            next_s[...] = end_r[...]
            da_o[...] = jnp.zeros_like(da_o)
            for ref in (gstep_o, dskip_o, dbias_o):
                ref[...] = jnp.zeros_like(ref)
            turned_s[...] = jnp.zeros_like(turned_s)

        @pl.when(pl.program_id(0) % per == 0)
        def _():
            wait_block(held, sems, place // per)

        mix = held[place // per, pl.ds(pl.multiple_of(place % per * TIME_BLOCK, TIME_BLOCK), TIME_BLOCK)]
        mix_o[...] = mix
        d_gated = mm_t(mix, wout[...])
        z = z_r[...]
        s = sigmoid(z)
        dz_o[...] = (d_gated * mixed_r[...] * (s * (1.0 + z * (1.0 - s)))).astype(bf16)
        dy_s[...] = d_gated * (z * s)
        x_all = act_r[...].astype(f32)
        dskip_o[...] += jnp.sum(dy_s[...] * x_all, axis=0, keepdims=True)
        dt_s[...] = softplus(lin_r[...])
        u_s[...] = dt_s[...] * x_all
        low = sel_r[...]
        turned = low.astype(f32).T
        in_sel, out_sel = turned[IN_AT : IN_AT + NS, :], turned[OUT_AT : OUT_AT + NS, :]
        a2 = a_r[...]

        def fold(v):
            total = v[:, :LANES]
            for k in range(1, wid // LANES):
                total = total + v[:, k * LANES : (k + 1) * LANES]
            return total

        masks = row_masks(wid)
        p, after, acc = lam_s[...], next_s[...], da_o[...]
        first, second = [None] * 8, [None] * 8
        for t in range(TIME_BLOCK - 1, -1, -1):
            before = kept_r[t]
            dt_t, dy_t = dt_s[t : t + 1, :], dy_s[t : t + 1, :]
            lam = dy_t * out_sel[:, t : t + 1] + p
            p = lam * jnp.exp2(dt_t * a2)
            moved = p * before
            acc = acc + dt_t * moved
            term = lam * in_sel[:, t : t + 1]
            first[t % 8] = term[:8] + term[8:]
            term = a2 * moved
            second[t % 8] = term[:8] + term[8:]
            if t % 8 == 0:
                s1_s[t : t + 8, :] = row_sums(first, masks)
                s2_s[t : t + 8, :] = row_sums(second, masks)
            pb_s[t] = fold(lam * u_s[t : t + 1, :])
            pc_s[t] = fold(after * dy_t)
            after = before
        lam_s[...] = p
        next_s[...] = after
        da_o[...] = acc
        ones = jnp.ones((LANES, LANES), bf16)
        lane = lax.broadcasted_iota(jnp.int32, (NS, TIME_BLOCK), 1)
        for source, at in ((pb_s, IN_AT), (pc_s, OUT_AT)):
            sums = mm(source[...].reshape(TIME_BLOCK * NS, LANES).astype(bf16), ones)
            sums = sums.reshape(TIME_BLOCK, NS, LANES)
            parts = [jnp.zeros((NS, TIME_BLOCK), f32)] * 4
            for t in range(TIME_BLOCK):
                parts[t % 4] = jnp.where(lane == t, sums[t], parts[t % 4])
            turned_s[at : at + NS, :] = (parts[0] + parts[1]) + (parts[2] + parts[3])
        through = s1_s[...]
        d_step = s2_s[...] * LN2 + x_all * through
        dact_o[...] = dt_s[...] * through + skip_r[...] * dy_s[...]
        grad = d_step * sigmoid(lin_r[...])
        dbias_o[...] += jnp.sum(grad, axis=0, keepdims=True)
        grad = grad.astype(bf16)
        gstep_o[...] += t_mm(grad, low)
        part[...] = (mm(grad, wstep[...]) + turned_s[...].T).astype(bf16)

    here = lambda i, s: blocks - 1 - i
    rel = lambda i, s: (((blocks - 1 - i) // per) ^ s) * per + (blocks - 1 - i) % per
    row = (TIME_BLOCK, wid)
    one = ((1, wid), f32, (1, wid), None)
    return call(
        kernel,
        blocks,
        flip,
        [
            *[(part, None, None) for group in d_mix for part in group],
            (weight_out, (wid, D), None),
            (sel, (TIME_BLOCK, LANES), here),
            (act, row, here),
            (proj_z, row, here),
            (lin, row, here),
            (mixed, row, here),
            (kept, (TIME_BLOCK, NS, wid), here),
            (end, (NS, wid), None),
            (weight_step, (wid, LANES), None),
            (skip, (1, wid), None),
            (a2, (NS, wid), None),
        ],
        [
            ((length, D), bf16, (TIME_BLOCK, D), here),
            ((length, wid), bf16, row, rel),
            ((length, LANES), bf16, (TIME_BLOCK, LANES), here),
            ((length, wid), f32, row, here),
            ((wid, LANES), f32, (wid, LANES), None),
            ((NS, wid), f32, (NS, wid), None),
            one,
            one,
        ],
        [pltpu.VMEM((NS, wid), f32)] * 2
        + [pltpu.VMEM((TIME_BLOCK, NS, LANES), f32)] * 2
        + [pltpu.VMEM(row, f32)] * 5
        + [pltpu.VMEM((LANES, TIME_BLOCK), f32)]
        + [
            pltpu.VMEM((lax.axis_size("wide"), length // lax.axis_size("wide"), D), bf16),
            pltpu.SemaphoreType.DMA((lax.axis_size("wide"),)),
        ],
        length * wid * (20 * NS + 2 * D + 2 * LANES),
        length * NS * wid,
    )


def tail(
    flip, d_sel, d_act, conv, proj, d_z, normed, act, weight_x, weight_z, weight_sel, taps,
    grad_step, grad_flat, grad_z, grad_out, beyond, chans,
):
    length, wid = act.shape
    blocks, count = lax.axis_size("wide"), lax.axis_size("narrow")
    rows = length // blocks
    group, c_rows = D // (blocks * count), chans // count

    def kernel(
        s_ref, sel_r, dact_r, conv_r, proj_r, dz_r, n_r, act_r, wx, wz, wsel, taps_r, gstep_r, flat_r,
        gz_r, gout_r, *refs,
    ):
        (parts, packs), refs = taken(refs, [blocks, count])
        gx_o, ext, gx, gsel, flat, held, stage, sems = refs
        i = pl.program_id(0)

        @pl.when(pl.program_id(0) == 0)
        def _():
            ext[rows:, :] = jnp.zeros((8, wid), f32)
            gx[...] = jnp.zeros_like(gx)
            gsel[...] = jnp.zeros_like(gsel)
            flat[...] = flat_r[...]

        low = sel_r[...]
        c = conv_r[...]
        q = sigmoid(c)
        d_conv = (mm_t(low, wsel[...]) + dact_r[...]) * (q * (1.0 + c * (1.0 - q)))
        ext[:rows, :] = d_conv
        flat[CONV : CONV + 1, :] += jnp.sum(d_conv, axis=0, keepdims=True)
        x = proj_r[...]
        d_x = jnp.zeros((rows, wid), f32)
        for k in range(CONV):
            moved = ext[CONV - 1 - k : CONV - 1 - k + rows, :]
            d_x = d_x + taps_r[k : k + 1, :] * moved
            flat[k : k + 1, :] += jnp.sum(moved * x, axis=0, keepdims=True)
        ext[rows:, :] = d_conv[:8, :]
        d_x = d_x.astype(bf16)
        value = (mm_t(d_x, wx[...]) + mm_t(dz_r[...], wz[...])).astype(bf16)
        send_rows(value, stage, sems, parts, i, blocks, (blocks - 1 - i) ^ s_ref[0], 0)
        gx[...] += t_mm(n_r[...], d_x)
        gsel[...] += t_mm(act_r[...], low)

        @pl.when(pl.program_id(0) == blocks - 1)
        def _():
            for k in range(blocks * count):
                x = gx[k * group : (k + 1) * group, :chans]
                gx_o[k] = jnp.concatenate([x, gz_r[k].astype(f32)], axis=1).astype(bf16)
            tall = jnp.concatenate(
                [jnp.zeros((DT_RANK, wid), f32), flat[...], jnp.zeros((LANES - DT_RANK - FLAT, wid), f32)], axis=0
            )
            lane = lax.broadcasted_iota(jnp.int32, (wid, LANES), 1)
            left = jnp.where(lane < DT_RANK, gstep_r[...], tall.T)
            held[:, :LANES] = left
            held[:, LANES:] = gsel[...]
            for k, out in enumerate(packs):
                if c_rows % 8 == 0:
                    at = pl.multiple_of(s_ref[1 + k] * c_rows, 8)
                    out[:, :D] = gout_r[pl.ds(at, c_rows), :].astype(bf16)
                    out[:, D:] = held[pl.ds(at, c_rows), :].astype(bf16)
                    continue
                for p in range(count):

                    @pl.when(s_ref[1 + k] == p)
                    def _(out=out, at=p * c_rows):
                        out[:, :D] = gout_r[at : at + c_rows, :].astype(bf16)
                        out[:, D:] = held[at : at + c_rows, :].astype(bf16)

    here = lambda i, s: blocks - 1 - i
    rel = lambda i, s: (blocks - 1 - i) ^ s
    row = (rows, wid)
    pack = (c_rows, D + 2 * LANES)
    sent = (blocks * count, group, 2 * chans)
    return call(
        kernel,
        blocks,
        jnp.concatenate([flip, beyond]),
        [
            (d_sel, (rows, LANES), here),
            (d_act, row, here),
            (conv, row, here),
            (proj, row, here),
            (d_z, row, rel),
            (normed, (rows, D), rel),
            (act, row, here),
            (weight_x, (D, wid), None),
            (weight_z, (D, wid), None),
            (weight_sel, (wid, LANES), None),
            (taps, (CONV, wid), None),
            (grad_step, (wid, LANES), None),
            (grad_flat, (FLAT, wid), None),
            (grad_z, grad_z.shape, None),
            (grad_out, (wid, D), None),
        ],
        [*[((rows, D), bf16, None, None)] * blocks, *[(pack, bf16, pack, None)] * count, (sent, bf16, sent, None)],
        [
            pltpu.VMEM((rows + 8, wid), f32),
            pltpu.VMEM((D, wid), f32),
            pltpu.VMEM((wid, LANES), f32),
            pltpu.VMEM((FLAT, wid), f32),
            pltpu.VMEM((wid, 2 * LANES), f32),
            pltpu.VMEM((2, rows, D), bf16),
            pltpu.SemaphoreType.DMA((2,)),
        ],
        2 * length * wid * (3 * D + 2 * LANES),
    )


def row_grad(flip, a, b, cols, group, along):
    narrow = lax.axis_size("narrow")
    length, total = a.shape
    n = b.shape[1]
    blocks = lax.axis_size("wide")
    rows = length // blocks

    def kernel(s_ref, a_r, b_r, out, acc):
        @pl.when(pl.program_id(0) == 0)
        def _():
            acc[...] = jnp.zeros_like(acc)

        acc[...] += t_mm(a_r[...], b_r[...])

        @pl.when(pl.program_id(0) == blocks - 1)
        def _():
            for k in range(total // group):
                at = k % narrow * blocks + k // narrow if along else k
                out[at] = acc[k * group : (k + 1) * group, :cols].astype(bf16)

    here = lambda i, s: i
    return call(
        kernel,
        blocks,
        flip,
        [(a, (rows, total), here), (b, (rows, n), here)],
        [((total // group, group, cols), bf16, (total // group, group, cols), None)],
        [pltpu.VMEM((total, n), f32)],
        2 * length * total * n,
    )[0]


def joined(got):
    wide, narrow, rows, cols = got.shape
    half = cols // 2

    def kernel(got_r, out):
        parts = [sum(got_r[w, k].astype(f32) for k in range(narrow)) for w in range(wide)]
        out[:, : wide * half] = jnp.concatenate([p[:, :half] for p in parts], axis=1)
        out[:, wide * half :] = jnp.concatenate([p[:, half:] for p in parts], axis=1)

    vmem = pl.BlockSpec(memory_space=pltpu.VMEM)
    return pl.pallas_call(
        kernel,
        in_specs=[vmem],
        out_specs=vmem,
        out_shape=jax.ShapeDtypeStruct((rows, wide * cols), f32),
        compiler_params=pltpu.CompilerParams(vmem_limit_bytes=VMEM),
    )(got)


def norm_backward(values, inverse, gain_vec, upstream):
    scaled = upstream * gain_vec
    inner_mean = jnp.mean(values * scaled, axis=-1, keepdims=True)
    return inverse * scaled - values * (inverse * inverse * inverse) * inner_mean


def local(
    tokens,
    mixer_gain,
    in_weight,
    conv_weight,
    conv_bias,
    select_weight,
    step_weight,
    step_bias,
    decay_log,
    skip_weight,
    out_weight,
    expert_gain,
    router_weight,
    up_weight,
    down_weight,
    routes,
    lengths,
    cotangent,
):
    wide, narrow = lax.axis_size("wide"), lax.axis_size("narrow")
    w = lax.axis_index("wide")
    rows = tokens.shape[1]
    chans = DI // wide
    wid = -(-chans // LANES) * LANES
    ff = FF // wide
    d_rows = D // (wide * narrow)
    c_rows = DI // (wide * narrow)
    f_rows = FF // (wide * narrow)
    both = EXPERTS * ff
    flip = w if relative() else 0 * w
    span = jnp.stack([flip, lengths[0]]).astype(jnp.int32)

    tokens_own = tokens[0].astype(f32)

    in_parts = in_weight.reshape(d_rows, 2, wide, chans).transpose(1, 2, 0, 3)
    gains = jnp.stack([mixer_gain, expert_gain], axis=1)
    gains = jnp.broadcast_to(gains[None], (wide, d_rows, 2))
    zero_col = jnp.zeros((c_rows, 1), bf16)
    channel_pack = jnp.concatenate(
        [
            conv_weight.T,
            conv_bias[:, None],
            step_bias[:, None],
            skip_weight[:, None],
            zero_col,
            decay_log.T,
            step_weight.T,
            select_weight,
        ],
        axis=1,
    )
    pack_cols = channel_pack.shape[1]
    wide_cols = -(-pack_cols // LANES) * LANES
    channel_pack = pad_to(channel_pack, 1, wide_cols)
    x_parts = jnp.concatenate([in_parts[0], gains], axis=2)
    tokens_all, channel_pack = gather_wide(tokens[0], lambda block: turns(channel_pack))
    x_full = gather_rows(after(x_parts, channel_pack))
    x_full, tokens_all = lax.optimization_barrier((x_full, tokens_all))
    weight_x = pad_to(x_full[:, :chans], 1, wid)
    gains = x_full[:, chans:].T.astype(f32)
    gain_one, gain_two = gains[:1], gains[1:]
    up_parts = up_weight.reshape(EXPERTS, d_rows, wide, ff).transpose(2, 1, 0, 3)
    up_parts = up_parts.reshape(wide, d_rows, both)
    router_parts = jnp.broadcast_to(router_weight[None], (wide, d_rows, EXPERTS))
    up_parts = jnp.concatenate([up_parts, router_parts, in_parts[1]], axis=2)
    up_parts = lax.all_to_all(after(up_parts, x_full), "wide", 0, 0)
    up_parts = up_parts.reshape(wide * d_rows, both + EXPERTS + chans)
    route_cols = jnp.broadcast_to(routes[0].astype(bf16)[:, None], (rows, LANES))
    cot_ext = jnp.concatenate([cotangent[0], route_cols], axis=1)
    cot_all = lax.all_gather(after(cot_ext, tokens_all), "wide", axis=0, tiled=True)
    (packed,) = gather_channels(channel_pack, (wide_cols,), wid)
    flat = packed[:, :FLAT].T.astype(f32)
    taps = flat[:CONV]
    conv_shift, step_shift, skip = (flat[CONV + k : CONV + k + 1] for k in range(3))
    a_neg = -jnp.exp(flat[CONV + 4 :])
    a2 = a_neg * (1.0 / LN2)
    weight_step = pad_to(packed[:, FLAT : FLAT + DT_RANK], 1, LANES)
    weight_sel = pad_to(packed[:, FLAT + DT_RANK : pack_cols], 1, LANES)

    normed, proj_x, conv_sum, conv_act, sel_part = front(
        flip[None], tokens_all, gain_one, weight_x, taps, conv_shift, weight_sel
    )
    out_pieces = turns(after(out_weight, x_full))
    sel_part, up_parts, out_pieces = lax.optimization_barrier((sel_part, up_parts, out_pieces))
    z_pieces = turns(up_parts[:, both + EXPERTS :])
    up_parts = up_parts[:, : both + EXPERTS]
    selected, z_pieces = reduce_wide(sel_part, lambda low: z_pieces)
    weight_z = ordered_rows(z_pieces, d_rows, wid)

    up_cols = -(-(both + EXPERTS) // LANES) * LANES
    up_pieces = turns(after(up_parts, selected, out_pieces))
    valid_own = (w * rows + jnp.arange(rows))[:, None] < lengths[0]
    upstream = jnp.where(valid_own, cotangent[0].astype(f32), 0.0)

    (weight_out,) = gather_channels(out_pieces, (D,), wid)
    proj_z, step_lin, kept, end, mixed, gated, *mix_part = middle(
        flip[None], selected, conv_act, normed, weight_z, weight_step, step_shift, skip, a2, weight_out
    )
    mix_part, up_pieces = lax.optimization_barrier((mix_part, up_pieces))
    down_full = lax.all_gather(after(down_weight, cot_all, *up_pieces), "narrow")
    up_full = ordered_rows(up_pieces, d_rows, up_cols)
    mixer_sum, up_full = scatter_wide(mix_part, up_full, True)
    hidden_one = tokens_own + mixer_sum
    inverse_two = lax.rsqrt(jnp.mean(hidden_one * hidden_one, axis=-1, keepdims=True) + EPSILON)
    own = (hidden_one * inverse_two * gain_two).astype(bf16)

    pieces, _ = gather_wide(own)
    back_parts, out_parts, made = experts(span, pieces, cot_all, up_full, down_full, ff)
    normed_two, hidden_both, d_both, d_expert = made

    def beside(hop):
        hidden, outs = lax.optimization_barrier((hidden_both, out_parts, hop))[:2]
        grad = t_mm(hidden, d_expert).astype(bf16)
        grad = grad.reshape(EXPERTS, narrow, f_rows, D).transpose(1, 0, 2, 3)
        if not relative():
            return grad, outs
        pair = lambda q: outs[2 * q].astype(f32) + swap(outs[2 * q + 1], 1).astype(f32)
        return grad, [pair(q).astype(bf16) for q in range(4)]

    d_normed_two, (grad_down, out_sums) = scatter_wide(back_parts, beside, True)
    grad_down = lax.psum_scatter(grad_down, "narrow", scatter_dimension=0)
    d_hidden_one = upstream + norm_backward(hidden_one, inverse_two, gain_two, d_normed_two)
    d_low = d_hidden_one.astype(bf16)
    d_mix, grad_up = gather_wide(
        d_low,
        lambda low: row_grad(flip[None], normed_two, after(d_both, low), both + EXPERTS, d_rows, True),
    )
    grad_up = lax.psum_scatter(
        after(grad_up, d_mix).reshape(narrow, wide, d_rows, both + EXPERTS), "narrow", scatter_dimension=0
    )
    if relative():
        sent = after(out_sums, d_mix)
        out_got = [swap(sent[q], 2 * q) for q in (1, 2, 3)]
    else:
        out_got = []

    d_mix_all, d_z, d_sel_part, d_act, grad_step, d_a, grad_skip, grad_step_bias = back(
        flip[None], d_mix, weight_out, selected, conv_act, proj_z, step_lin, mixed, kept, end,
        weight_step, skip, a2,
    )

    d_sel_part, out_got = lax.optimization_barrier((d_sel_part, out_got))

    def meanwhile(low):
        grad_out = t_mm(after(gated, low), d_mix_all)
        return grad_out, row_grad(flip[None], after(normed, low), d_z, chans, d_rows, False)

    d_sel, (grad_out, grad_z) = reduce_wide(d_sel_part, meanwhile)
    z = lax.axis_index("narrow")
    beyond = jnp.stack([(z + k) % narrow for k in range(narrow)]).astype(jnp.int32)
    grad_flat = jnp.concatenate(
        [jnp.zeros((CONV + 1, wid), f32), grad_step_bias, grad_skip, jnp.zeros((1, wid), f32), d_a * a_neg],
        axis=0,
    )
    grad_up = lax.all_to_all(after(grad_up, d_sel), "wide", 0, 0)
    made = tail(
        flip[None], d_sel, d_act, conv_sum, proj_x, d_z, normed, conv_act, weight_x, weight_z,
        weight_sel, taps, grad_step, grad_flat, grad_z, grad_out, beyond, chans,
    )
    in_part, channel_grads, grad_in = made[:wide], made[wide:-1], made[-1]
    in_part, grad_up = lax.optimization_barrier((in_part, grad_up))
    grad_in = scatter_rows(grad_in)

    def beside(hop):
        up, down = lax.optimization_barrier((grad_up, grad_down, hop))[:2]
        up = up.astype(f32)
        router = jnp.sum(up[:, :, both:], axis=0)
        up = up[:, :, :both].reshape(wide, d_rows, EXPERTS, ff)
        up = up.transpose(2, 1, 0, 3).reshape(EXPERTS, d_rows, FF)
        gain = (
            jnp.sum(up_weight.astype(f32) * up, axis=(0, 2))
            + jnp.sum(router_weight.astype(f32) * router, axis=1)
        ) / expert_gain.astype(f32)
        if relative():
            out = sum(p.astype(f32) for p in lax.optimization_barrier(([out_sums[0], *out_got], hop))[0])
        else:
            out, _ = scatter_wide(out_sums)
        return up, router, gain, down.astype(f32), out, turned(channel_grads)

    d_normed, made = scatter_wide(in_part, beside)
    channel_grads = made[-1]
    made = made[:-1]
    grad_up, grad_router, grad_gain_two, grad_down, expert_sum = made
    d_normed, grad_in = lax.optimization_barrier((d_normed, grad_in))
    channel_grads = sum(p.astype(f32) for p in channel_grads)
    grad_out, channel_grads = channel_grads[:, :D], channel_grads[:, D:]
    inverse_one = lax.rsqrt(jnp.mean(tokens_own * tokens_own, axis=-1, keepdims=True) + EPSILON)
    token_grad = d_hidden_one + norm_backward(tokens_own, inverse_one, gain_one, d_normed)
    output = (hidden_one + expert_sum).astype(bf16)

    grad_in = joined(grad_in)
    grad_gain_one = jnp.sum(in_weight.astype(f32) * grad_in, axis=1) / mixer_gain.astype(f32)
    flat_grads = channel_grads[:, DT_RANK : DT_RANK + FLAT].T
    return (
        output[None],
        token_grad[None],
        grad_gain_one,
        grad_in,
        flat_grads[:CONV],
        flat_grads[CONV],
        channel_grads[:, LANES : LANES + DT_RANK + 2 * NS],
        channel_grads[:, :DT_RANK].T,
        flat_grads[CONV + 1],
        flat_grads[CONV + 4 :],
        flat_grads[CONV + 2],
        grad_out,
        grad_gain_two,
        grad_router,
        grad_up,
        grad_down,
    )


def solution(mesh):
    both = ("wide", "narrow")
    return jax.shard_map(
        local,
        mesh=mesh,
        in_specs=(
            P("narrow", "wide", None),
            P(both),
            P(both, None),
            P(None, both),
            P(both),
            P(both, None),
            P(None, both),
            P(both),
            P(None, both),
            P(both),
            P(both, None),
            P(both),
            P(both, None),
            P(None, both, None),
            P(None, both, None),
            P("narrow", "wide"),
            P("narrow"),
            P("narrow", "wide", None),
        ),
        out_specs=(
            P("narrow", "wide", None),
            P("narrow", "wide", None),
            P(both),
            P(both, None),
            P(None, both),
            P(both),
            P(both, None),
            P(None, both),
            P(both),
            P(None, both),
            P(both),
            P(both, None),
            P(both),
            P(both, None),
            P(None, both, None),
            P(None, both, None),
        ),
        check_vma=False,
    )
```

```python
import math

import jax
import jax.numpy as jnp
from jax import lax
from jax.experimental import pallas as pl
from jax.experimental.pallas import tpu as pltpu
from jax.sharding import PartitionSpec as P

D = 1152
DI = 2304
NS = 16
DT_RANK = 72
CONV = 4
FF = 3072
EXPERTS = 2
EPSILON = 1e-05
TIME_BLOCK = 128
VMEM = 60 * 2**20
LANES = 128
LN2 = math.log(2.0)

f32 = jnp.float32
bf16 = jnp.bfloat16


def relative():
    return lax.axis_size("wide") == 8


def swap(x, k):
    n = lax.axis_size("wide")
    return lax.ppermute(x, "wide", [(i, i ^ k) for i in range(n)])


def turn(x, k):
    n = lax.axis_size("narrow")
    return lax.ppermute(x, "narrow", [(i, (i + k) % n) for i in range(n)])


def pick(x, i, axis=0):
    return lax.dynamic_index_in_dim(x, i, axis, False)


def blocks_of(x):
    return [[b] for b in jnp.split(x, lax.axis_size("wide"), axis=0)]


def gather_wide(block, meanwhile=None, second=None):
    if not relative():
        made = meanwhile(block) if meanwhile else ()
        made = (made, second(block)) if second else made
        return blocks_of(lax.all_gather(block, "wide", axis=0, tiled=True)), made
    half = block.shape[0] // 2
    mate = swap(block, 1)
    a, b = swap(block, 2), swap(block, 4)
    made = ()
    if meanwhile:
        made = meanwhile(block)
        a, b, made = lax.optimization_barrier((a, b, made))
    c0, c1 = swap(a[:half], 4), swap(b[half:], 2)
    if second:
        c0, c1, late = lax.optimization_barrier((c0, c1, second(a)))
        made = (made, late)
    out = [[block], [mate], [a], [swap(a, 1)], [b], [swap(b, 1)], [c0, c1], [swap(c0, 1), swap(c1, 1)]]
    return out, made


def scatter_wide(parts, beside=(), eager=False):
    if not relative():
        whole = jnp.concatenate(parts, axis=0)
        total = lax.psum_scatter(whole, "wide", scatter_dimension=0, tiled=True).astype(f32)
        return total, beside(total) if callable(beside) else beside
    half = parts[0].shape[0] // 2

    def summed(q):
        return parts[2 * q].astype(f32) + swap(parts[2 * q + 1], 1).astype(f32)

    far = summed(3).astype(bf16)
    r0, r1 = swap(far[:half], 2), swap(far[half:], 4)
    sx, sy = summed(1), summed(2)
    x0, y1 = swap(sx[:half].astype(bf16), 2), swap(sy[half:].astype(bf16), 4)
    if eager:
        r0, r1, x0, y1 = lax.optimization_barrier((r0, r1, x0, y1))
    x1 = swap((sx[half:] + r1.astype(f32)).astype(bf16), 2)
    y0 = swap((sy[:half] + r0.astype(f32)).astype(bf16), 4)
    x1, y0, beside = lax.optimization_barrier((x1, y0, beside(r0) if callable(beside) else beside))
    x = jnp.concatenate([x0, x1], axis=0).astype(f32)
    y = jnp.concatenate([y0, y1], axis=0).astype(f32)
    return summed(0) + x + y, beside


def reduce_wide(partial, meanwhile):
    if not relative():
        return lax.psum(partial, "wide"), meanwhile(partial)
    core = lax.axis_index("wide") % 2
    half = partial.shape[0] // 2
    parts = partial.reshape(2, half, partial.shape[1])
    total = pick(parts, core).astype(f32) + swap(pick(parts, 1 - core), 1).astype(f32)
    low = total.astype(bf16)
    got = [swap(low, 2), swap(low, 4), swap(low, 6)]
    got, made = lax.optimization_barrier((got, meanwhile(low)))
    total = total + sum(p.astype(f32) for p in got)
    low = total.astype(bf16)
    mate = swap(low, 1)
    first = core == 0
    out = jnp.concatenate([jnp.where(first, low, mate), jnp.where(first, mate, low)], axis=0)
    return out, made


def after(x, *others):
    return lax.optimization_barrier((x,) + others)[0]


def turns(x):
    return [x] + [turn(x, k) for k in range(1, lax.axis_size("narrow"))]


def pad_to(x, axis, size):
    pads = [(0, 0)] * x.ndim
    pads[axis] = (0, size - x.shape[axis])
    return jnp.pad(x, pads)


def ordered_rows(pieces, group, cols):
    n, z = lax.axis_size("narrow"), lax.axis_index("narrow")
    rows, width = pieces[0].shape
    order = jnp.stack([(z - k) % n * group for k in range(n)]).astype(jnp.int32)

    def kernel(order_ref, *refs):
        out = refs[n]
        r = lax.broadcasted_iota(jnp.int32, (n * rows, rows), 0)
        j = lax.broadcasted_iota(jnp.int32, (n * rows, rows), 1)
        spot = j
        for i in range(1, rows // group):
            spot = spot + jnp.where(j >= i * group, (n - 1) * group, 0)
        value = jnp.zeros((n * rows, width), f32)
        for k in range(n):
            spots = jnp.where(r == spot + order_ref[k], 1.0, 0.0).astype(bf16)
            value = value + jnp.dot(spots, refs[k][...], preferred_element_type=f32)
        out[...] = jnp.zeros(out.shape, bf16)
        out[:, :width] = value.astype(bf16)

    vmem = pl.BlockSpec(memory_space=pltpu.VMEM)
    return pl.pallas_call(
        kernel,
        in_specs=[pl.BlockSpec(memory_space=pltpu.SMEM)] + [vmem] * n,
        out_specs=vmem,
        out_shape=jax.ShapeDtypeStruct((n * rows, cols), bf16),
        compiler_params=pltpu.CompilerParams(vmem_limit_bytes=VMEM),
    )(order, *pieces)


def gather_channels(pieces, splits, total):
    n, z = lax.axis_size("narrow"), lax.axis_index("narrow")
    rows, cols = pieces[0].shape
    order = jnp.stack([(z - k) % n * rows for k in range(n)]).astype(jnp.int32)

    def kernel(order_ref, *refs):
        value = jnp.zeros((total, cols), f32)
        r = lax.broadcasted_iota(jnp.int32, (total, rows), 0)
        j = lax.broadcasted_iota(jnp.int32, (total, rows), 1)
        for k in range(n):
            spots = jnp.where(r == j + order_ref[k], 1.0, 0.0).astype(bf16)
            value = value + jnp.dot(spots, refs[k][...], preferred_element_type=f32)
        value = value.astype(bf16)
        at = 0
        for out in refs[n:]:
            out[...] = value[:, at : at + out.shape[1]]
            at += out.shape[1]

    vmem = pl.BlockSpec(memory_space=pltpu.VMEM)
    return pl.pallas_call(
        kernel,
        in_specs=[pl.BlockSpec(memory_space=pltpu.SMEM)] + [vmem] * n,
        out_specs=[vmem] * len(splits),
        out_shape=[jax.ShapeDtypeStruct((total, c), bf16) for c in splits],
        compiler_params=pltpu.CompilerParams(vmem_limit_bytes=VMEM),
    )(order, *pieces)


def turns(x):
    return [x] + [turn(x, k) for k in range(1, lax.axis_size("narrow"))]


def turned(pieces):
    return [pieces[0]] + [turn(pieces[k], k) for k in range(1, len(pieces))]


def split_narrow(x, axis):
    n, z = lax.axis_size("narrow"), lax.axis_index("narrow")
    return [pick(x, (z + k) % n, axis) for k in range(n)]


def exchange(x):
    return lax.all_to_all(x, ("wide", "narrow"), 0, 0)


def gather_rows(parts):
    wide, rows, cols = parts.shape
    narrow = lax.axis_size("narrow")
    parts = jnp.broadcast_to(parts[:, None], (wide, narrow, rows, cols))
    got = exchange(parts.reshape(wide * narrow, rows, cols))
    return got.reshape(wide * narrow * rows, cols)


def scatter_rows(grad):
    got = exchange(grad)
    return got.reshape(lax.axis_size("wide"), lax.axis_size("narrow"), *grad.shape[1:])


def summed_rows(got):
    return sum(got[:, k].astype(f32) for k in range(got.shape[1]))


def mm(a, b):
    return jnp.dot(a, b, preferred_element_type=f32)


def mm_t(a, b):
    return lax.dot_general(a, b, (((1,), (1,)), ((), ())), preferred_element_type=f32)


def t_mm(a, b):
    return lax.dot_general(a, b, (((0,), (0,)), ((), ())), preferred_element_type=f32)


def sigmoid(v):
    return 1.0 / (1.0 + jnp.exp(-v))


def softplus(v):
    return jnp.maximum(v, 0.0) + jnp.log1p(jnp.exp(-jnp.abs(v)))


def call(kernel, grid, flip, ins, outs, scratch, flops, exps=0, aliases={}):
    def spec(block, where):
        if block is None:
            return pl.BlockSpec(memory_space=pltpu.HBM)
        if where is None:
            zeros = (0,) * len(block)
            return pl.BlockSpec(block, lambda i, s: zeros)
        return pl.BlockSpec(block, lambda i, s: (where(i, s[0]),) + (0,) * (len(block) - 1))

    size = sum(a.size * a.dtype.itemsize for a, _, _ in ins)
    size += sum(math.prod(o[0]) * jnp.dtype(o[1]).itemsize for o in outs)
    return pl.pallas_call(
        kernel,
        grid_spec=pltpu.PrefetchScalarGridSpec(
            num_scalar_prefetch=1,
            grid=(grid,),
            in_specs=[spec(b, f) for _, b, f in ins],
            out_specs=[spec(b, f) for _, _, b, f in outs],
            scratch_shapes=scratch,
        ),
        out_shape=[jax.ShapeDtypeStruct(o[0], o[1]) for o in outs],
        input_output_aliases=aliases,
        compiler_params=pltpu.CompilerParams(vmem_limit_bytes=VMEM),
        cost_estimate=pl.CostEstimate(flops=flops // 64, bytes_accessed=size // 64, transcendentals=0),
    )(flip, *[a for a, _, _ in ins])


def fetch_blocks(groups, held, sems, shift):
    for k, group in enumerate(groups):
        at = 0
        for ref in group:
            n = ref.shape[0]
            pltpu.make_async_copy(ref, held.at[k ^ shift, pl.ds(at, n)], sems.at[k ^ shift]).start()
            at += n


def wait_block(held, sems, i):
    pltpu.make_async_copy(held.at[i], held.at[i], sems.at[i]).wait()


def send_ready(stage, sems, step):
    @pl.when(step >= 2)
    def _():
        pltpu.make_async_copy(stage.at[step % 2], stage.at[step % 2], sems.at[step % 2]).wait()


def send_rows(stage, sems, outs, step, steps, block, at):
    slot = step % 2
    for k, out in enumerate(outs):

        @pl.when(block == k)
        def _(out=out):
            part = out.at[pl.ds(at, stage.shape[1])]
            pltpu.make_async_copy(stage.at[slot], part, sems.at[slot]).start()

    @pl.when(step == steps - 1)
    def _():
        for k in range(2):
            pltpu.make_async_copy(stage.at[k], stage.at[k], sems.at[k]).wait()


def taken(refs, lengths):
    out, at = [], 0
    for n in lengths:
        out.append(refs[at : at + n])
        at += n
    return out, refs[at:]


def front(flip, tokens, gain, weight_x, taps, shift, weight_sel):
    wid = weight_x.shape[1]
    blocks = lax.axis_size("wide")
    rows = tokens[0][0].shape[0]
    length = rows * blocks
    counts = [len(g) for g in tokens]

    def kernel(s_ref, *refs):
        groups, refs = taken(refs, counts)
        gain_r, wx, taps_r, shift_r, wsel, normed, proj, conv, act, part, pad, held, sems = refs
        i = pl.program_id(0)

        @pl.when(i == 0)
        def _():
            fetch_blocks(groups, held, sems, s_ref[0])
            pad[:8, :] = jnp.zeros((8, wid), f32)

        wait_block(held, sems, i)
        values = held[i].astype(f32)
        inverse = lax.rsqrt(jnp.mean(values * values, axis=-1, keepdims=True) + EPSILON)
        low = (values * inverse * gain_r[...]).astype(bf16)
        normed[...] = low
        x = mm(low, wx[...])
        proj[...] = x
        pad[8:, :] = x
        total = shift_r[...] + taps_r[CONV - 1 : CONV, :] * x
        for k in range(CONV - 1):
            start = 8 - (CONV - 1) + k
            total = total + taps_r[k : k + 1, :] * pad[start : start + rows, :]
        pad[:8, :] = x[rows - 8 :, :]
        conv[...] = total
        low = (total * sigmoid(total)).astype(bf16)
        act[...] = low
        part[...] = mm(low, wsel[...]).astype(bf16)

    here = lambda i, s: i
    rel = lambda i, s: i ^ s
    return call(
        kernel,
        blocks,
        flip,
        [
            *[(part, None, None) for group in tokens for part in group],
            (gain, (1, D), None),
            (weight_x, (D, wid), None),
            (taps, (CONV, wid), None),
            (shift, (1, wid), None),
            (weight_sel, (wid, LANES), None),
        ],
        [
            ((length, D), bf16, (rows, D), rel),
            ((length, wid), f32, (rows, wid), here),
            ((length, wid), f32, (rows, wid), here),
            ((length, wid), bf16, (rows, wid), here),
            ((length, LANES), bf16, (rows, LANES), here),
        ],
        [
            pltpu.VMEM((rows + 8, wid), f32),
            pltpu.VMEM((blocks, rows, D), bf16),
            pltpu.SemaphoreType.DMA((blocks,)),
        ],
        2 * length * wid * (D + LANES),
    )


FLAT = CONV + 4 + NS
def row_sums(terms, masks):
    high, mid, low = masks
    c = [
        jnp.where(high, terms[i + 4], terms[i])
        + pltpu.roll(jnp.where(high, terms[i], terms[i + 4]), 4, 0)
        for i in range(4)
    ]
    c = [
        jnp.where(mid, c[i + 2] + pltpu.roll(c[i + 2], 2, 0), c[i] + pltpu.roll(c[i], 6, 0))
        for i in range(2)
    ]
    return jnp.where(low, c[1] + pltpu.roll(c[1], 1, 0), c[0] + pltpu.roll(c[0], 7, 0))


def row_masks(wid):
    row = lax.broadcasted_iota(jnp.int32, (8, wid), 0)
    return row >= 4, (row & 2) > 0, (row & 1) > 0


IN_AT = DT_RANK
OUT_AT = DT_RANK + NS


def middle(flip, sel, act, normed, weight_z, weight_step, shift, skip, a2, weight_out):
    length, wid = act.shape
    blocks = length // TIME_BLOCK
    per = blocks // lax.axis_size("wide")

    wide = lax.axis_size("wide")

    def kernel(
        s_ref, sel_r, act_r, n_r, wz, wstep, shift_r, skip_r, a_r, wout, z_o, lin_o, kept, end, mixed, gated_o, *refs
    ):
        (parts,), refs = taken(refs, [wide])
        state, dt_s, u_s, y_s, stage, sems = refs
        i = pl.program_id(0)

        send_ready(stage, sems, i)

        @pl.when(i == 0)
        def _():
            state[...] = jnp.zeros_like(state)

        low = sel_r[...]
        lin = mm_t(low, wstep[...]) + shift_r[...]
        lin_o[...] = lin
        dt_s[...] = softplus(lin)
        u_s[...] = dt_s[...] * act_r[...].astype(f32)
        turned = low.astype(f32).T
        in_sel, out_sel = turned[IN_AT : IN_AT + NS, :], turned[OUT_AT : OUT_AT + NS, :]
        a2 = a_r[...]

        masks = row_masks(wid)
        h = state[...]
        terms = [None] * 8
        for t in range(TIME_BLOCK):
            kept[t] = h
            h = jnp.exp2(dt_s[t : t + 1, :] * a2) * h + u_s[t : t + 1, :] * in_sel[:, t : t + 1]
            y = h * out_sel[:, t : t + 1]
            terms[t % 8] = y[:8] + y[8:]
            if t % 8 == 7:
                y_s[t - 7 : t + 1, :] = row_sums(terms, masks)
        state[...] = h
        end[...] = h
        out = y_s[...] + skip_r[...] * act_r[...].astype(f32)
        mixed[...] = out
        z = mm(n_r[...], wz[...])
        z_o[...] = z
        gated = (out * z * sigmoid(z)).astype(bf16)
        gated_o[...] = gated
        stage[i % 2] = mm(gated, wout[...]).astype(bf16)
        send_rows(stage, sems, parts, i, blocks, (i // per) ^ s_ref[0], i % per * TIME_BLOCK)

    here = lambda i, s: i
    rel = lambda i, s: ((i // per) ^ s) * per + i % per
    row = (TIME_BLOCK, wid)
    return call(
        kernel,
        blocks,
        flip,
        [
            (sel, (TIME_BLOCK, LANES), here),
            (act, row, here),
            (normed, (TIME_BLOCK, D), rel),
            (weight_z, (D, wid), None),
            (weight_step, (wid, LANES), None),
            (shift, (1, wid), None),
            (skip, (1, wid), None),
            (a2, (NS, wid), None),
            (weight_out, (wid, D), None),
        ],
        [
            ((length, wid), f32, row, here),
            ((length, wid), f32, row, here),
            ((length, NS, wid), f32, (TIME_BLOCK, NS, wid), here),
            ((NS, wid), f32, (NS, wid), None),
            ((length, wid), f32, row, here),
            ((length, wid), bf16, row, here),
            *[((length // wide, D), bf16, None, None)] * wide,
        ],
        [pltpu.VMEM((NS, wid), f32)]
        + [pltpu.VMEM(row, f32)] * 3
        + [pltpu.VMEM((2, TIME_BLOCK, D), bf16), pltpu.SemaphoreType.DMA((2,))],
        length * wid * (8 * NS + 4 * D + 2 * LANES),
        length * NS * wid,
    )


def experts(span, normed, cot, up, down, ff):
    rows = sum(p.shape[0] for p in normed[0])
    blocks = lax.axis_size("wide")
    length = rows * blocks
    cols = up.shape[1]
    share = down.shape[2]
    counts = [len(g) for g in normed]

    def kernel(s_ref, *refs):
        groups, refs = taken(refs, counts)
        ((cot_r, up_r, down_r), backs, outs), refs = taken(refs, [3, blocks, blocks])
        n_o, hid_o, both_o, dex_o, down_s, held, sems, stage, stage_sems, stage_2, stage_2_sems = refs
        i = pl.program_id(0)

        @pl.when(i == 0)
        def _():
            fetch_blocks(groups, held, sems, 0)
            for k in range(down.shape[0]):
                for e in range(EXPERTS):
                    down_s[e * ff + k * share : e * ff + (k + 1) * share, :] = down_r[k, e]

        slot = i % 2

        def sent(k):
            for buffer, sem in ((stage, stage_sems), (stage_2, stage_2_sems)):
                pltpu.make_async_copy(buffer.at[k], buffer.at[k], sem.at[k]).wait()

        @pl.when(i >= 2)
        def _():
            sent(slot)

        wait_block(held, sems, i)
        n_o[...] = held[i]
        position = (i ^ s_ref[0]) * rows + lax.broadcasted_iota(jnp.int32, (rows, 1), 0)
        cot_b = cot_r[...]
        second = cot_b[:, D : D + 1] > 0.5
        upstream = jnp.where(position < s_ref[1], cot_b[:, :D], jnp.zeros((), bf16))
        raised = mm(n_o[...], up_r[...])
        first_l, second_l = raised[:, EXPERTS * ff : EXPERTS * ff + 1], raised[:, EXPERTS * ff + 1 : EXPERTS * ff + 2]
        lead = jnp.where(second, second_l - first_l, first_l - second_l)
        gate = sigmoid(lead)
        other = sigmoid(-lead)
        pre = jnp.where(second, raised[:, ff : 2 * ff], raised[:, :ff])
        bell = (1.0 + lax.erf(pre * (1.0 / math.sqrt(2.0)))) * 0.5
        hidden = pre * bell
        slope = bell + pre * jnp.exp(-0.5 * pre * pre) * (1.0 / math.sqrt(2.0 * math.pi))
        hidden = hidden.astype(bf16)
        hid_f = hidden.astype(f32)
        both = jnp.concatenate(
            [jnp.where(second, 0.0, hid_f), jnp.where(second, hid_f, 0.0)], axis=1
        ).astype(bf16)
        hid_o[...] = both
        stage_2[slot] = (gate * mm(both, down_s[...])).astype(bf16)
        dex_o[...] = (gate * upstream.astype(f32)).astype(bf16)
        lowered = mm_t(upstream, down_s[...])
        d_hid = jnp.where(second, lowered[:, ff:], lowered[:, :ff])
        d_gate = jnp.sum(hid_f * d_hid, axis=-1, keepdims=True)
        d_pre = gate * d_hid * slope
        d_lead = gate * other * d_gate
        lane = lax.broadcasted_iota(jnp.int32, (rows, cols - EXPERTS * ff), 1)
        d_second = jnp.where(second, d_lead, -d_lead)
        d_logits = jnp.where(lane == 1, d_second, jnp.where(lane == 0, -d_second, 0.0))
        d_both = jnp.concatenate(
            [jnp.where(second, 0.0, d_pre), jnp.where(second, d_pre, 0.0), d_logits], axis=1
        ).astype(bf16)
        both_o[...] = d_both
        stage[slot] = mm_t(d_both, up_r[...]).astype(bf16)
        for k in range(blocks):

            @pl.when(i == k)
            def _(k=k):
                for buffer, sem, out in ((stage, stage_sems, backs[k]), (stage_2, stage_2_sems, outs[k])):
                    pltpu.make_async_copy(buffer.at[k % 2], out, sem.at[k % 2]).start()

        @pl.when(i == blocks - 1)
        def _():
            sent(0)
            sent(1)

    here = lambda i, s: i
    made = call(
        kernel,
        blocks,
        span,
        [
            *[(part, None, None) for group in normed for part in group],
            (cot, (rows, D + LANES), lambda i, s: i ^ s),
            (up, up.shape, None),
            (down, down.shape, None),
        ],
        [
            *[((rows, D), bf16, None, None)] * (2 * blocks),
            ((length, D), bf16, (rows, D), here),
            ((length, EXPERTS * ff), bf16, (rows, EXPERTS * ff), here),
            ((length, cols), bf16, (rows, cols), here),
            ((length, D), bf16, (rows, D), here),
        ],
        [
            pltpu.VMEM((EXPERTS * ff, D), bf16),
            pltpu.VMEM((blocks, rows, D), bf16),
            pltpu.SemaphoreType.DMA((blocks,)),
            pltpu.VMEM((2, rows, D), bf16),
            pltpu.SemaphoreType.DMA((2,)),
            pltpu.VMEM((2, rows, D), bf16),
            pltpu.SemaphoreType.DMA((2,)),
        ],
        4 * length * D * (cols + EXPERTS * ff),
        3 * length * ff,
    )
    return made[:blocks], made[blocks : 2 * blocks], made[2 * blocks :]


def back(flip, d_mix, weight_out, sel, act, proj_z, lin, mixed, kept, end, weight_step, skip, a2):
    length, wid = act.shape
    blocks = length // TIME_BLOCK
    per = blocks // lax.axis_size("wide")

    counts = [len(g) for g in d_mix]

    def kernel(s_ref, *refs):
        mix_groups, refs = taken(refs, counts)
        (
            wout, sel_r, act_r, z_r, lin_r, mixed_r, kept_r, end_r, wstep, skip_r, a_r,
            mix_o, dz_o, part, dact_o, gstep_o, da_o, dskip_o, dbias_o,
            lam_s, next_s, pb_s, pc_s, dt_s, u_s, dy_s, s1_s, s2_s, turned_s, held, sems,
        ) = refs
        place = blocks - 1 - pl.program_id(0)

        @pl.when(pl.program_id(0) == 0)
        def _():
            fetch_blocks(mix_groups, held, sems, s_ref[0])
            lam_s[...] = jnp.zeros_like(lam_s)
            next_s[...] = end_r[...]
            da_o[...] = jnp.zeros_like(da_o)
            for ref in (gstep_o, dskip_o, dbias_o):
                ref[...] = jnp.zeros_like(ref)
            turned_s[...] = jnp.zeros_like(turned_s)

        @pl.when(pl.program_id(0) % per == 0)
        def _():
            wait_block(held, sems, place // per)

        mix = held[place // per, pl.ds(pl.multiple_of(place % per * TIME_BLOCK, TIME_BLOCK), TIME_BLOCK)]
        mix_o[...] = mix
        d_gated = mm_t(mix, wout[...])
        z = z_r[...]
        s = sigmoid(z)
        dz_o[...] = (d_gated * mixed_r[...] * (s * (1.0 + z * (1.0 - s)))).astype(bf16)
        dy_s[...] = d_gated * (z * s)
        x_all = act_r[...].astype(f32)
        dskip_o[...] += jnp.sum(dy_s[...] * x_all, axis=0, keepdims=True)
        dt_s[...] = softplus(lin_r[...])
        u_s[...] = dt_s[...] * x_all
        low = sel_r[...]
        turned = low.astype(f32).T
        in_sel, out_sel = turned[IN_AT : IN_AT + NS, :], turned[OUT_AT : OUT_AT + NS, :]
        a2 = a_r[...]

        def fold(v):
            total = v[:, :LANES]
            for k in range(1, wid // LANES):
                total = total + v[:, k * LANES : (k + 1) * LANES]
            return total

        masks = row_masks(wid)
        p, after, acc = lam_s[...], next_s[...], da_o[...]
        first, second = [None] * 8, [None] * 8
        for t in range(TIME_BLOCK - 1, -1, -1):
            before = kept_r[t]
            dt_t, dy_t = dt_s[t : t + 1, :], dy_s[t : t + 1, :]
            lam = dy_t * out_sel[:, t : t + 1] + p
            p = lam * jnp.exp2(dt_t * a2)
            moved = p * before
            acc = acc + dt_t * moved
            term = lam * in_sel[:, t : t + 1]
            first[t % 8] = term[:8] + term[8:]
            term = a2 * moved
            second[t % 8] = term[:8] + term[8:]
            if t % 8 == 0:
                s1_s[t : t + 8, :] = row_sums(first, masks)
                s2_s[t : t + 8, :] = row_sums(second, masks)
            pb_s[t] = fold(lam * u_s[t : t + 1, :])
            pc_s[t] = fold(after * dy_t)
            after = before
        lam_s[...] = p
        next_s[...] = after
        da_o[...] = acc
        ones = jnp.ones((LANES, LANES), bf16)
        lane = lax.broadcasted_iota(jnp.int32, (NS, TIME_BLOCK), 1)
        for source, at in ((pb_s, IN_AT), (pc_s, OUT_AT)):
            sums = mm(source[...].reshape(TIME_BLOCK * NS, LANES).astype(bf16), ones)
            sums = sums.reshape(TIME_BLOCK, NS, LANES)
            parts = [jnp.zeros((NS, TIME_BLOCK), f32)] * 4
            for t in range(TIME_BLOCK):
                parts[t % 4] = jnp.where(lane == t, sums[t], parts[t % 4])
            turned_s[at : at + NS, :] = (parts[0] + parts[1]) + (parts[2] + parts[3])
        through = s1_s[...]
        d_step = s2_s[...] * LN2 + x_all * through
        dact_o[...] = dt_s[...] * through + skip_r[...] * dy_s[...]
        grad = d_step * sigmoid(lin_r[...])
        dbias_o[...] += jnp.sum(grad, axis=0, keepdims=True)
        grad = grad.astype(bf16)
        gstep_o[...] += t_mm(grad, low)
        part[...] = (mm(grad, wstep[...]) + turned_s[...].T).astype(bf16)

    here = lambda i, s: blocks - 1 - i
    rel = lambda i, s: (((blocks - 1 - i) // per) ^ s) * per + (blocks - 1 - i) % per
    row = (TIME_BLOCK, wid)
    one = ((1, wid), f32, (1, wid), None)
    return call(
        kernel,
        blocks,
        flip,
        [
            *[(part, None, None) for group in d_mix for part in group],
            (weight_out, (wid, D), None),
            (sel, (TIME_BLOCK, LANES), here),
            (act, row, here),
            (proj_z, row, here),
            (lin, row, here),
            (mixed, row, here),
            (kept, (TIME_BLOCK, NS, wid), here),
            (end, (NS, wid), None),
            (weight_step, (wid, LANES), None),
            (skip, (1, wid), None),
            (a2, (NS, wid), None),
        ],
        [
            ((length, D), bf16, (TIME_BLOCK, D), here),
            ((length, wid), bf16, row, rel),
            ((length, LANES), bf16, (TIME_BLOCK, LANES), here),
            ((length, wid), f32, row, here),
            ((wid, LANES), f32, (wid, LANES), None),
            ((NS, wid), f32, (NS, wid), None),
            one,
            one,
        ],
        [pltpu.VMEM((NS, wid), f32)] * 2
        + [pltpu.VMEM((TIME_BLOCK, NS, LANES), f32)] * 2
        + [pltpu.VMEM(row, f32)] * 5
        + [pltpu.VMEM((LANES, TIME_BLOCK), f32)]
        + [
            pltpu.VMEM((lax.axis_size("wide"), length // lax.axis_size("wide"), D), bf16),
            pltpu.SemaphoreType.DMA((lax.axis_size("wide"),)),
        ],
        length * wid * (20 * NS + 2 * D + 2 * LANES),
        length * NS * wid,
    )


def tail(
    flip, d_sel, d_act, conv, proj, d_z, normed, act, weight_x, weight_z, weight_sel, taps,
    grad_step, grad_flat, grad_z, grad_out, beyond, chans,
):
    length, wid = act.shape
    blocks, count = lax.axis_size("wide"), lax.axis_size("narrow")
    rows = length // blocks
    group, c_rows = D // (blocks * count), chans // count

    def kernel(
        s_ref, sel_r, dact_r, conv_r, proj_r, dz_r, n_r, act_r, wx, wz, wsel, taps_r, gstep_r, flat_r,
        gz_r, gout_r, *refs,
    ):
        (parts, packs), refs = taken(refs, [blocks, count])
        gx_o, ext, gx, gsel, flat, held, stage, sems = refs
        i = pl.program_id(0)

        send_ready(stage, sems, i)

        @pl.when(pl.program_id(0) == 0)
        def _():
            ext[rows:, :] = jnp.zeros((8, wid), f32)
            gx[...] = jnp.zeros_like(gx)
            gsel[...] = jnp.zeros_like(gsel)
            flat[...] = flat_r[...]

        low = sel_r[...]
        c = conv_r[...]
        q = sigmoid(c)
        d_conv = (mm_t(low, wsel[...]) + dact_r[...]) * (q * (1.0 + c * (1.0 - q)))
        ext[:rows, :] = d_conv
        flat[CONV : CONV + 1, :] += jnp.sum(d_conv, axis=0, keepdims=True)
        x = proj_r[...]
        d_x = jnp.zeros((rows, wid), f32)
        for k in range(CONV):
            moved = ext[CONV - 1 - k : CONV - 1 - k + rows, :]
            d_x = d_x + taps_r[k : k + 1, :] * moved
            flat[k : k + 1, :] += jnp.sum(moved * x, axis=0, keepdims=True)
        ext[rows:, :] = d_conv[:8, :]
        d_x = d_x.astype(bf16)
        stage[i % 2] = (mm_t(d_x, wx[...]) + mm_t(dz_r[...], wz[...])).astype(bf16)
        gx[...] += t_mm(n_r[...], d_x)
        gsel[...] += t_mm(act_r[...], low)
        send_rows(stage, sems, parts, i, blocks, (blocks - 1 - i) ^ s_ref[0], 0)

        @pl.when(pl.program_id(0) == blocks - 1)
        def _():
            for k in range(blocks * count):
                x = gx[k * group : (k + 1) * group, :chans]
                gx_o[k] = jnp.concatenate([x, gz_r[k].astype(f32)], axis=1).astype(bf16)
            tall = jnp.concatenate(
                [jnp.zeros((DT_RANK, wid), f32), flat[...], jnp.zeros((LANES - DT_RANK - FLAT, wid), f32)], axis=0
            )
            lane = lax.broadcasted_iota(jnp.int32, (wid, LANES), 1)
            left = jnp.where(lane < DT_RANK, gstep_r[...], tall.T)
            held[:, :LANES] = left
            held[:, LANES:] = gsel[...]
            for k, out in enumerate(packs):
                if c_rows % 8 == 0:
                    at = pl.multiple_of(s_ref[1 + k] * c_rows, 8)
                    out[:, :D] = gout_r[pl.ds(at, c_rows), :].astype(bf16)
                    out[:, D:] = held[pl.ds(at, c_rows), :].astype(bf16)
                    continue
                for p in range(count):

                    @pl.when(s_ref[1 + k] == p)
                    def _(out=out, at=p * c_rows):
                        out[:, :D] = gout_r[at : at + c_rows, :].astype(bf16)
                        out[:, D:] = held[at : at + c_rows, :].astype(bf16)

    here = lambda i, s: blocks - 1 - i
    rel = lambda i, s: (blocks - 1 - i) ^ s
    row = (rows, wid)
    pack = (c_rows, D + 2 * LANES)
    sent = (blocks * count, group, 2 * chans)
    return call(
        kernel,
        blocks,
        jnp.concatenate([flip, beyond]),
        [
            (d_sel, (rows, LANES), here),
            (d_act, row, here),
            (conv, row, here),
            (proj, row, here),
            (d_z, row, rel),
            (normed, (rows, D), rel),
            (act, row, here),
            (weight_x, (D, wid), None),
            (weight_z, (D, wid), None),
            (weight_sel, (wid, LANES), None),
            (taps, (CONV, wid), None),
            (grad_step, (wid, LANES), None),
            (grad_flat, (FLAT, wid), None),
            (grad_z, grad_z.shape, None),
            (grad_out, (wid, D), None),
        ],
        [*[((rows, D), bf16, None, None)] * blocks, *[(pack, bf16, pack, None)] * count, (sent, bf16, sent, None)],
        [
            pltpu.VMEM((rows + 8, wid), f32),
            pltpu.VMEM((D, wid), f32),
            pltpu.VMEM((wid, LANES), f32),
            pltpu.VMEM((FLAT, wid), f32),
            pltpu.VMEM((wid, 2 * LANES), f32),
            pltpu.VMEM((2, rows, D), bf16),
            pltpu.SemaphoreType.DMA((2,)),
        ],
        2 * length * wid * (3 * D + 2 * LANES),
    )


def row_grad(flip, a, b, cols, group, along):
    narrow = lax.axis_size("narrow")
    length, total = a.shape
    n = b.shape[1]
    blocks = lax.axis_size("wide")
    rows = length // blocks

    def kernel(s_ref, a_r, b_r, out, acc):
        @pl.when(pl.program_id(0) == 0)
        def _():
            acc[...] = jnp.zeros_like(acc)

        acc[...] += t_mm(a_r[...], b_r[...])

        @pl.when(pl.program_id(0) == blocks - 1)
        def _():
            for k in range(total // group):
                at = k % narrow * blocks + k // narrow if along else k
                out[at] = acc[k * group : (k + 1) * group, :cols].astype(bf16)

    here = lambda i, s: i
    return call(
        kernel,
        blocks,
        flip,
        [(a, (rows, total), here), (b, (rows, n), here)],
        [((total // group, group, cols), bf16, (total // group, group, cols), None)],
        [pltpu.VMEM((total, n), f32)],
        2 * length * total * n,
    )[0]


def joined(got):
    wide, narrow, rows, cols = got.shape
    half = cols // 2

    def kernel(got_r, out):
        parts = [sum(got_r[w, k].astype(f32) for k in range(narrow)) for w in range(wide)]
        out[:, : wide * half] = jnp.concatenate([p[:, :half] for p in parts], axis=1)
        out[:, wide * half :] = jnp.concatenate([p[:, half:] for p in parts], axis=1)

    vmem = pl.BlockSpec(memory_space=pltpu.VMEM)
    return pl.pallas_call(
        kernel,
        in_specs=[vmem],
        out_specs=vmem,
        out_shape=jax.ShapeDtypeStruct((rows, wide * cols), f32),
        compiler_params=pltpu.CompilerParams(vmem_limit_bytes=VMEM),
    )(got)


def norm_backward(values, inverse, gain_vec, upstream):
    scaled = upstream * gain_vec
    inner_mean = jnp.mean(values * scaled, axis=-1, keepdims=True)
    return inverse * scaled - values * (inverse * inverse * inverse) * inner_mean


def local(
    tokens,
    mixer_gain,
    in_weight,
    conv_weight,
    conv_bias,
    select_weight,
    step_weight,
    step_bias,
    decay_log,
    skip_weight,
    out_weight,
    expert_gain,
    router_weight,
    up_weight,
    down_weight,
    routes,
    lengths,
    cotangent,
):
    wide, narrow = lax.axis_size("wide"), lax.axis_size("narrow")
    w = lax.axis_index("wide")
    rows = tokens.shape[1]
    chans = DI // wide
    wid = -(-chans // LANES) * LANES
    ff = FF // wide
    d_rows = D // (wide * narrow)
    c_rows = DI // (wide * narrow)
    f_rows = FF // (wide * narrow)
    both = EXPERTS * ff
    flip = w if relative() else 0 * w
    span = jnp.stack([flip, lengths[0]]).astype(jnp.int32)

    tokens_own = tokens[0].astype(f32)

    in_parts = in_weight.reshape(d_rows, 2, wide, chans).transpose(1, 2, 0, 3)
    gains = jnp.stack([mixer_gain, expert_gain], axis=1)
    gains = jnp.broadcast_to(gains[None], (wide, d_rows, 2))
    zero_col = jnp.zeros((c_rows, 1), bf16)
    channel_pack = jnp.concatenate(
        [
            conv_weight.T,
            conv_bias[:, None],
            step_bias[:, None],
            skip_weight[:, None],
            zero_col,
            decay_log.T,
            step_weight.T,
            select_weight,
        ],
        axis=1,
    )
    pack_cols = channel_pack.shape[1]
    wide_cols = -(-pack_cols // LANES) * LANES
    channel_pack = pad_to(channel_pack, 1, wide_cols)
    x_parts = jnp.concatenate([in_parts[0], gains], axis=2)
    tokens_all, channel_pack = gather_wide(tokens[0], lambda block: turns(channel_pack))
    x_full = gather_rows(after(x_parts, channel_pack))
    x_full, tokens_all = lax.optimization_barrier((x_full, tokens_all))
    weight_x = pad_to(x_full[:, :chans], 1, wid)
    gains = x_full[:, chans:].T.astype(f32)
    gain_one, gain_two = gains[:1], gains[1:]
    up_parts = up_weight.reshape(EXPERTS, d_rows, wide, ff).transpose(2, 1, 0, 3)
    up_parts = up_parts.reshape(wide, d_rows, both)
    router_parts = jnp.broadcast_to(router_weight[None], (wide, d_rows, EXPERTS))
    up_parts = jnp.concatenate([up_parts, router_parts, in_parts[1]], axis=2)
    up_parts = lax.all_to_all(after(up_parts, x_full), "wide", 0, 0)
    up_parts = up_parts.reshape(wide * d_rows, both + EXPERTS + chans)
    route_cols = jnp.broadcast_to(routes[0].astype(bf16)[:, None], (rows, LANES))
    cot_ext = jnp.concatenate([cotangent[0], route_cols], axis=1)
    cot_all = lax.all_gather(after(cot_ext, tokens_all), "wide", axis=0, tiled=True)
    (packed,) = gather_channels(channel_pack, (wide_cols,), wid)
    flat = packed[:, :FLAT].T.astype(f32)
    taps = flat[:CONV]
    conv_shift, step_shift, skip = (flat[CONV + k : CONV + k + 1] for k in range(3))
    a_neg = -jnp.exp(flat[CONV + 4 :])
    a2 = a_neg * (1.0 / LN2)
    weight_step = pad_to(packed[:, FLAT : FLAT + DT_RANK], 1, LANES)
    weight_sel = pad_to(packed[:, FLAT + DT_RANK : pack_cols], 1, LANES)

    normed, proj_x, conv_sum, conv_act, sel_part = front(
        flip[None], tokens_all, gain_one, weight_x, taps, conv_shift, weight_sel
    )
    out_pieces = turns(after(out_weight, x_full))
    sel_part, up_parts, out_pieces = lax.optimization_barrier((sel_part, up_parts, out_pieces))
    z_pieces = turns(up_parts[:, both + EXPERTS :])
    up_parts = up_parts[:, : both + EXPERTS]
    selected, (z_pieces, weight_out) = reduce_wide(
        sel_part, lambda low: (z_pieces, gather_channels(out_pieces, (D,), wid)[0])
    )
    weight_z = ordered_rows(z_pieces, d_rows, wid)

    up_cols = -(-(both + EXPERTS) // LANES) * LANES
    up_pieces = turns(after(up_parts, selected, out_pieces))
    valid_own = (w * rows + jnp.arange(rows))[:, None] < lengths[0]
    upstream = jnp.where(valid_own, cotangent[0].astype(f32), 0.0)

    proj_z, step_lin, kept, end, mixed, gated, *mix_part = middle(
        flip[None], selected, conv_act, normed, weight_z, weight_step, step_shift, skip, a2, weight_out
    )
    mix_part, up_pieces = lax.optimization_barrier((mix_part, up_pieces))
    down_full = lax.all_gather(after(down_weight, cot_all, *up_pieces), "narrow")
    up_full = ordered_rows(up_pieces, d_rows, up_cols)
    mixer_sum, up_full = scatter_wide(mix_part, up_full, True)
    hidden_one = tokens_own + mixer_sum
    inverse_two = lax.rsqrt(jnp.mean(hidden_one * hidden_one, axis=-1, keepdims=True) + EPSILON)
    own = (hidden_one * inverse_two * gain_two).astype(bf16)

    pieces, _ = gather_wide(own)
    back_parts, out_parts, made = experts(span, pieces, cot_all, up_full, down_full, ff)
    normed_two, hidden_both, d_both, d_expert = made

    def beside(hop):
        hidden = after(hidden_both, hop)
        grad = t_mm(hidden, d_expert).astype(bf16)
        grad = grad.reshape(EXPERTS, narrow, f_rows, D).transpose(1, 0, 2, 3)
        return grad

    d_normed_two, grad_down = scatter_wide(back_parts, beside, True)
    grad_down = lax.psum_scatter(grad_down, "narrow", scatter_dimension=0)
    d_hidden_one = upstream + norm_backward(hidden_one, inverse_two, gain_two, d_normed_two)
    d_low = d_hidden_one.astype(bf16)
    def output_sums(hop):
        outs = after(out_parts, hop)
        if not relative():
            return outs
        pair = lambda q: outs[2 * q].astype(f32) + swap(outs[2 * q + 1], 1).astype(f32)
        return [pair(q).astype(bf16) for q in range(4)]

    d_mix, (grad_up, out_sums) = gather_wide(
        d_low,
        lambda low: row_grad(flip[None], normed_two, after(d_both, low), both + EXPERTS, d_rows, True),
        output_sums,
    )
    grad_up = lax.psum_scatter(
        after(grad_up, d_mix).reshape(narrow, wide, d_rows, both + EXPERTS), "narrow", scatter_dimension=0
    )
    if relative():
        sent = after(out_sums, d_mix)
        out_got = [swap(sent[q], 2 * q) for q in (1, 2, 3)]
    else:
        out_got = []

    d_mix_all, d_z, d_sel_part, d_act, grad_step, d_a, grad_skip, grad_step_bias = back(
        flip[None], d_mix, weight_out, selected, conv_act, proj_z, step_lin, mixed, kept, end,
        weight_step, skip, a2,
    )

    d_sel_part, out_got = lax.optimization_barrier((d_sel_part, out_got))

    def meanwhile(low):
        grad_out = t_mm(after(gated, low), d_mix_all)
        return grad_out, row_grad(flip[None], after(normed, low), d_z, chans, d_rows, False)

    d_sel, (grad_out, grad_z) = reduce_wide(d_sel_part, meanwhile)
    z = lax.axis_index("narrow")
    beyond = jnp.stack([(z + k) % narrow for k in range(narrow)]).astype(jnp.int32)
    grad_flat = jnp.concatenate(
        [jnp.zeros((CONV + 1, wid), f32), grad_step_bias, grad_skip, jnp.zeros((1, wid), f32), d_a * a_neg],
        axis=0,
    )
    grad_up = lax.all_to_all(after(grad_up, d_sel), "wide", 0, 0)
    made = tail(
        flip[None], d_sel, d_act, conv_sum, proj_x, d_z, normed, conv_act, weight_x, weight_z,
        weight_sel, taps, grad_step, grad_flat, grad_z, grad_out, beyond, chans,
    )
    in_part, channel_grads, grad_in = made[:wide], made[wide:-1], made[-1]
    in_part, grad_up = lax.optimization_barrier((in_part, grad_up))
    grad_in = scatter_rows(grad_in)

    def beside(hop):
        up, down = lax.optimization_barrier((grad_up, grad_down, hop))[:2]
        up = up.astype(f32)
        router = jnp.sum(up[:, :, both:], axis=0)
        up = up[:, :, :both].reshape(wide, d_rows, EXPERTS, ff)
        up = up.transpose(2, 1, 0, 3).reshape(EXPERTS, d_rows, FF)
        gain = (
            jnp.sum(up_weight.astype(f32) * up, axis=(0, 2))
            + jnp.sum(router_weight.astype(f32) * router, axis=1)
        ) / expert_gain.astype(f32)
        if relative():
            out = sum(p.astype(f32) for p in lax.optimization_barrier(([out_sums[0], *out_got], hop))[0])
        else:
            out, _ = scatter_wide(out_sums)
        return up, router, gain, down.astype(f32), out, turned(channel_grads)

    d_normed, made = scatter_wide(in_part, beside)
    channel_grads = made[-1]
    made = made[:-1]
    grad_up, grad_router, grad_gain_two, grad_down, expert_sum = made
    d_normed, grad_in = lax.optimization_barrier((d_normed, grad_in))
    channel_grads = sum(p.astype(f32) for p in channel_grads)
    grad_out, channel_grads = channel_grads[:, :D], channel_grads[:, D:]
    inverse_one = lax.rsqrt(jnp.mean(tokens_own * tokens_own, axis=-1, keepdims=True) + EPSILON)
    token_grad = d_hidden_one + norm_backward(tokens_own, inverse_one, gain_one, d_normed)
    output = (hidden_one + expert_sum).astype(bf16)

    grad_in = joined(grad_in)
    grad_gain_one = jnp.sum(in_weight.astype(f32) * grad_in, axis=1) / mixer_gain.astype(f32)
    flat_grads = channel_grads[:, DT_RANK : DT_RANK + FLAT].T
    return (
        output[None],
        token_grad[None],
        grad_gain_one,
        grad_in,
        flat_grads[:CONV],
        flat_grads[CONV],
        channel_grads[:, LANES : LANES + DT_RANK + 2 * NS],
        channel_grads[:, :DT_RANK].T,
        flat_grads[CONV + 1],
        flat_grads[CONV + 4 :],
        flat_grads[CONV + 2],
        grad_out,
        grad_gain_two,
        grad_router,
        grad_up,
        grad_down,
    )


def solution(mesh):
    both = ("wide", "narrow")
    return jax.shard_map(
        local,
        mesh=mesh,
        in_specs=(
            P("narrow", "wide", None),
            P(both),
            P(both, None),
            P(None, both),
            P(both),
            P(both, None),
            P(None, both),
            P(both),
            P(None, both),
            P(both),
            P(both, None),
            P(both),
            P(both, None),
            P(None, both, None),
            P(None, both, None),
            P("narrow", "wide"),
            P("narrow"),
            P("narrow", "wide", None),
        ),
        out_specs=(
            P("narrow", "wide", None),
            P("narrow", "wide", None),
            P(both),
            P(both, None),
            P(None, both),
            P(both),
            P(both, None),
            P(None, both),
            P(both),
            P(None, both),
            P(both),
            P(both, None),
            P(both),
            P(both, None),
            P(None, both, None),
            P(None, both, None),
        ),
        check_vma=False,
    )
```

```python
import math

import jax
import jax.numpy as jnp
from jax import lax
from jax.experimental import pallas as pl
from jax.experimental.pallas import tpu as pltpu
from jax.sharding import PartitionSpec as P

D = 1152
DI = 2304
NS = 16
DT_RANK = 72
CONV = 4
FF = 3072
EXPERTS = 2
EPSILON = 1e-05
TIME_BLOCK = 128
VMEM = 60 * 2**20
LANES = 128
LN2 = math.log(2.0)

f32 = jnp.float32
bf16 = jnp.bfloat16


def relative():
    return lax.axis_size("wide") == 8


def swap(x, k):
    n = lax.axis_size("wide")
    return lax.ppermute(x, "wide", [(i, i ^ k) for i in range(n)])


def turn(x, k):
    n = lax.axis_size("narrow")
    return lax.ppermute(x, "narrow", [(i, (i + k) % n) for i in range(n)])


def pick(x, i, axis=0):
    return lax.dynamic_index_in_dim(x, i, axis, False)


def blocks_of(x):
    return [[b] for b in jnp.split(x, lax.axis_size("wide"), axis=0)]


def gather_wide(block, meanwhile=None, second=None):
    if not relative():
        made = meanwhile(block) if meanwhile else ()
        made = (made, second(block)) if second else made
        return blocks_of(lax.all_gather(block, "wide", axis=0, tiled=True)), made
    half = block.shape[0] // 2
    mate = swap(block, 1)
    a, b = swap(block, 2), swap(block, 4)
    made = ()
    if meanwhile:
        made = meanwhile(block)
        a, b, made = lax.optimization_barrier((a, b, made))
    c0, c1 = swap(a[:half], 4), swap(b[half:], 2)
    if second:
        c0, c1, late = lax.optimization_barrier((c0, c1, second(a)))
        made = (made, late)
    out = [[block], [mate], [a], [swap(a, 1)], [b], [swap(b, 1)], [c0, c1], [swap(c0, 1), swap(c1, 1)]]
    return out, made


def scatter_wide(parts, beside=(), eager=False):
    if not relative():
        whole = jnp.concatenate(parts, axis=0)
        total = lax.psum_scatter(whole, "wide", scatter_dimension=0, tiled=True).astype(f32)
        return total, beside(total) if callable(beside) else beside
    half = parts[0].shape[0] // 2

    def summed(q):
        return parts[2 * q].astype(f32) + swap(parts[2 * q + 1], 1).astype(f32)

    far = summed(3).astype(bf16)
    r0, r1 = swap(far[:half], 2), swap(far[half:], 4)
    sx, sy = summed(1), summed(2)
    x0, y1 = swap(sx[:half].astype(bf16), 2), swap(sy[half:].astype(bf16), 4)
    if eager:
        r0, r1, x0, y1 = lax.optimization_barrier((r0, r1, x0, y1))
    x1 = swap((sx[half:] + r1.astype(f32)).astype(bf16), 2)
    y0 = swap((sy[:half] + r0.astype(f32)).astype(bf16), 4)
    x1, y0, beside = lax.optimization_barrier((x1, y0, beside(r0) if callable(beside) else beside))
    x = jnp.concatenate([x0, x1], axis=0).astype(f32)
    y = jnp.concatenate([y0, y1], axis=0).astype(f32)
    return summed(0) + x + y, beside


def reduce_wide(partial, meanwhile):
    if not relative():
        return lax.psum(partial, "wide"), meanwhile(partial)
    core = lax.axis_index("wide") % 2
    half = partial.shape[0] // 2
    parts = partial.reshape(2, half, partial.shape[1])
    total = pick(parts, core).astype(f32) + swap(pick(parts, 1 - core), 1).astype(f32)
    low = total.astype(bf16)
    got = [swap(low, 2), swap(low, 4), swap(low, 6)]
    got, made = lax.optimization_barrier((got, meanwhile(low)))
    total = total + sum(p.astype(f32) for p in got)
    low = total.astype(bf16)
    mate = swap(low, 1)
    first = core == 0
    out = jnp.concatenate([jnp.where(first, low, mate), jnp.where(first, mate, low)], axis=0)
    return out, made


def after(x, *others):
    return lax.optimization_barrier((x,) + others)[0]


def turns(x):
    return [x] + [turn(x, k) for k in range(1, lax.axis_size("narrow"))]


def pad_to(x, axis, size):
    pads = [(0, 0)] * x.ndim
    pads[axis] = (0, size - x.shape[axis])
    return jnp.pad(x, pads)


def ordered_rows(pieces, group, cols):
    n, z = lax.axis_size("narrow"), lax.axis_index("narrow")
    rows, width = pieces[0].shape
    order = jnp.stack([(z - k) % n * group for k in range(n)]).astype(jnp.int32)

    def kernel(order_ref, *refs):
        out = refs[n]
        r = lax.broadcasted_iota(jnp.int32, (n * rows, rows), 0)
        j = lax.broadcasted_iota(jnp.int32, (n * rows, rows), 1)
        spot = j
        for i in range(1, rows // group):
            spot = spot + jnp.where(j >= i * group, (n - 1) * group, 0)
        value = jnp.zeros((n * rows, width), f32)
        for k in range(n):
            spots = jnp.where(r == spot + order_ref[k], 1.0, 0.0).astype(bf16)
            value = value + jnp.dot(spots, refs[k][...], preferred_element_type=f32)
        out[...] = jnp.zeros(out.shape, bf16)
        out[:, :width] = value.astype(bf16)

    vmem = pl.BlockSpec(memory_space=pltpu.VMEM)
    return pl.pallas_call(
        kernel,
        in_specs=[pl.BlockSpec(memory_space=pltpu.SMEM)] + [vmem] * n,
        out_specs=vmem,
        out_shape=jax.ShapeDtypeStruct((n * rows, cols), bf16),
        compiler_params=pltpu.CompilerParams(vmem_limit_bytes=VMEM),
    )(order, *pieces)


def gather_channels(pieces, splits, total):
    n, z = lax.axis_size("narrow"), lax.axis_index("narrow")
    rows, cols = pieces[0].shape
    order = jnp.stack([(z - k) % n * rows for k in range(n)]).astype(jnp.int32)

    def kernel(order_ref, *refs):
        value = jnp.zeros((total, cols), f32)
        r = lax.broadcasted_iota(jnp.int32, (total, rows), 0)
        j = lax.broadcasted_iota(jnp.int32, (total, rows), 1)
        for k in range(n):
            spots = jnp.where(r == j + order_ref[k], 1.0, 0.0).astype(bf16)
            value = value + jnp.dot(spots, refs[k][...], preferred_element_type=f32)
        value = value.astype(bf16)
        at = 0
        for out in refs[n:]:
            out[...] = value[:, at : at + out.shape[1]]
            at += out.shape[1]

    vmem = pl.BlockSpec(memory_space=pltpu.VMEM)
    return pl.pallas_call(
        kernel,
        in_specs=[pl.BlockSpec(memory_space=pltpu.SMEM)] + [vmem] * n,
        out_specs=[vmem] * len(splits),
        out_shape=[jax.ShapeDtypeStruct((total, c), bf16) for c in splits],
        compiler_params=pltpu.CompilerParams(vmem_limit_bytes=VMEM),
    )(order, *pieces)


def turns(x):
    return [x] + [turn(x, k) for k in range(1, lax.axis_size("narrow"))]


def turned(pieces):
    return [pieces[0]] + [turn(pieces[k], k) for k in range(1, len(pieces))]


def split_narrow(x, axis):
    n, z = lax.axis_size("narrow"), lax.axis_index("narrow")
    return [pick(x, (z + k) % n, axis) for k in range(n)]


def exchange(x):
    return lax.all_to_all(x, ("wide", "narrow"), 0, 0)


def gather_rows(parts):
    wide, rows, cols = parts.shape
    narrow = lax.axis_size("narrow")
    parts = jnp.broadcast_to(parts[:, None], (wide, narrow, rows, cols))
    got = exchange(parts.reshape(wide * narrow, rows, cols))
    return got.reshape(wide * narrow * rows, cols)


def scatter_rows(grad):
    got = exchange(grad)
    return got.reshape(lax.axis_size("wide"), lax.axis_size("narrow"), *grad.shape[1:])


def summed_rows(got):
    return sum(got[:, k].astype(f32) for k in range(got.shape[1]))


def mm(a, b):
    return jnp.dot(a, b, preferred_element_type=f32)


def mm_t(a, b):
    return lax.dot_general(a, b, (((1,), (1,)), ((), ())), preferred_element_type=f32)


def t_mm(a, b):
    return lax.dot_general(a, b, (((0,), (0,)), ((), ())), preferred_element_type=f32)


def sigmoid(v):
    return 1.0 / (1.0 + jnp.exp(-v))


def softplus(v):
    return jnp.maximum(v, 0.0) + jnp.log1p(jnp.exp(-jnp.abs(v)))


def call(kernel, grid, flip, ins, outs, scratch, flops, exps=0, aliases={}):
    def spec(block, where):
        if block is None:
            return pl.BlockSpec(memory_space=pltpu.HBM)
        if where is None:
            zeros = (0,) * len(block)
            return pl.BlockSpec(block, lambda i, s: zeros)
        return pl.BlockSpec(block, lambda i, s: (where(i, s[0]),) + (0,) * (len(block) - 1))

    size = sum(a.size * a.dtype.itemsize for a, _, _ in ins)
    size += sum(math.prod(o[0]) * jnp.dtype(o[1]).itemsize for o in outs)
    return pl.pallas_call(
        kernel,
        grid_spec=pltpu.PrefetchScalarGridSpec(
            num_scalar_prefetch=1,
            grid=(grid,),
            in_specs=[spec(b, f) for _, b, f in ins],
            out_specs=[spec(b, f) for _, _, b, f in outs],
            scratch_shapes=scratch,
        ),
        out_shape=[jax.ShapeDtypeStruct(o[0], o[1]) for o in outs],
        input_output_aliases=aliases,
        compiler_params=pltpu.CompilerParams(vmem_limit_bytes=VMEM),
        cost_estimate=pl.CostEstimate(flops=flops // 64, bytes_accessed=size // 64, transcendentals=0),
    )(flip, *[a for a, _, _ in ins])


def fetch_blocks(groups, held, sems, shift):
    for k, group in enumerate(groups):
        at = 0
        for ref in group:
            n = ref.shape[0]
            pltpu.make_async_copy(ref, held.at[k ^ shift, pl.ds(at, n)], sems.at[k ^ shift]).start()
            at += n


def wait_block(held, sems, i):
    pltpu.make_async_copy(held.at[i], held.at[i], sems.at[i]).wait()


def send_ready(stage, sems, step):
    @pl.when(step >= 2)
    def _():
        pltpu.make_async_copy(stage.at[step % 2], stage.at[step % 2], sems.at[step % 2]).wait()


def send_rows(stage, sems, outs, step, steps, block, at):
    slot = step % 2
    for k, out in enumerate(outs):

        @pl.when(block == k)
        def _(out=out):
            part = out.at[pl.ds(at, stage.shape[1])]
            pltpu.make_async_copy(stage.at[slot], part, sems.at[slot]).start()

    @pl.when(step == steps - 1)
    def _():
        for k in range(2):
            pltpu.make_async_copy(stage.at[k], stage.at[k], sems.at[k]).wait()


def taken(refs, lengths):
    out, at = [], 0
    for n in lengths:
        out.append(refs[at : at + n])
        at += n
    return out, refs[at:]


def front(flip, tokens, gain, weight_x, taps, shift, weight_sel):
    wid = weight_x.shape[1]
    blocks = lax.axis_size("wide")
    rows = tokens[0][0].shape[0]
    length = rows * blocks
    counts = [len(g) for g in tokens]

    def kernel(s_ref, *refs):
        groups, refs = taken(refs, counts)
        gain_r, wx, taps_r, shift_r, wsel, normed, proj, conv, act, part, pad, held, sems = refs
        i = pl.program_id(0)

        @pl.when(i == 0)
        def _():
            fetch_blocks(groups, held, sems, s_ref[0])
            pad[:8, :] = jnp.zeros((8, wid), f32)

        wait_block(held, sems, i)
        values = held[i].astype(f32)
        inverse = lax.rsqrt(jnp.mean(values * values, axis=-1, keepdims=True) + EPSILON)
        low = (values * inverse * gain_r[...]).astype(bf16)
        normed[...] = low
        x = mm(low, wx[...])
        proj[...] = x
        pad[8:, :] = x
        total = shift_r[...] + taps_r[CONV - 1 : CONV, :] * x
        for k in range(CONV - 1):
            start = 8 - (CONV - 1) + k
            total = total + taps_r[k : k + 1, :] * pad[start : start + rows, :]
        pad[:8, :] = x[rows - 8 :, :]
        conv[...] = total
        low = (total * sigmoid(total)).astype(bf16)
        act[...] = low
        part[...] = mm(low, wsel[...]).astype(bf16)

    here = lambda i, s: i
    rel = lambda i, s: i ^ s
    return call(
        kernel,
        blocks,
        flip,
        [
            *[(part, None, None) for group in tokens for part in group],
            (gain, (1, D), None),
            (weight_x, (D, wid), None),
            (taps, (CONV, wid), None),
            (shift, (1, wid), None),
            (weight_sel, (wid, LANES), None),
        ],
        [
            ((length, D), bf16, (rows, D), rel),
            ((length, wid), f32, (rows, wid), here),
            ((length, wid), f32, (rows, wid), here),
            ((length, wid), bf16, (rows, wid), here),
            ((length, LANES), bf16, (rows, LANES), here),
        ],
        [
            pltpu.VMEM((rows + 8, wid), f32),
            pltpu.VMEM((blocks, rows, D), bf16),
            pltpu.SemaphoreType.DMA((blocks,)),
        ],
        2 * length * wid * (D + LANES),
    )


FLAT = CONV + 4 + NS
def row_sums(terms, masks):
    high, mid, low = masks
    c = [
        jnp.where(high, terms[i + 4], terms[i])
        + pltpu.roll(jnp.where(high, terms[i], terms[i + 4]), 4, 0)
        for i in range(4)
    ]
    c = [
        jnp.where(mid, c[i + 2] + pltpu.roll(c[i + 2], 2, 0), c[i] + pltpu.roll(c[i], 6, 0))
        for i in range(2)
    ]
    return jnp.where(low, c[1] + pltpu.roll(c[1], 1, 0), c[0] + pltpu.roll(c[0], 7, 0))


def row_masks(wid):
    row = lax.broadcasted_iota(jnp.int32, (8, wid), 0)
    return row >= 4, (row & 2) > 0, (row & 1) > 0


IN_AT = DT_RANK
OUT_AT = DT_RANK + NS


def middle(flip, sel, act, normed, weight_z, weight_step, shift, skip, a2, weight_out):
    length, wid = act.shape
    blocks = length // TIME_BLOCK
    per = blocks // lax.axis_size("wide")

    wide = lax.axis_size("wide")

    def kernel(
        s_ref, sel_r, act_r, n_r, wz, wstep, shift_r, skip_r, a_r, wout, z_o, lin_o, kept, end, mixed, gated_o, *refs
    ):
        (parts,), refs = taken(refs, [wide])
        state, dt_s, u_s, y_s, stage, sems = refs
        i = pl.program_id(0)

        send_ready(stage, sems, i)

        @pl.when(i == 0)
        def _():
            state[...] = jnp.zeros_like(state)

        low = sel_r[...]
        lin = mm_t(low, wstep[...]) + shift_r[...]
        lin_o[...] = lin
        dt_s[...] = softplus(lin)
        u_s[...] = dt_s[...] * act_r[...].astype(f32)
        turned = low.astype(f32).T
        in_sel, out_sel = turned[IN_AT : IN_AT + NS, :], turned[OUT_AT : OUT_AT + NS, :]
        a2 = a_r[...]

        masks = row_masks(wid)
        h = state[...]
        terms = [None] * 8
        for t in range(TIME_BLOCK):
            kept[t] = h
            h = jnp.exp2(dt_s[t : t + 1, :] * a2) * h + u_s[t : t + 1, :] * in_sel[:, t : t + 1]
            y = h * out_sel[:, t : t + 1]
            terms[t % 8] = y[:8] + y[8:]
            if t % 8 == 7:
                y_s[t - 7 : t + 1, :] = row_sums(terms, masks)
        state[...] = h
        end[...] = h
        out = y_s[...] + skip_r[...] * act_r[...].astype(f32)
        mixed[...] = out
        z = mm(n_r[...], wz[...])
        z_o[...] = z
        gated = (out * z * sigmoid(z)).astype(bf16)
        gated_o[...] = gated
        stage[i % 2] = mm(gated, wout[...]).astype(bf16)
        send_rows(stage, sems, parts, i, blocks, (i // per) ^ s_ref[0], i % per * TIME_BLOCK)

    here = lambda i, s: i
    rel = lambda i, s: ((i // per) ^ s) * per + i % per
    row = (TIME_BLOCK, wid)
    return call(
        kernel,
        blocks,
        flip,
        [
            (sel, (TIME_BLOCK, LANES), here),
            (act, row, here),
            (normed, (TIME_BLOCK, D), rel),
            (weight_z, (D, wid), None),
            (weight_step, (wid, LANES), None),
            (shift, (1, wid), None),
            (skip, (1, wid), None),
            (a2, (NS, wid), None),
            (weight_out, (wid, D), None),
        ],
        [
            ((length, wid), f32, row, here),
            ((length, wid), f32, row, here),
            ((length, NS, wid), f32, (TIME_BLOCK, NS, wid), here),
            ((NS, wid), f32, (NS, wid), None),
            ((length, wid), f32, row, here),
            ((length, wid), bf16, row, here),
            *[((length // wide, D), bf16, None, None)] * wide,
        ],
        [pltpu.VMEM((NS, wid), f32)]
        + [pltpu.VMEM(row, f32)] * 3
        + [pltpu.VMEM((2, TIME_BLOCK, D), bf16), pltpu.SemaphoreType.DMA((2,))],
        length * wid * (8 * NS + 4 * D + 2 * LANES),
        length * NS * wid,
    )


def experts(span, normed, cot, up, down, ff):
    rows = sum(p.shape[0] for p in normed[0])
    blocks = lax.axis_size("wide")
    length = rows * blocks
    cols = up.shape[1]
    share = down.shape[2]
    counts = [len(g) for g in normed]

    def kernel(s_ref, *refs):
        groups, refs = taken(refs, counts)
        ((cot_r, up_r, down_r), backs, outs), refs = taken(refs, [3, blocks, blocks])
        n_o, hid_o, both_o, dex_o, down_s, held, sems, stage, stage_sems, stage_2, stage_2_sems = refs
        i = pl.program_id(0)

        @pl.when(i == 0)
        def _():
            fetch_blocks(groups, held, sems, 0)
            for k in range(down.shape[0]):
                for e in range(EXPERTS):
                    down_s[e * ff + k * share : e * ff + (k + 1) * share, :] = down_r[k, e]

        slot = i % 2

        def sent(k):
            for buffer, sem in ((stage, stage_sems), (stage_2, stage_2_sems)):
                pltpu.make_async_copy(buffer.at[k], buffer.at[k], sem.at[k]).wait()

        @pl.when(i >= 2)
        def _():
            sent(slot)

        wait_block(held, sems, i)
        n_o[...] = held[i]
        position = (i ^ s_ref[0]) * rows + lax.broadcasted_iota(jnp.int32, (rows, 1), 0)
        cot_b = cot_r[...]
        second = cot_b[:, D : D + 1] > 0.5
        upstream = jnp.where(position < s_ref[1], cot_b[:, :D], jnp.zeros((), bf16))
        raised = mm(n_o[...], up_r[...])
        first_l, second_l = raised[:, EXPERTS * ff : EXPERTS * ff + 1], raised[:, EXPERTS * ff + 1 : EXPERTS * ff + 2]
        lead = jnp.where(second, second_l - first_l, first_l - second_l)
        gate = sigmoid(lead)
        other = sigmoid(-lead)
        pre = jnp.where(second, raised[:, ff : 2 * ff], raised[:, :ff])
        bell = (1.0 + lax.erf(pre * (1.0 / math.sqrt(2.0)))) * 0.5
        hidden = pre * bell
        slope = bell + pre * jnp.exp(-0.5 * pre * pre) * (1.0 / math.sqrt(2.0 * math.pi))
        hidden = hidden.astype(bf16)
        hid_f = hidden.astype(f32)
        both = jnp.concatenate(
            [jnp.where(second, 0.0, hid_f), jnp.where(second, hid_f, 0.0)], axis=1
        ).astype(bf16)
        hid_o[...] = both
        stage_2[slot] = (gate * mm(both, down_s[...])).astype(bf16)
        dex_o[...] = (gate * upstream.astype(f32)).astype(bf16)
        lowered = mm_t(upstream, down_s[...])
        d_hid = jnp.where(second, lowered[:, ff:], lowered[:, :ff])
        d_gate = jnp.sum(hid_f * d_hid, axis=-1, keepdims=True)
        d_pre = gate * d_hid * slope
        d_lead = gate * other * d_gate
        lane = lax.broadcasted_iota(jnp.int32, (rows, cols - EXPERTS * ff), 1)
        d_second = jnp.where(second, d_lead, -d_lead)
        d_logits = jnp.where(lane == 1, d_second, jnp.where(lane == 0, -d_second, 0.0))
        d_both = jnp.concatenate(
            [jnp.where(second, 0.0, d_pre), jnp.where(second, d_pre, 0.0), d_logits], axis=1
        ).astype(bf16)
        both_o[...] = d_both
        stage[slot] = mm_t(d_both, up_r[...]).astype(bf16)
        for k in range(blocks):

            @pl.when(i == k)
            def _(k=k):
                for buffer, sem, out in ((stage, stage_sems, backs[k]), (stage_2, stage_2_sems, outs[k])):
                    pltpu.make_async_copy(buffer.at[k % 2], out, sem.at[k % 2]).start()

        @pl.when(i == blocks - 1)
        def _():
            sent(0)
            sent(1)

    here = lambda i, s: i
    made = call(
        kernel,
        blocks,
        span,
        [
            *[(part, None, None) for group in normed for part in group],
            (cot, (rows, D + LANES), lambda i, s: i ^ s),
            (up, up.shape, None),
            (down, down.shape, None),
        ],
        [
            *[((rows, D), bf16, None, None)] * (2 * blocks),
            ((length, D), bf16, (rows, D), here),
            ((length, EXPERTS * ff), bf16, (rows, EXPERTS * ff), here),
            ((length, cols), bf16, (rows, cols), here),
            ((length, D), bf16, (rows, D), here),
        ],
        [
            pltpu.VMEM((EXPERTS * ff, D), bf16),
            pltpu.VMEM((blocks, rows, D), bf16),
            pltpu.SemaphoreType.DMA((blocks,)),
            pltpu.VMEM((2, rows, D), bf16),
            pltpu.SemaphoreType.DMA((2,)),
            pltpu.VMEM((2, rows, D), bf16),
            pltpu.SemaphoreType.DMA((2,)),
        ],
        4 * length * D * (cols + EXPERTS * ff),
        3 * length * ff,
    )
    return made[:blocks], made[blocks : 2 * blocks], made[2 * blocks :]


def back(flip, d_mix, weight_out, sel, act, proj_z, lin, mixed, kept, end, weight_step, skip, a2):
    length, wid = act.shape
    blocks = length // TIME_BLOCK
    per = blocks // lax.axis_size("wide")

    counts = [len(g) for g in d_mix]

    def kernel(s_ref, *refs):
        mix_groups, refs = taken(refs, counts)
        (
            wout, sel_r, act_r, z_r, lin_r, mixed_r, kept_r, end_r, wstep, skip_r, a_r,
            mix_o, dz_o, part, dact_o, gstep_o, da_o, dskip_o, dbias_o,
            lam_s, next_s, pb_s, pc_s, dt_s, u_s, dy_s, s1_s, s2_s, turned_s, held, sems,
        ) = refs
        place = blocks - 1 - pl.program_id(0)

        @pl.when(pl.program_id(0) == 0)
        def _():
            fetch_blocks(mix_groups, held, sems, s_ref[0])
            lam_s[...] = jnp.zeros_like(lam_s)
            next_s[...] = end_r[...]
            da_o[...] = jnp.zeros_like(da_o)
            for ref in (gstep_o, dskip_o, dbias_o):
                ref[...] = jnp.zeros_like(ref)
            turned_s[...] = jnp.zeros_like(turned_s)

        @pl.when(pl.program_id(0) % per == 0)
        def _():
            wait_block(held, sems, place // per)

        mix = held[place // per, pl.ds(pl.multiple_of(place % per * TIME_BLOCK, TIME_BLOCK), TIME_BLOCK)]
        mix_o[...] = mix
        d_gated = mm_t(mix, wout[...])
        z = z_r[...]
        s = sigmoid(z)
        dz_o[...] = (d_gated * mixed_r[...] * (s * (1.0 + z * (1.0 - s)))).astype(bf16)
        dy_s[...] = d_gated * (z * s)
        x_all = act_r[...].astype(f32)
        dskip_o[...] += jnp.sum(dy_s[...] * x_all, axis=0, keepdims=True)
        dt_s[...] = softplus(lin_r[...])
        u_s[...] = dt_s[...] * x_all
        low = sel_r[...]
        turned = low.astype(f32).T
        in_sel, out_sel = turned[IN_AT : IN_AT + NS, :], turned[OUT_AT : OUT_AT + NS, :]
        a2 = a_r[...]

        def fold(v):
            total = v[:, :LANES]
            for k in range(1, wid // LANES):
                total = total + v[:, k * LANES : (k + 1) * LANES]
            return total

        masks = row_masks(wid)
        p, after, acc = lam_s[...], next_s[...], da_o[...]
        first, second = [None] * 8, [None] * 8
        for t in range(TIME_BLOCK - 1, -1, -1):
            before = kept_r[t]
            dt_t, dy_t = dt_s[t : t + 1, :], dy_s[t : t + 1, :]
            lam = dy_t * out_sel[:, t : t + 1] + p
            p = lam * jnp.exp2(dt_t * a2)
            moved = p * before
            acc = acc + dt_t * moved
            term = lam * in_sel[:, t : t + 1]
            first[t % 8] = term[:8] + term[8:]
            term = a2 * moved
            second[t % 8] = term[:8] + term[8:]
            if t % 8 == 0:
                s1_s[t : t + 8, :] = row_sums(first, masks)
                s2_s[t : t + 8, :] = row_sums(second, masks)
            pb_s[t] = fold(lam * u_s[t : t + 1, :])
            pc_s[t] = fold(after * dy_t)
            after = before
        lam_s[...] = p
        next_s[...] = after
        da_o[...] = acc
        ones = jnp.ones((LANES, LANES), bf16)
        lane = lax.broadcasted_iota(jnp.int32, (NS, TIME_BLOCK), 1)
        for source, at in ((pb_s, IN_AT), (pc_s, OUT_AT)):
            sums = mm(source[...].reshape(TIME_BLOCK * NS, LANES).astype(bf16), ones)
            sums = sums.reshape(TIME_BLOCK, NS, LANES)
            parts = [jnp.zeros((NS, TIME_BLOCK), f32)] * 4
            for t in range(TIME_BLOCK):
                parts[t % 4] = jnp.where(lane == t, sums[t], parts[t % 4])
            turned_s[at : at + NS, :] = (parts[0] + parts[1]) + (parts[2] + parts[3])
        through = s1_s[...]
        d_step = s2_s[...] * LN2 + x_all * through
        dact_o[...] = dt_s[...] * through + skip_r[...] * dy_s[...]
        grad = d_step * sigmoid(lin_r[...])
        dbias_o[...] += jnp.sum(grad, axis=0, keepdims=True)
        grad = grad.astype(bf16)
        gstep_o[...] += t_mm(grad, low)
        part[...] = (mm(grad, wstep[...]) + turned_s[...].T).astype(bf16)

    here = lambda i, s: blocks - 1 - i
    rel = lambda i, s: (((blocks - 1 - i) // per) ^ s) * per + (blocks - 1 - i) % per
    row = (TIME_BLOCK, wid)
    one = ((1, wid), f32, (1, wid), None)
    return call(
        kernel,
        blocks,
        flip,
        [
            *[(part, None, None) for group in d_mix for part in group],
            (weight_out, (wid, D), None),
            (sel, (TIME_BLOCK, LANES), here),
            (act, row, here),
            (proj_z, row, here),
            (lin, row, here),
            (mixed, row, here),
            (kept, (TIME_BLOCK, NS, wid), here),
            (end, (NS, wid), None),
            (weight_step, (wid, LANES), None),
            (skip, (1, wid), None),
            (a2, (NS, wid), None),
        ],
        [
            ((length, D), bf16, (TIME_BLOCK, D), here),
            ((length, wid), bf16, row, rel),
            ((length, LANES), bf16, (TIME_BLOCK, LANES), here),
            ((length, wid), f32, row, here),
            ((wid, LANES), f32, (wid, LANES), None),
            ((NS, wid), f32, (NS, wid), None),
            one,
            one,
        ],
        [pltpu.VMEM((NS, wid), f32)] * 2
        + [pltpu.VMEM((TIME_BLOCK, NS, LANES), f32)] * 2
        + [pltpu.VMEM(row, f32)] * 5
        + [pltpu.VMEM((LANES, TIME_BLOCK), f32)]
        + [
            pltpu.VMEM((lax.axis_size("wide"), length // lax.axis_size("wide"), D), bf16),
            pltpu.SemaphoreType.DMA((lax.axis_size("wide"),)),
        ],
        length * wid * (20 * NS + 2 * D + 2 * LANES),
        length * NS * wid,
    )


def tail(
    flip, d_sel, d_act, conv, proj, d_z, normed, act, weight_x, weight_z, weight_sel, taps,
    grad_step, grad_flat, grad_z, grad_out, beyond, chans,
):
    length, wid = act.shape
    blocks, count = lax.axis_size("wide"), lax.axis_size("narrow")
    rows = length // blocks
    group, c_rows = D // (blocks * count), chans // count

    def kernel(
        s_ref, sel_r, dact_r, conv_r, proj_r, dz_r, n_r, act_r, wx, wz, wsel, taps_r, gstep_r, flat_r,
        gz_r, gout_r, *refs,
    ):
        (parts, packs), refs = taken(refs, [blocks, count])
        gx_o, ext, gx, gsel, flat, held, stage, sems = refs
        i = pl.program_id(0)

        send_ready(stage, sems, i)

        @pl.when(pl.program_id(0) == 0)
        def _():
            ext[rows:, :] = jnp.zeros((8, wid), f32)
            gx[...] = jnp.zeros_like(gx)
            gsel[...] = jnp.zeros_like(gsel)
            flat[...] = flat_r[...]

        low = sel_r[...]
        c = conv_r[...]
        q = sigmoid(c)
        d_conv = (mm_t(low, wsel[...]) + dact_r[...]) * (q * (1.0 + c * (1.0 - q)))
        ext[:rows, :] = d_conv
        flat[CONV : CONV + 1, :] += jnp.sum(d_conv, axis=0, keepdims=True)
        x = proj_r[...]
        d_x = jnp.zeros((rows, wid), f32)
        for k in range(CONV):
            moved = ext[CONV - 1 - k : CONV - 1 - k + rows, :]
            d_x = d_x + taps_r[k : k + 1, :] * moved
            flat[k : k + 1, :] += jnp.sum(moved * x, axis=0, keepdims=True)
        ext[rows:, :] = d_conv[:8, :]
        d_x = d_x.astype(bf16)
        stage[i % 2] = (mm_t(d_x, wx[...]) + mm_t(dz_r[...], wz[...])).astype(bf16)
        gx[...] += t_mm(n_r[...], d_x)
        gsel[...] += t_mm(act_r[...], low)
        send_rows(stage, sems, parts, i, blocks, (blocks - 1 - i) ^ s_ref[0], 0)

        @pl.when(pl.program_id(0) == blocks - 1)
        def _():
            for k in range(blocks * count):
                x = gx[k * group : (k + 1) * group, :chans]
                z = gz_r[k * group : (k + 1) * group, :chans]
                gx_o[k] = jnp.concatenate([x, z], axis=1).astype(bf16)
            tall = jnp.concatenate(
                [jnp.zeros((DT_RANK, wid), f32), flat[...], jnp.zeros((LANES - DT_RANK - FLAT, wid), f32)], axis=0
            )
            lane = lax.broadcasted_iota(jnp.int32, (wid, LANES), 1)
            left = jnp.where(lane < DT_RANK, gstep_r[...], tall.T)
            held[:, :LANES] = left
            held[:, LANES:] = gsel[...]
            for k, out in enumerate(packs):
                if c_rows % 8 == 0:
                    at = pl.multiple_of(s_ref[1 + k] * c_rows, 8)
                    out[:, :D] = gout_r[pl.ds(at, c_rows), :].astype(bf16)
                    out[:, D:] = held[pl.ds(at, c_rows), :].astype(bf16)
                    continue
                for p in range(count):

                    @pl.when(s_ref[1 + k] == p)
                    def _(out=out, at=p * c_rows):
                        out[:, :D] = gout_r[at : at + c_rows, :].astype(bf16)
                        out[:, D:] = held[at : at + c_rows, :].astype(bf16)

    here = lambda i, s: blocks - 1 - i
    rel = lambda i, s: (blocks - 1 - i) ^ s
    row = (rows, wid)
    pack = (c_rows, D + 2 * LANES)
    sent = (blocks * count, group, 2 * chans)
    return call(
        kernel,
        blocks,
        jnp.concatenate([flip, beyond]),
        [
            (d_sel, (rows, LANES), here),
            (d_act, row, here),
            (conv, row, here),
            (proj, row, here),
            (d_z, row, rel),
            (normed, (rows, D), rel),
            (act, row, here),
            (weight_x, (D, wid), None),
            (weight_z, (D, wid), None),
            (weight_sel, (wid, LANES), None),
            (taps, (CONV, wid), None),
            (grad_step, (wid, LANES), None),
            (grad_flat, (FLAT, wid), None),
            (grad_z, grad_z.shape, None),
            (grad_out, (wid, D), None),
        ],
        [*[((rows, D), bf16, None, None)] * blocks, *[(pack, bf16, pack, None)] * count, (sent, bf16, sent, None)],
        [
            pltpu.VMEM((rows + 8, wid), f32),
            pltpu.VMEM((D, wid), f32),
            pltpu.VMEM((wid, LANES), f32),
            pltpu.VMEM((FLAT, wid), f32),
            pltpu.VMEM((wid, 2 * LANES), f32),
            pltpu.VMEM((2, rows, D), bf16),
            pltpu.SemaphoreType.DMA((2,)),
        ],
        2 * length * wid * (3 * D + 2 * LANES),
    )


def row_grad(flip, a, b, cols, group, along):
    narrow = lax.axis_size("narrow")
    length, total = a.shape
    n = b.shape[1]
    blocks = lax.axis_size("wide")
    rows = length // blocks

    def kernel(s_ref, a_r, b_r, out, acc):
        @pl.when(pl.program_id(0) == 0)
        def _():
            acc[...] = jnp.zeros_like(acc)

        acc[...] += t_mm(a_r[...], b_r[...])

        @pl.when(pl.program_id(0) == blocks - 1)
        def _():
            for k in range(total // group):
                at = k % narrow * blocks + k // narrow if along else k
                out[at] = acc[k * group : (k + 1) * group, :cols].astype(bf16)

    here = lambda i, s: i
    return call(
        kernel,
        blocks,
        flip,
        [(a, (rows, total), here), (b, (rows, n), here)],
        [((total // group, group, cols), bf16, (total // group, group, cols), None)],
        [pltpu.VMEM((total, n), f32)],
        2 * length * total * n,
    )[0]


def joined(got):
    wide, narrow, rows, cols = got.shape
    half = cols // 2

    def kernel(got_r, out):
        parts = [sum(got_r[w, k].astype(f32) for k in range(narrow)) for w in range(wide)]
        out[:, : wide * half] = jnp.concatenate([p[:, :half] for p in parts], axis=1)
        out[:, wide * half :] = jnp.concatenate([p[:, half:] for p in parts], axis=1)

    vmem = pl.BlockSpec(memory_space=pltpu.VMEM)
    return pl.pallas_call(
        kernel,
        in_specs=[vmem],
        out_specs=vmem,
        out_shape=jax.ShapeDtypeStruct((rows, wide * cols), f32),
        compiler_params=pltpu.CompilerParams(vmem_limit_bytes=VMEM),
    )(got)


def norm_backward(values, inverse, gain_vec, upstream):
    scaled = upstream * gain_vec
    inner_mean = jnp.mean(values * scaled, axis=-1, keepdims=True)
    return inverse * scaled - values * (inverse * inverse * inverse) * inner_mean


def local(
    tokens,
    mixer_gain,
    in_weight,
    conv_weight,
    conv_bias,
    select_weight,
    step_weight,
    step_bias,
    decay_log,
    skip_weight,
    out_weight,
    expert_gain,
    router_weight,
    up_weight,
    down_weight,
    routes,
    lengths,
    cotangent,
):
    wide, narrow = lax.axis_size("wide"), lax.axis_size("narrow")
    w = lax.axis_index("wide")
    rows = tokens.shape[1]
    chans = DI // wide
    wid = -(-chans // LANES) * LANES
    ff = FF // wide
    d_rows = D // (wide * narrow)
    c_rows = DI // (wide * narrow)
    f_rows = FF // (wide * narrow)
    both = EXPERTS * ff
    flip = w if relative() else 0 * w
    span = jnp.stack([flip, lengths[0]]).astype(jnp.int32)

    tokens_own = tokens[0].astype(f32)

    in_parts = in_weight.reshape(d_rows, 2, wide, chans).transpose(1, 2, 0, 3)
    gains = jnp.stack([mixer_gain, expert_gain], axis=1)
    gains = jnp.broadcast_to(gains[None], (wide, d_rows, 2))
    zero_col = jnp.zeros((c_rows, 1), bf16)
    channel_pack = jnp.concatenate(
        [
            conv_weight.T,
            conv_bias[:, None],
            step_bias[:, None],
            skip_weight[:, None],
            zero_col,
            decay_log.T,
            step_weight.T,
            select_weight,
        ],
        axis=1,
    )
    pack_cols = channel_pack.shape[1]
    wide_cols = -(-pack_cols // LANES) * LANES
    channel_pack = pad_to(channel_pack, 1, wide_cols)
    x_parts = jnp.concatenate([in_parts[0], gains], axis=2)
    tokens_all, channel_pack = gather_wide(tokens[0], lambda block: turns(channel_pack))
    x_full = gather_rows(after(x_parts, channel_pack))
    x_full, tokens_all = lax.optimization_barrier((x_full, tokens_all))
    weight_x = pad_to(x_full[:, :chans], 1, wid)
    gains = x_full[:, chans:].T.astype(f32)
    gain_one, gain_two = gains[:1], gains[1:]
    up_parts = up_weight.reshape(EXPERTS, d_rows, wide, ff).transpose(2, 1, 0, 3)
    up_parts = up_parts.reshape(wide, d_rows, both)
    router_parts = jnp.broadcast_to(router_weight[None], (wide, d_rows, EXPERTS))
    up_parts = jnp.concatenate([up_parts, router_parts, in_parts[1]], axis=2)
    up_parts = lax.all_to_all(after(up_parts, x_full), "wide", 0, 0)
    up_parts = up_parts.reshape(wide * d_rows, both + EXPERTS + chans)
    route_cols = jnp.broadcast_to(routes[0].astype(bf16)[:, None], (rows, LANES))
    cot_ext = jnp.concatenate([cotangent[0], route_cols], axis=1)
    cot_all = lax.all_gather(after(cot_ext, tokens_all), "wide", axis=0, tiled=True)
    (packed,) = gather_channels(channel_pack, (wide_cols,), wid)
    flat = packed[:, :FLAT].T.astype(f32)
    taps = flat[:CONV]
    conv_shift, step_shift, skip = (flat[CONV + k : CONV + k + 1] for k in range(3))
    a_neg = -jnp.exp(flat[CONV + 4 :])
    a2 = a_neg * (1.0 / LN2)
    weight_step = pad_to(packed[:, FLAT : FLAT + DT_RANK], 1, LANES)
    weight_sel = pad_to(packed[:, FLAT + DT_RANK : pack_cols], 1, LANES)

    normed, proj_x, conv_sum, conv_act, sel_part = front(
        flip[None], tokens_all, gain_one, weight_x, taps, conv_shift, weight_sel
    )
    out_pieces = turns(after(out_weight, x_full))
    sel_part, up_parts, out_pieces = lax.optimization_barrier((sel_part, up_parts, out_pieces))
    z_pieces = turns(up_parts[:, both + EXPERTS :])
    up_parts = up_parts[:, : both + EXPERTS]
    selected, (z_pieces, weight_out) = reduce_wide(
        sel_part, lambda low: (z_pieces, gather_channels(out_pieces, (D,), wid)[0])
    )
    weight_z = ordered_rows(z_pieces, d_rows, wid)

    up_cols = -(-(both + EXPERTS) // LANES) * LANES
    up_pieces = turns(after(up_parts, selected, out_pieces))
    valid_own = (w * rows + jnp.arange(rows))[:, None] < lengths[0]
    upstream = jnp.where(valid_own, cotangent[0].astype(f32), 0.0)

    proj_z, step_lin, kept, end, mixed, gated, *mix_part = middle(
        flip[None], selected, conv_act, normed, weight_z, weight_step, step_shift, skip, a2, weight_out
    )
    mix_part, up_pieces = lax.optimization_barrier((mix_part, up_pieces))
    down_full = lax.all_gather(after(down_weight, cot_all, *up_pieces), "narrow")
    up_full = ordered_rows(up_pieces, d_rows, up_cols)
    mixer_sum, up_full = scatter_wide(mix_part, up_full, True)
    hidden_one = tokens_own + mixer_sum
    inverse_two = lax.rsqrt(jnp.mean(hidden_one * hidden_one, axis=-1, keepdims=True) + EPSILON)
    own = (hidden_one * inverse_two * gain_two).astype(bf16)

    pieces, _ = gather_wide(own)
    back_parts, out_parts, made = experts(span, pieces, cot_all, up_full, down_full, ff)
    normed_two, hidden_both, d_both, d_expert = made

    def beside(hop):
        hidden = after(hidden_both, hop)
        grad = t_mm(hidden, d_expert).astype(bf16)
        grad = grad.reshape(EXPERTS, narrow, f_rows, D).transpose(1, 0, 2, 3)
        return grad

    d_normed_two, grad_down = scatter_wide(back_parts, beside, True)
    grad_down = lax.psum_scatter(grad_down, "narrow", scatter_dimension=0)
    d_hidden_one = upstream + norm_backward(hidden_one, inverse_two, gain_two, d_normed_two)
    d_low = d_hidden_one.astype(bf16)
    def output_sums(hop):
        outs = after(out_parts, hop)
        if not relative():
            return outs
        pair = lambda q: outs[2 * q].astype(f32) + swap(outs[2 * q + 1], 1).astype(f32)
        return [pair(q).astype(bf16) for q in range(4)]

    d_mix, (grad_up, out_sums) = gather_wide(
        d_low,
        lambda low: row_grad(flip[None], normed_two, after(d_both, low), both + EXPERTS, d_rows, True),
        output_sums,
    )
    grad_up = lax.psum_scatter(
        after(grad_up, d_mix).reshape(narrow, wide, d_rows, both + EXPERTS), "narrow", scatter_dimension=0
    )
    if relative():
        sent = after(out_sums, d_mix)
        out_got = [swap(sent[q], 2 * q) for q in (1, 2, 3)]
    else:
        out_got = []

    d_mix_all, d_z, d_sel_part, d_act, grad_step, d_a, grad_skip, grad_step_bias = back(
        flip[None], d_mix, weight_out, selected, conv_act, proj_z, step_lin, mixed, kept, end,
        weight_step, skip, a2,
    )

    d_sel_part, out_got = lax.optimization_barrier((d_sel_part, out_got))

    def meanwhile(low):
        grad_out = t_mm(after(gated, low), d_mix_all)
        return grad_out, t_mm(after(normed, low), d_z)

    d_sel, (grad_out, grad_z) = reduce_wide(d_sel_part, meanwhile)
    z = lax.axis_index("narrow")
    beyond = jnp.stack([(z + k) % narrow for k in range(narrow)]).astype(jnp.int32)
    grad_flat = jnp.concatenate(
        [jnp.zeros((CONV + 1, wid), f32), grad_step_bias, grad_skip, jnp.zeros((1, wid), f32), d_a * a_neg],
        axis=0,
    )
    grad_up = lax.all_to_all(after(grad_up, d_sel), "wide", 0, 0)
    made = tail(
        flip[None], d_sel, d_act, conv_sum, proj_x, d_z, normed, conv_act, weight_x, weight_z,
        weight_sel, taps, grad_step, grad_flat, grad_z, grad_out, beyond, chans,
    )
    in_part, channel_grads, grad_in = made[:wide], made[wide:-1], made[-1]
    in_part, grad_up = lax.optimization_barrier((in_part, grad_up))
    grad_in = scatter_rows(grad_in)

    def beside(hop):
        up, down = lax.optimization_barrier((grad_up, grad_down, hop))[:2]
        up = up.astype(f32)
        router = jnp.sum(up[:, :, both:], axis=0)
        up = up[:, :, :both].reshape(wide, d_rows, EXPERTS, ff)
        up = up.transpose(2, 1, 0, 3).reshape(EXPERTS, d_rows, FF)
        gain = (
            jnp.sum(up_weight.astype(f32) * up, axis=(0, 2))
            + jnp.sum(router_weight.astype(f32) * router, axis=1)
        ) / expert_gain.astype(f32)
        if relative():
            out = sum(p.astype(f32) for p in lax.optimization_barrier(([out_sums[0], *out_got], hop))[0])
        else:
            out, _ = scatter_wide(out_sums)
        return up, router, gain, down.astype(f32), out, turned(channel_grads)

    d_normed, made = scatter_wide(in_part, beside)
    channel_grads = made[-1]
    made = made[:-1]
    grad_up, grad_router, grad_gain_two, grad_down, expert_sum = made
    d_normed, grad_in = lax.optimization_barrier((d_normed, grad_in))
    channel_grads = sum(p.astype(f32) for p in channel_grads)
    grad_out, channel_grads = channel_grads[:, :D], channel_grads[:, D:]
    inverse_one = lax.rsqrt(jnp.mean(tokens_own * tokens_own, axis=-1, keepdims=True) + EPSILON)
    token_grad = d_hidden_one + norm_backward(tokens_own, inverse_one, gain_one, d_normed)
    output = (hidden_one + expert_sum).astype(bf16)

    grad_in = joined(grad_in)
    grad_gain_one = jnp.sum(in_weight.astype(f32) * grad_in, axis=1) / mixer_gain.astype(f32)
    flat_grads = channel_grads[:, DT_RANK : DT_RANK + FLAT].T
    return (
        output[None],
        token_grad[None],
        grad_gain_one,
        grad_in,
        flat_grads[:CONV],
        flat_grads[CONV],
        channel_grads[:, LANES : LANES + DT_RANK + 2 * NS],
        channel_grads[:, :DT_RANK].T,
        flat_grads[CONV + 1],
        flat_grads[CONV + 4 :],
        flat_grads[CONV + 2],
        grad_out,
        grad_gain_two,
        grad_router,
        grad_up,
        grad_down,
    )


def solution(mesh):
    both = ("wide", "narrow")
    return jax.shard_map(
        local,
        mesh=mesh,
        in_specs=(
            P("narrow", "wide", None),
            P(both),
            P(both, None),
            P(None, both),
            P(both),
            P(both, None),
            P(None, both),
            P(both),
            P(None, both),
            P(both),
            P(both, None),
            P(both),
            P(both, None),
            P(None, both, None),
            P(None, both, None),
            P("narrow", "wide"),
            P("narrow"),
            P("narrow", "wide", None),
        ),
        out_specs=(
            P("narrow", "wide", None),
            P("narrow", "wide", None),
            P(both),
            P(both, None),
            P(None, both),
            P(both),
            P(both, None),
            P(None, both),
            P(both),
            P(None, both),
            P(both),
            P(both, None),
            P(both),
            P(both, None),
            P(None, both, None),
            P(None, both, None),
        ),
        check_vma=False,
    )
```
